256 devices in a mesh: dap: 8 (over z_lo, core), dp: 32 (over y, x, z_hi).
Axes of the slice: x: 4, y: 4, z: 8 (z_hi: 2, z_lo: 4; z = z_hi * 4 + z_lo), core: 2. Of those that a mesh axis runs over, the one named last changes fastest.
Arguments:
- pair_rep: bfloat16 [3072, 96, 128], P(('dp', 'dap')), parts along dimension 0, may hold values from -6 to 6
- cotangent: bfloat16 [3072, 96, 128], P(('dp', 'dap')), parts along dimension 0, may hold values from -6 to 6
- residue_mask: int32 [3072], P('dp'), parts along dimension 0, may hold values from 0 to 1, as said below
- ln_gain: float32 [2, 128], replicated, may hold values from 0.5 to 1.5
- ln_shift: float32 [2, 128], replicated, may hold values from -3 to 3
- w_proj: bfloat16 [2, 128, 512], replicated, may hold values from -2.828427 to 2.828427
- w_bias: bfloat16 [2, 128, 4], replicated, may hold values from -0.5 to 0.5
- gate_bias: float32 [2, 128], replicated, may hold values from -4 to 4
- w_out: bfloat16 [2, 128, 128], replicated, may hold values from -0.5 to 0.5
- out_bias: float32 [2, 128], replicated, may hold values from -3 to 3
Outputs:
- grad_pair: bfloat16 [3072, 96, 128], P(('dp', 'dap')), parts along dimension 0
- grad_gain: float32 [64, 128], P('dp'), parts along dimension 0
- grad_shift: float32 [64, 128], P('dp'), parts along dimension 0
- grad_proj: float32 [64, 128, 512], P('dp'), parts along dimension 0
- grad_bias_w: float32 [64, 128, 4], P('dp'), parts along dimension 0
- grad_gate: float32 [64, 128], P('dp'), parts along dimension 0
- grad_out_w: float32 [64, 128, 128], P('dp'), parts along dimension 0
- grad_out_bias: float32 [64, 128], P('dp'), parts along dimension 0
The draws below stay inside these ranges and needn't reach their ends.
There are 32 independent parts, one for each index of `dp`. The reference program is written for one: setup_inputs(seed, part) draws one part's arguments, and reference() takes and returns one part's arrays. A program takes and returns all parts, laid end to end along the dimension named above; an argument that names none is the same for every part. Nothing has to cross between parts.
Inputs may be any that keep to these rules, and one draw needn't show every extreme that they name: residue_mask is 1 below a crop length of at least 48 and 0 from there on; the last position is always 0.
All inputs are finite; a program needn't handle non-finite values.
Results may differ from the reference program's by a relative error of at most 0.029.
The reference program's roundings to bfloat16 on the way count: a program that leaves them out, or rounds other values in their place, can miss the bound.
Values may be sent and summed in bfloat16 or wider, within the bound.
No kernel may reach another device: no remote copies, remote signals or barrier semaphores. Data moves between devices by JAX's collectives and lax.ppermute only.
A program may use at most 128 MiB of HBM per device.

```python
import jax
import jax.numpy as jnp
from jax import lax

CHANNELS = 128
HEAD_COUNT = 4
HEAD_WIDTH = 32
RESIDUES = 96


def draw_residue_mask(key, part):
    key = jax.random.fold_in(key, 7)
    length = jax.random.randint(key, (), RESIDUES // 2, RESIDUES)
    return (jnp.arange(RESIDUES) < length).astype(jnp.int32)


def draw_w_proj(key, part):
    key = jax.random.fold_in(key, 11)
    width = HEAD_COUNT * HEAD_WIDTH
    key_base = jax.random.fold_in(key, 0)
    scale = CHANNELS ** (-0.5)
    base = jax.random.truncated_normal(key_base, -4.0, 4.0, (2, CHANNELS, 4 * width), jnp.float32) * scale
    return base.astype(jnp.bfloat16)


def block_scale(key, dims, cuts, low, top_value):
    level, own = 1.0, jax.random.fold_in(key, 6)
    for axis_at, parts in cuts:
        steps = jnp.exp(jax.random.uniform(jax.random.fold_in(own, axis_at), (parts,), jnp.float32, low / len(cuts), top_value / len(cuts)))
        level = level * jnp.repeat(steps, dims[axis_at] // parts).reshape([-1 if axis == axis_at else 1 for axis in range(len(dims))])
    return level


def bell_draw(key, shape, scale, limit, cuts=(), dtype=jnp.bfloat16):
    array = scale * jax.random.normal(key, shape, jnp.float32)
    if cuts:
        array = array * block_scale(key, shape, cuts, -0.22, 0.18)
    return jnp.clip(array, -limit, limit).astype(dtype)


def setup_inputs(seed: int = 0, part: int = 0) -> dict:
    key_of = jax.random.split(jax.random.key(seed), 11)
    part_keys = jax.random.split(jax.random.fold_in(key_of[10], part), 11)
    pair_rep = bell_draw(part_keys[0], (RESIDUES, RESIDUES, CHANNELS), 1.0, 6.0, ((0, 8),))
    cotangent = bell_draw(part_keys[1], (RESIDUES, RESIDUES, CHANNELS), 1.0, 6.0, ((0, 8),))
    residue_mask = draw_residue_mask(jax.random.fold_in(jax.random.fold_in(key_of[10], part), 71), part)
    ln_gain = jnp.clip(1.0 + 0.1 * jax.random.normal(key_of[3], (2, CHANNELS), jnp.float32), 0.5, 1.5)
    ln_shift = bell_draw(key_of[4], (2, CHANNELS), 0.5, 3.0, (), jnp.float32)
    w_proj = draw_w_proj(jax.random.fold_in(key_of[10], 71), part)
    w_bias = bell_draw(key_of[6], (2, CHANNELS, HEAD_COUNT), CHANNELS ** -0.5, 0.5)
    gate_bias = bell_draw(key_of[7], (2, HEAD_COUNT * HEAD_WIDTH), 1.0, 4.0, (), jnp.float32)
    w_out = bell_draw(key_of[8], (2, HEAD_COUNT * HEAD_WIDTH, CHANNELS), (HEAD_COUNT * HEAD_WIDTH) ** -0.5, 0.5)
    out_bias = bell_draw(key_of[9], (2, CHANNELS), 0.5, 3.0, (), jnp.float32)
    return {"pair_rep": pair_rep, "cotangent": cotangent, "residue_mask": residue_mask, "ln_gain": ln_gain, "ln_shift": ln_shift, "w_proj": w_proj, "w_bias": w_bias, "gate_bias": gate_bias, "w_out": w_out, "out_bias": out_bias}


EPSILON = 1e-05

def layer_norm(inputs, gain, shift):
    floats = inputs.astype(jnp.float32)
    center = lax.optimization_barrier(jnp.mean(floats, axis=-1, keepdims=True))
    spread = lax.optimization_barrier(jnp.mean(jnp.square(floats - center), axis=-1, keepdims=True))
    inverse = lax.rsqrt(spread + EPSILON)
    normed = (floats - center) * inverse
    return ((normed * gain + shift).astype(jnp.bfloat16), normed, inverse)

def split_heads(tensor):
    return tensor.reshape(tensor.shape[0], tensor.shape[1], HEAD_COUNT, HEAD_WIDTH)

def prepare(inputs, gain, shift, w_proj, w_bias, gate_bias):
    width = HEAD_COUNT * HEAD_WIDTH
    normed_x, normed, inverse = layer_norm(inputs, gain, shift)
    joint = jnp.dot(normed_x, w_proj, preferred_element_type=jnp.float32)
    scaling = HEAD_WIDTH ** (-0.5)
    query = (joint[..., :width] * scaling).astype(jnp.bfloat16)
    keys = joint[..., width:2 * width].astype(jnp.bfloat16)
    values = joint[..., 2 * width:3 * width].astype(jnp.bfloat16)
    gate = jax.nn.sigmoid(joint[..., 3 * width:] + gate_bias)
    bias_rows = jnp.dot(normed_x, w_bias, preferred_element_type=jnp.float32).astype(jnp.bfloat16)
    bias_full = jnp.transpose(bias_rows, (2, 0, 1))
    return (normed_x, normed, inverse, query, keys, values, gate, bias_full)

def row_probs(query_row, keys_row, bias_full, key_term):
    scores = jnp.einsum('jhc,khc->hjk', query_row.astype(jnp.float32), keys_row.astype(jnp.float32))
    scores = scores + bias_full.astype(jnp.float32) + key_term[None, None, :]
    row_top = lax.optimization_barrier(jnp.max(scores, axis=-1, keepdims=True))
    expo = jnp.exp(scores - row_top)
    return expo / lax.optimization_barrier(jnp.sum(expo, axis=-1, keepdims=True))

def attend(state, key_term):
    normed_x, normed, inverse, query, keys, values, gate, bias_full = state

    def one_row(items):
        query_row, keys_row, values_row = items
        probab = row_probs(query_row, keys_row, bias_full, key_term).astype(jnp.bfloat16)
        return jnp.einsum('hjk,khc->jhc', probab.astype(jnp.float32), values_row.astype(jnp.float32))
    attended = lax.map(one_row, (split_heads(query), split_heads(keys), split_heads(values)))
    return attended.reshape(query.shape)

def module_output(inputs, state, attended, w_out, out_bias):
    gate = state[6]
    mixed = (gate * attended).astype(jnp.bfloat16)
    projected = jnp.dot(mixed, w_out, preferred_element_type=jnp.float32)
    return (inputs.astype(jnp.float32) + projected + out_bias).astype(jnp.bfloat16)

def module_backward(state, attended, gain, w_proj, w_bias, w_out, key_term, upstream):
    normed_x, normed, inverse, query, keys, values, gate, bias_full = state
    scaling = HEAD_WIDTH ** (-0.5)
    upstream_f = upstream.astype(jnp.float32)
    mixed = (gate * attended).astype(jnp.bfloat16)
    grad_out_w = jnp.einsum('rnd,rnc->dc', mixed.astype(jnp.float32), upstream_f)
    grad_out_bias = lax.optimization_barrier(jnp.sum(upstream_f, axis=(0, 1)))
    grad_mixed = jnp.dot(upstream, w_out.T, preferred_element_type=jnp.float32)
    grad_att = (grad_mixed * gate).astype(jnp.bfloat16)
    grad_logit = (grad_mixed * attended * gate * (1.0 - gate)).astype(jnp.bfloat16)

    def row_back(carry, items):
        query_row, keys_row, values_row, grad_row = items
        probab = row_probs(query_row, keys_row, bias_full, key_term)
        probab_b = probab.astype(jnp.bfloat16).astype(jnp.float32)
        grad_row_f = grad_row.astype(jnp.float32)
        grad_probs = jnp.einsum('jhc,khc->hjk', grad_row_f, values_row.astype(jnp.float32))
        grad_values = jnp.einsum('hjk,jhc->khc', probab_b, grad_row_f).astype(jnp.bfloat16)
        inner = lax.optimization_barrier(jnp.sum(probab * grad_probs, axis=-1, keepdims=True))
        grad_scores = probab * (grad_probs - inner)
        scores_b = grad_scores.astype(jnp.bfloat16).astype(jnp.float32)
        grad_query = (jnp.einsum('hjk,khc->jhc', scores_b, keys_row.astype(jnp.float32)) * scaling).astype(jnp.bfloat16)
        grad_keys = jnp.einsum('hjk,jhc->khc', scores_b, query_row.astype(jnp.float32)).astype(jnp.bfloat16)
        return (carry + grad_scores, (grad_query, grad_keys, grad_values))
    start_carry = jnp.zeros(bias_full.shape, jnp.float32)
    total, (grad_query, grad_keys, grad_values) = lax.scan(row_back, start_carry, (split_heads(query), split_heads(keys), split_heads(values), split_heads(grad_att)))
    grad_bias_b = total.astype(jnp.bfloat16)
    grad_joint = jnp.concatenate([grad_query.reshape(query.shape), grad_keys.reshape(query.shape), grad_values.reshape(query.shape), grad_logit], axis=-1)
    grad_proj = jnp.einsum('rnc,rnd->cd', normed_x.astype(jnp.float32), grad_joint.astype(jnp.float32))
    grad_gate = lax.optimization_barrier(jnp.sum(grad_logit.astype(jnp.float32), axis=(0, 1)))
    grad_bias_w = jnp.einsum('rnc,hrn->ch', normed_x.astype(jnp.float32), grad_bias_b.astype(jnp.float32))
    grad_normed = jnp.dot(grad_joint, w_proj.T, preferred_element_type=jnp.float32)
    grad_normed = grad_normed + jnp.einsum('hrn,ch->rnc', grad_bias_b.astype(jnp.float32), w_bias.astype(jnp.float32))
    grad_gain = lax.optimization_barrier(jnp.sum(grad_normed * normed, axis=(0, 1)))
    grad_shift = lax.optimization_barrier(jnp.sum(grad_normed, axis=(0, 1)))
    scaled = grad_normed * gain
    grad_ln = inverse * (scaled - lax.optimization_barrier(jnp.mean(scaled, axis=-1, keepdims=True)) - normed * lax.optimization_barrier(jnp.mean(scaled * normed, axis=-1, keepdims=True)))
    grads = (grad_gain, grad_shift, grad_proj, grad_bias_w, grad_gate, grad_out_w, grad_out_bias)
    return (upstream_f + grad_ln, grads)

def reference(pair_rep, cotangent, residue_mask, ln_gain, ln_shift, w_proj, w_bias, gate_bias, w_out, out_bias):
    key_term = jnp.where(residue_mask > 0, 0.0, -1000000000.0).astype(jnp.float32)
    state_start = prepare(pair_rep, ln_gain[0], ln_shift[0], w_proj[0], w_bias[0], gate_bias[0])
    attended_start = attend(state_start, key_term)
    first = module_output(pair_rep, state_start, attended_start, w_out[0], out_bias[0])
    first_t = jnp.transpose(first, (1, 0, 2))
    upstream_t = jnp.transpose(cotangent, (1, 0, 2))
    state_end = prepare(first_t, ln_gain[1], ln_shift[1], w_proj[1], w_bias[1], gate_bias[1])
    attended_end = attend(state_end, key_term)
    grad_t, grads_end = module_backward(state_end, attended_end, ln_gain[1], w_proj[1], w_bias[1], w_out[1], key_term, upstream_t)
    grad_first = jnp.transpose(grad_t.astype(jnp.bfloat16), (1, 0, 2))
    grad_in, grads_start = module_backward(state_start, attended_start, ln_gain[0], w_proj[0], w_bias[0], w_out[0], key_term, grad_first)
    stacked = [jnp.stack([left, right]) / RESIDUES for left, right in zip(grads_start, grads_end)]
    return (grad_in.astype(jnp.bfloat16), stacked[0], stacked[1], stacked[2], stacked[3], stacked[4], stacked[5], stacked[6])
```

```python
import jax
import jax.numpy as jnp
from jax import lax
from jax.experimental import pallas as pl
from jax.experimental.pallas import tpu as pltpu
from jax.sharding import PartitionSpec as P

HEADS = 4
WIDTH = 32
CH = 128
N = 96
GROUP = 8
ROWS = N // GROUP
CELLS = ROWS * N
BLOCK = ROWS * ROWS
BROWS = HEADS * ROWS
PACK = BLOCK + BROWS
SLICE = CH // GROUP
WROWS = 5 * SLICE
EPSILON = 1e-05
SCALING = WIDTH ** (-0.5)
F32 = jnp.float32
BF16 = jnp.bfloat16


def dot_nn(a, b):
    return lax.dot_general(a, b, (((1,), (0,)), ((), ())), preferred_element_type=F32)


def dot_nt(a, b):
    return lax.dot_general(a, b, (((1,), (1,)), ((), ())), preferred_element_type=F32)


def dot_tn(a, b):
    return lax.dot_general(a, b, (((0,), (0,)), ((), ())), preferred_element_type=F32)


def normalise(x):
    center = jnp.mean(x, axis=-1, keepdims=True)
    moved = x - center
    spread = jnp.mean(jnp.square(moved), axis=-1, keepdims=True)
    inverse = lax.rsqrt(spread + EPSILON)
    return moved * inverse, inverse


def norm_back(grad_normed, gain, normed, inverse):
    scaled = grad_normed * gain
    return inverse * (
        scaled
        - jnp.mean(scaled, axis=-1, keepdims=True)
        - normed * jnp.mean(scaled * normed, axis=-1, keepdims=True)
    )


def fold8(x):
    return jnp.sum(x.reshape(x.shape[0] // 8, 8, x.shape[1]), axis=0)


def head_stack(x):
    lane = lax.broadcasted_iota(jnp.int32, x.shape, 1) // WIDTH
    zero = jnp.zeros_like(x)
    return jnp.concatenate([jnp.where(lane == h, x, zero) for h in range(HEADS)], axis=0)


def head_pick(x):
    lane = lax.broadcasted_iota(jnp.int32, (N, CH), 1) // WIDTH
    out = x[0:N]
    for h in range(1, HEADS):
        out = jnp.where(lane == h, x[h * N : (h + 1) * N], out)
    return out


def project(nx, w_proj, gate_bias):
    joint = dot_nn(nx, w_proj)
    q = (joint[:, 0:CH] * SCALING).astype(BF16)
    k = joint[:, CH : 2 * CH].astype(BF16)
    v = joint[:, 2 * CH : 3 * CH].astype(BF16)
    gate = jax.nn.sigmoid(joint[:, 3 * CH :] + gate_bias)
    return q, k, v, gate


def probabilities(q, k, bias_ref):
    scores = dot_nt(head_stack(k), q)
    out = []
    for h in range(HEADS):
        s = scores[h * N : (h + 1) * N] + bias_ref[h]
        e = jnp.exp(s - jnp.max(s, axis=0, keepdims=True))
        out.append(e * (1.0 / jnp.sum(e, axis=0, keepdims=True)))
    return out


def weighted(x, mats):
    x_t = x.T
    parts = [dot_nn(x_t[h * WIDTH : (h + 1) * WIDTH], mats[h]) for h in range(HEADS)]
    return jnp.concatenate(parts, axis=0).T


def key_column(mask_ref):
    row = jnp.where(mask_ref[...] > 0, 0.0, -1000000000.0).astype(F32)
    wide = jnp.broadcast_to(row, (N, N))
    diag = lax.broadcasted_iota(jnp.int32, (N, N), 0) == lax.broadcasted_iota(jnp.int32, (N, N), 1)
    return jnp.sum(jnp.where(diag, wide, 0.0), axis=1, keepdims=True)


def attention_back(probs, q, k, v, grad_att, sum_ref):
    grad_probs = dot_nt(head_stack(v), grad_att)
    probs_b = []
    scores_b = []
    for h in range(HEADS):
        p = probs[h]
        gp = grad_probs[h * N : (h + 1) * N]
        inner = jnp.sum(p * gp, axis=0, keepdims=True)
        ds = p * (gp - inner)
        sum_ref[h] += ds
        probs_b.append(p.astype(BF16))
        scores_b.append(ds.astype(BF16))
    grad_v = head_pick(dot_nn(jnp.concatenate(probs_b, axis=0), grad_att)).astype(BF16)
    grad_k = head_pick(dot_nn(jnp.concatenate(scores_b, axis=0), q)).astype(BF16)
    grad_q = (weighted(k, scores_b) * SCALING).astype(BF16)
    return grad_q, grad_k, grad_v


def bias_rows(nx, w_bias_t):
    return dot_nt(w_bias_t, nx)


def w_bias_rows(w_bias_ref, m):
    wide = jnp.concatenate([w_bias_ref[m].astype(F32), jnp.zeros((CH, CH - HEADS), F32)], axis=1)
    return wide.T[0:8].astype(BF16)


def k1_body(x_ref, cot_ref, gain_ref, shift_ref, wb_ref, nx_ref, msg_ref, bias_s, cot_s):
    gain, shift = gain_ref[0:1], shift_ref[0:1]
    wb = w_bias_rows(wb_ref, 0)

    def row(i, _):
        normed, _inv = normalise(x_ref[i].astype(F32))
        nx = (normed * gain + shift).astype(BF16)
        nx_ref[i] = nx
        bias_s[i, :, 0:N] = bias_rows(nx, wb)[0:HEADS]
        cot_s[pl.ds(i, N, stride=ROWS), :] = cot_ref[i].astype(F32)
        return 0

    bias_s[...] = jnp.zeros_like(bias_s)
    lax.fori_loop(0, ROWS, row, 0)
    bias = bias_s[...].reshape(BROWS, CH).astype(BF16)
    for e in range(GROUP):
        msg_ref[e, 0:BLOCK] = cot_s[e * BLOCK : (e + 1) * BLOCK].astype(BF16)
        msg_ref[e, BLOCK:PACK] = bias


def k1b_body(nx_ref, wp_ref, gb_ref, q_ref, k_ref, v_ref, gate_ref):
    def row(i, _):
        q, k, v, gate = project(nx_ref[i], wp_ref[0], gb_ref[0:1])
        q_ref[i] = q
        k_ref[i] = k
        v_ref[i] = v
        gate_ref[i] = gate
        return 0

    lax.fori_loop(0, ROWS, row, 0)


def gather_rows(recv_ref, flat_s, row_s):
    for d in range(GROUP):
        flat_s[d * BLOCK : (d + 1) * BLOCK] = recv_ref[d, 0:BLOCK].astype(F32)
    for i in range(ROWS):
        for d in range(GROUP):
            at = d * BLOCK + i * ROWS
            row_s[i, d * ROWS : (d + 1) * ROWS] = flat_s[at : at + ROWS]


def k2_body(
    x_ref, q_ref, k_ref, v_ref, gate_ref, recv_ref, mask_ref, wo_ref, ob_ref, gain_ref, shift_ref, wb_ref,
    att_ref, first_ref, bias_ref, msg_ref, raw_s, bias_s, first_s,
):
    key = key_column(mask_ref)
    for d in range(GROUP):
        raw_s[d * BROWS : (d + 1) * BROWS] = recv_ref[d, BLOCK:PACK].astype(F32)
    for h in range(HEADS):
        bias_ref[h] = raw_s[pl.ds(h, N, stride=HEADS), :].T[0:N] + key
    wb = w_bias_rows(wb_ref, 1)
    w_out = wo_ref[0]
    out_bias = ob_ref[0:1]
    gain, shift = gain_ref[1:2], shift_ref[1:2]
    bias_s[...] = jnp.zeros_like(bias_s)

    def row(i, _):
        probs = probabilities(q_ref[i], k_ref[i], bias_ref)
        att = weighted(v_ref[i], [p.astype(BF16) for p in probs])
        att_ref[i] = att
        mixed = (gate_ref[i] * att).astype(BF16)
        first = (x_ref[i].astype(F32) + dot_nn(mixed, w_out) + out_bias).astype(BF16)
        first_ref[i] = first
        first_f = first.astype(F32)
        first_s[pl.ds(i, N, stride=ROWS), :] = first_f
        normed, _inv = normalise(first_f)
        nx = (normed * gain + shift).astype(BF16)
        bias_s[i, :, 0:N] = bias_rows(nx, wb)[0:HEADS]
        return 0

    lax.fori_loop(0, ROWS, row, 0)
    bias = bias_s[...].reshape(BROWS, CH).astype(BF16)
    for e in range(GROUP):
        msg_ref[e, 0:BLOCK] = first_s[e * BLOCK : (e + 1) * BLOCK].astype(BF16)
        msg_ref[e, BLOCK:PACK] = bias


def weight_grads(nx_s, joint_s, mixed_s, up_s, out_ref):
    nx = nx_s[...]
    for block in range(4):
        part = dot_tn(nx, joint_s[:, block * CH : (block + 1) * CH]).astype(BF16)
        for e in range(GROUP):
            out_ref[e, block * SLICE : (block + 1) * SLICE] = part[e * SLICE : (e + 1) * SLICE]
    part = dot_tn(mixed_s[...], up_s[...]).astype(BF16)
    for e in range(GROUP):
        out_ref[e, 4 * SLICE : 5 * SLICE] = part[e * SLICE : (e + 1) * SLICE]


def k3_body(
    recv0_ref, recv1_ref, mask_ref, gain_ref, shift_ref, wp_ref, wb_ref, gb_ref, wo_ref,
    msg_ref, wg_ref, small_ref,
    flat_s, x_s, up_s, raw_s, bias_s, sum_s, nx_s, joint_s, mixed_s, upb_s,
):
    key = key_column(mask_ref)
    for d in range(GROUP):
        raw_s[d * BROWS : (d + 1) * BROWS] = recv1_ref[d, BLOCK:PACK].astype(F32)
    for h in range(HEADS):
        bias_s[h] = raw_s[pl.ds(h, N, stride=HEADS), :][:, 0:N] + key
    gather_rows(recv0_ref, flat_s, up_s)
    gather_rows(recv1_ref, flat_s, x_s)
    sum_s[...] = jnp.zeros_like(sum_s)
    small_ref[...] = jnp.zeros_like(small_ref)
    gain, shift = gain_ref[1:2], shift_ref[1:2]
    gate_bias = gb_ref[1:2]

    def row(i, _):
        normed, inverse = normalise(x_s[i])
        nx = (normed * gain + shift).astype(BF16)
        nx_s[pl.ds(i * N, N), :] = nx
        q, k, v, gate = project(nx, wp_ref[1], gate_bias)
        probs = probabilities(q, k, bias_s)
        att = weighted(v, [p.astype(BF16) for p in probs])
        mixed_s[pl.ds(i * N, N), :] = (gate * att).astype(BF16)
        up_f = up_s[i]
        up = up_f.astype(BF16)
        upb_s[pl.ds(i * N, N), :] = up
        grad_mixed = dot_nt(up, wo_ref[1])
        grad_att = (grad_mixed * gate).astype(BF16)
        grad_logit = (grad_mixed * att * gate * (1.0 - gate)).astype(BF16)
        grad_q, grad_k, grad_v = attention_back(probs, q, k, v, grad_att, sum_s)
        joint = jnp.concatenate([grad_q, grad_k, grad_v, grad_logit], axis=1)
        joint_s[pl.ds(i * N, N), :] = joint
        grad_normed = dot_nt(joint, wp_ref[1])
        flat_s[pl.ds(i, N, stride=ROWS), :] = norm_back(grad_normed, gain, normed, inverse)
        small_ref[0:8] += fold8(grad_normed * normed)
        small_ref[8:16] += fold8(grad_normed)
        small_ref[16:24] += fold8(grad_logit.astype(F32))
        small_ref[24:32] += fold8(up_f)
        return 0

    lax.fori_loop(0, ROWS, row, 0)
    for e in range(GROUP):
        msg_ref[e, 0:BLOCK] = flat_s[e * BLOCK : (e + 1) * BLOCK].astype(BF16)
        rows = [sum_s[h, e * ROWS : (e + 1) * ROWS] for h in range(HEADS)]
        msg_ref[e, BLOCK:PACK, 0:N] = jnp.concatenate(rows, axis=0).astype(BF16)
        msg_ref[e, BLOCK:PACK, N:CH] = jnp.zeros((BROWS, CH - N), BF16)
    weight_grads(nx_s, joint_s, mixed_s, upb_s, wg_ref)


def bias_sum(recv_ref, start, gb_s):
    total = recv_ref[0, start : start + BROWS].astype(F32)
    for d in range(1, GROUP):
        total += recv_ref[d, start : start + BROWS].astype(F32)
    gb_s[...] = jnp.zeros_like(gb_s)
    total = total.astype(BF16).astype(F32)
    for r in range(ROWS):
        for h in range(HEADS):
            gb_s[r * 8 + h : r * 8 + h + 1] = total[h * ROWS + r : h * ROWS + r + 1]
    return gb_s[...].T[0:N].astype(BF16)


def bias_part(i, gb_s, gb_t, wb_tiled, nx):
    rows = lax.broadcasted_iota(jnp.int32, (ROWS * 8, CH), 0) // 8
    picked = jnp.where(rows == i, wb_tiled, jnp.zeros_like(wb_tiled))
    grad_w = dot_nn(gb_s[pl.ds(pl.multiple_of(i * 8, 8), 8), 0:N].astype(BF16), nx)
    return dot_nn(gb_t, picked), grad_w


def k4_body(
    recv_ref, first_ref, cot_ref, x_ref, q_ref, k_ref, v_ref, gate_ref, att_ref, nx_ref, bias_ref,
    gain_ref, shift_ref, wp_ref, wb_ref, wo_ref, small1_ref, wg1_ref,
    up_ref, gn_ref, msg_ref, small_ref,
    flat_s, la_s, gb_s, sum_s, nx_s, joint_s, mixed_s, upb_s,
):
    gather_rows(recv_ref, flat_s, la_s)
    gb_t = bias_sum(recv_ref, BLOCK, gb_s)
    wb = w_bias_rows(wb_ref, 1)
    wb_tiled = jnp.concatenate([wb.astype(F32)] * ROWS, axis=0).astype(BF16)
    sum_s[...] = jnp.zeros_like(sum_s)
    small_ref[...] = jnp.zeros_like(small_ref)
    small_ref[0:32] = small1_ref[...]
    gain1, shift1 = gain_ref[1:2], shift_ref[1:2]

    def row(i, _):
        normed, inverse = normalise(first_ref[i].astype(F32))
        nx1 = (normed * gain1 + shift1).astype(BF16)
        from_bias, grad_w = bias_part(i, gb_s, gb_t, wb_tiled, nx1)
        small_ref[0:8] += fold8(from_bias * normed)
        small_ref[8:16] += fold8(from_bias)
        small_ref[32:40] += grad_w
        up_f = cot_ref[i].astype(F32) + la_s[i] + norm_back(from_bias, gain1, normed, inverse)
        up = up_f.astype(BF16)
        up_f = up.astype(F32)
        up_ref[i] = up
        upb_s[pl.ds(i * N, N), :] = up
        nx_s[pl.ds(i * N, N), :] = nx_ref[i]

        q, k, v, gate, att = q_ref[i], k_ref[i], v_ref[i], gate_ref[i], att_ref[i]
        probs = probabilities(q, k, bias_ref)
        mixed_s[pl.ds(i * N, N), :] = (gate * att).astype(BF16)
        grad_mixed = dot_nt(up, wo_ref[0])
        grad_att = (grad_mixed * gate).astype(BF16)
        grad_logit = (grad_mixed * att * gate * (1.0 - gate)).astype(BF16)
        grad_q, grad_k, grad_v = attention_back(probs, q, k, v, grad_att, sum_s)
        joint = jnp.concatenate([grad_q, grad_k, grad_v, grad_logit], axis=1)
        joint_s[pl.ds(i * N, N), :] = joint
        gn_ref[i] = dot_nt(joint, wp_ref[0])
        small_ref[40:48] += fold8(grad_logit.astype(F32))
        small_ref[48:56] += fold8(up_f)
        return 0

    lax.fori_loop(0, ROWS, row, 0)
    for h in range(HEADS):
        flat_s[h * N : (h + 1) * N, 0:N] = sum_s[h].T
    for e in range(GROUP):
        rows = [flat_s[h * N + e * ROWS : h * N + (e + 1) * ROWS, 0:N] for h in range(HEADS)]
        msg_ref[e, 2 * WROWS : 2 * WROWS + BROWS, 0:N] = jnp.concatenate(rows, axis=0).astype(BF16)
        msg_ref[e, 2 * WROWS : 2 * WROWS + BROWS, N:CH] = jnp.zeros((BROWS, CH - N), BF16)
        msg_ref[e, WROWS : 2 * WROWS] = wg1_ref[e]
    weight_grads(nx_s, joint_s, mixed_s, upb_s, msg_ref)


def split2(x):
    top = x.astype(BF16)
    return top, (x - top.astype(F32)).astype(BF16)


def k5_body(
    recv_ref, x_ref, up_ref, gn_ref, nx_ref, small_in_ref, gain_ref, wb_ref,
    out_ref, msg_ref, gb_s, small_s,
):
    gb_t = bias_sum(recv_ref, 2 * WROWS, gb_s)
    wb = w_bias_rows(wb_ref, 0)
    wb_tiled = jnp.concatenate([wb.astype(F32)] * ROWS, axis=0).astype(BF16)
    gain = gain_ref[0:1]
    small_s[...] = jnp.zeros_like(small_s)

    def row(i, _):
        normed, inverse = normalise(x_ref[i].astype(F32))
        from_bias, grad_w = bias_part(i, gb_s, gb_t, wb_tiled, nx_ref[i])
        grad_normed = gn_ref[i] + from_bias
        small_s[0:8] += fold8(grad_normed * normed)
        small_s[8:16] += fold8(grad_normed)
        small_s[16:24] += grad_w
        back = norm_back(grad_normed, gain, normed, inverse)
        out_ref[i] = (up_ref[i].astype(F32) + back).astype(BF16)
        return 0

    lax.fori_loop(0, ROWS, row, 0)
    total = recv_ref[0, 0 : 2 * WROWS].astype(F32)
    for d in range(1, GROUP):
        total += recv_ref[d, 0 : 2 * WROWS].astype(F32)
    total *= 1.0 / N
    total = total.astype(BF16)

    def one(x):
        return jnp.sum(x, axis=0, keepdims=True)

    rows = [
        one(small_s[0:8]), one(small_s[8:16]), one(small_in_ref[40:48]), one(small_in_ref[48:56]),
        small_s[16:20],
        one(small_in_ref[0:8]), one(small_in_ref[8:16]), one(small_in_ref[16:24]), one(small_in_ref[24:32]),
        small_in_ref[32:36],
    ]
    top, low = split2(jnp.concatenate(rows, axis=0))
    for e in range(GROUP):
        msg_ref[e, 0 : 2 * WROWS] = total
        msg_ref[e, 2 * WROWS : 2 * WROWS + 16] = top
        msg_ref[e, 2 * WROWS + 16 : 2 * WROWS + 32] = low


def k6_body(recv_ref, gain_ref, shift_ref, proj_ref, wb_ref, gate_ref, ow_ref, ob_ref):
    small = jnp.zeros((16, CH), F32)
    for d in range(GROUP):
        for m in range(2):
            for block in range(4):
                at = m * WROWS + block * SLICE
                proj_ref[m, d * SLICE : (d + 1) * SLICE, block * CH : (block + 1) * CH] = recv_ref[
                    d, at : at + SLICE
                ].astype(F32)
            at = m * WROWS + 4 * SLICE
            ow_ref[m, d * SLICE : (d + 1) * SLICE] = recv_ref[d, at : at + SLICE].astype(F32)
        at = 2 * WROWS
        small += recv_ref[d, at : at + 16].astype(F32) + recv_ref[d, at + 16 : at + 32].astype(F32)
    small = small * (1.0 / N)
    for m in range(2):
        at = m * 8
        gain_ref[m : m + 1] = small[at : at + 1]
        shift_ref[m : m + 1] = small[at + 1 : at + 2]
        gate_ref[m : m + 1] = small[at + 2 : at + 3]
        ob_ref[m : m + 1] = small[at + 3 : at + 4]
        wide = jnp.concatenate([small[at + 4 : at + 8], jnp.zeros((CH - HEADS, CH), F32)], axis=0)
        wb_ref[m] = wide.T[:, 0:HEADS]


def call(body, outs, scratch, name, flops=100000000):
    return pl.pallas_call(
        body,
        out_shape=[jax.ShapeDtypeStruct(shape, dtype) for shape, dtype in outs],
        scratch_shapes=[pltpu.VMEM(shape, dtype) for shape, dtype in scratch],
        compiler_params=pltpu.CompilerParams(vmem_limit_bytes=40 * 1024 * 1024),
        cost_estimate=pl.CostEstimate(flops=flops, bytes_accessed=2000000, transcendentals=500000),
        name=name,
    )


def swap(x):
    return lax.all_to_all(x, "dap", 0, 0, tiled=True)


def per_device(
    pair_rep, cotangent, residue_mask, ln_gain, ln_shift, w_proj, w_bias, gate_bias, w_out, out_bias
):
    mask = residue_mask.reshape(1, N)
    rows_b = ((ROWS, N, CH), BF16)
    rows_f = ((ROWS, N, CH), F32)
    flat_f = ((CELLS, CH), F32)
    flat_b = ((CELLS, CH), BF16)
    pack = ((GROUP, PACK, CH), BF16)
    mats = ((HEADS, N, N), F32)
    raw = ((GROUP * BROWS, CH), F32)
    own_bias = ((ROWS, HEADS, CH), F32)
    weights = [flat_b, ((CELLS, 4 * CH), BF16), flat_b, flat_b]

    nx, msg0 = call(k1_body, [rows_b, pack], [own_bias, flat_f], "norm_first")(
        pair_rep, cotangent, ln_gain, ln_shift, w_bias
    )
    recv0 = swap(msg0)
    q, k, v, gate = call(k1b_body, [rows_b, rows_b, rows_b, rows_f], [], "project_first")(
        nx, w_proj, gate_bias
    )
    att, first, bias0, msg1 = call(
        k2_body, [rows_f, rows_b, mats, pack], [raw, own_bias, flat_f], "attend_first"
    )(pair_rep, q, k, v, gate, recv0, mask, w_out, out_bias, ln_gain, ln_shift, w_bias)
    recv1 = swap(msg1)
    msg2, wg1, small1 = call(
        k3_body,
        [pack, ((GROUP, WROWS, CH), BF16), ((32, CH), F32)],
        [flat_f, rows_f, rows_f, raw, mats, mats] + weights,
        "second_module",
    )(recv0, recv1, mask, ln_gain, ln_shift, w_proj, w_bias, gate_bias, w_out)
    recv2 = swap(msg2)
    up, gn, msg3, small = call(
        k4_body,
        [rows_b, rows_f, ((GROUP, 2 * WROWS + BROWS, CH), BF16), ((56, CH), F32)],
        [flat_f, rows_f, ((ROWS * 8, CH), F32), mats] + weights,
        "back_first",
    )(
        recv2, first, cotangent, pair_rep, q, k, v, gate, att, nx, bias0,
        ln_gain, ln_shift, w_proj, w_bias, w_out, small1, wg1,
    )
    recv3 = swap(msg3)
    grad_pair, msg4 = call(
        k5_body,
        [rows_b, ((GROUP, 2 * WROWS + 32, CH), BF16)],
        [((ROWS * 8, CH), F32), ((24, CH), F32)],
        "grad_pair",
    )(recv3, pair_rep, up, gn, nx, small, ln_gain, w_bias)
    recv4 = swap(msg4)
    grad_gain, grad_shift, grad_proj, grad_bias_w, grad_gate, grad_out_w, grad_out_bias = call(
        k6_body,
        [
            ((2, CH), F32), ((2, CH), F32), ((2, CH, 4 * CH), F32), ((2, CH, HEADS), F32),
            ((2, CH), F32), ((2, CH, CH), F32), ((2, CH), F32),
        ],
        [],
        "weight_sums",
    )(recv4)
    return (
        grad_pair, grad_gain, grad_shift, grad_proj, grad_bias_w, grad_gate, grad_out_w, grad_out_bias
    )


def solution(mesh):
    in_specs = (
        P(("dp", "dap"), None, None),
        P(("dp", "dap"), None, None),
        P("dp"),
        P(),
        P(),
        P(),
        P(),
        P(),
        P(),
        P(),
    )
    out_specs = (
        P(("dp", "dap"), None, None),
        P("dp", None),
        P("dp", None),
        P("dp", None, None),
        P("dp", None, None),
        P("dp", None),
        P("dp", None, None),
        P("dp", None),
    )
    return jax.shard_map(
        per_device, mesh=mesh, in_specs=in_specs, out_specs=out_specs, check_vma=False
    )
```

```python
import jax
import jax.numpy as jnp
from jax import lax
from jax.experimental import pallas as pl
from jax.experimental.pallas import tpu as pltpu
from jax.sharding import PartitionSpec as P

HEADS = 4
WIDTH = 32
CH = 128
N = 96
GROUP = 8
ROWS = N // GROUP
CELLS = ROWS * N
BLOCK = ROWS * ROWS
BROWS = HEADS * ROWS
PACK = BLOCK + BROWS
SLICE = CH // GROUP
WROWS = 5 * SLICE
LOW2, LOW3 = 1, 0
EPSILON = 1e-05
SCALING = WIDTH ** (-0.5)
F32 = jnp.float32
BF16 = jnp.bfloat16


def dot_nn(a, b):
    return lax.dot_general(a, b, (((1,), (0,)), ((), ())), preferred_element_type=F32)


def dot_nt(a, b):
    return lax.dot_general(a, b, (((1,), (1,)), ((), ())), preferred_element_type=F32)


def dot_tn(a, b):
    return lax.dot_general(a, b, (((0,), (0,)), ((), ())), preferred_element_type=F32)


def normalise(x):
    center = jnp.mean(x, axis=-1, keepdims=True)
    moved = x - center
    spread = jnp.mean(jnp.square(moved), axis=-1, keepdims=True)
    inverse = lax.rsqrt(spread + EPSILON)
    return moved * inverse, inverse


def norm_back(grad_normed, gain, normed, inverse):
    scaled = grad_normed * gain
    return inverse * (
        scaled
        - jnp.mean(scaled, axis=-1, keepdims=True)
        - normed * jnp.mean(scaled * normed, axis=-1, keepdims=True)
    )


def fold8(x):
    return jnp.sum(x.reshape(x.shape[0] // 8, 8, x.shape[1]), axis=0)


def head_stack(x):
    lane = lax.broadcasted_iota(jnp.int32, x.shape, 1) // WIDTH
    zero = jnp.zeros_like(x)
    return jnp.concatenate([jnp.where(lane == h, x, zero) for h in range(HEADS)], axis=0)


def head_pick(x):
    lane = lax.broadcasted_iota(jnp.int32, (N, CH), 1) // WIDTH
    out = x[0:N]
    for h in range(1, HEADS):
        out = jnp.where(lane == h, x[h * N : (h + 1) * N], out)
    return out


def project(nx, w_proj, gate_bias):
    joint = dot_nn(nx, w_proj)
    q = (joint[:, 0:CH] * SCALING).astype(BF16)
    k = joint[:, CH : 2 * CH].astype(BF16)
    v = joint[:, 2 * CH : 3 * CH].astype(BF16)
    gate = jax.nn.sigmoid(joint[:, 3 * CH :] + gate_bias)
    return q, k, v, gate


def probabilities(q, k, bias_ref):
    scores = dot_nt(head_stack(k), q)
    out = []
    for h in range(HEADS):
        s = scores[h * N : (h + 1) * N] + bias_ref[h]
        e = jnp.exp(s - jnp.max(s, axis=0, keepdims=True))
        out.append(e * (1.0 / jnp.sum(e, axis=0, keepdims=True)))
    return out


def weighted(x, mats):
    x_t = x.T
    parts = [dot_nn(x_t[h * WIDTH : (h + 1) * WIDTH], mats[h]) for h in range(HEADS)]
    return jnp.concatenate(parts, axis=0).T


def key_column(mask_ref):
    row = jnp.where(mask_ref[...] > 0, 0.0, -1000000000.0).astype(F32)
    wide = jnp.broadcast_to(row, (N, N))
    diag = lax.broadcasted_iota(jnp.int32, (N, N), 0) == lax.broadcasted_iota(jnp.int32, (N, N), 1)
    return jnp.sum(jnp.where(diag, wide, 0.0), axis=1, keepdims=True)


def attention_back(probs, q, k, v, grad_att, sum_ref):
    grad_probs = dot_nt(head_stack(v), grad_att)
    probs_b = []
    scores_b = []
    for h in range(HEADS):
        p = probs[h]
        gp = grad_probs[h * N : (h + 1) * N]
        inner = jnp.sum(p * gp, axis=0, keepdims=True)
        ds = p * (gp - inner)
        sum_ref[h] += ds
        probs_b.append(p.astype(BF16))
        scores_b.append(ds.astype(BF16))
    grad_v = head_pick(dot_nn(jnp.concatenate(probs_b, axis=0), grad_att)).astype(BF16)
    grad_k = head_pick(dot_nn(jnp.concatenate(scores_b, axis=0), q)).astype(BF16)
    grad_q = (weighted(k, scores_b) * SCALING).astype(BF16)
    return jnp.concatenate([grad_q, grad_k, grad_v], axis=1)


def gate_back(grad_mixed, gate, part):
    return (grad_mixed * gate).astype(BF16), (grad_mixed * part).astype(BF16)


def bias_rows(nx, w_bias_t):
    return dot_nt(w_bias_t, nx)


def w_bias_rows(w_bias_ref, m):
    rows = w_bias_ref[m].astype(F32)
    return jnp.concatenate([rows, jnp.zeros((8 - HEADS, CH), F32)], axis=0).astype(BF16)


def fetch(pairs, sems):
    copies = [pltpu.make_async_copy(src, dst, sems.at[n]) for n, (src, dst) in enumerate(pairs)]
    for copy in copies:
        copy.start()
    return copies


def k1_body(
    x_hbm, cot_hbm, gain_hbm, shift_hbm, wb_hbm, nx_ref, msg_ref,
    x_ref, cot_ref, gain_ref, shift_ref, wb_ref, bias_s, cot_s, sems,
):
    copies = fetch(
        [(gain_hbm, gain_ref), (shift_hbm, shift_ref), (wb_hbm, wb_ref), (x_hbm, x_ref), (cot_hbm, cot_ref)],
        sems,
    )
    bias_s[...] = jnp.zeros_like(bias_s)
    for copy in copies[0:4]:
        copy.wait()
    gain, shift = gain_ref[0:1], shift_ref[0:1]
    wb = w_bias_rows(wb_ref, 0)
    for i in range(ROWS):
        normed, _inv = normalise(x_ref[i].astype(F32))
        nx = (normed * gain + shift).astype(BF16)
        nx_ref[i * N : (i + 1) * N] = nx
        bias_s[i, :, 0:N] = bias_rows(nx, wb)[0:HEADS]
    copies[4].wait()
    for i in range(ROWS):
        cot_s[pl.ds(i, N, stride=ROWS), :] = cot_ref[i].astype(F32)
    bias = bias_s[...].reshape(BROWS, CH).astype(BF16)
    for e in range(GROUP):
        msg_ref[e, 0:BLOCK] = cot_s[e * BLOCK : (e + 1) * BLOCK].astype(BF16)
        msg_ref[e, BLOCK:PACK] = bias


def k1b_body(nx_ref, wp_ref, gb_ref, q_ref, k_ref, v_ref, gate_ref):
    for i in range(ROWS):
        q, k, v, gate = project(nx_ref[i * N : (i + 1) * N], wp_ref[0], gb_ref[0:1])
        q_ref[i] = q
        k_ref[i] = k
        v_ref[i] = v
        gate_ref[i] = gate


def gather_rows(recv_ref, flat_s, row_s):
    for d in range(GROUP):
        flat_s[d * BLOCK : (d + 1) * BLOCK] = recv_ref[d, 0:BLOCK].astype(F32)
    for i in range(ROWS):
        for d in range(GROUP):
            at = d * BLOCK + i * ROWS
            row_s[i, d * ROWS : (d + 1) * ROWS] = flat_s[at : at + ROWS]


def k2_body(
    x_ref, q_ref, k_ref, v_ref, gate_ref, recv_ref, mask_ref, wo_ref, ob_ref, gain_ref, shift_ref, wb_ref,
    part_ref, mixed_ref, probs_ref, nx_ref, norm_ref, inv_ref, msg_ref,
    raw_s, own_s, first_s, row_ref, bias_ref,
):
    key = key_column(mask_ref)
    for d in range(GROUP):
        raw_s[d * BROWS : (d + 1) * BROWS] = recv_ref[d, BLOCK:PACK].astype(F32)
    for h in range(HEADS):
        bias_ref[h] = raw_s[pl.ds(h, N, stride=HEADS), :].T[0:N] + key
    wb = w_bias_rows(wb_ref, 1)
    w_out = wo_ref[0]
    out_bias = ob_ref[0:1]
    gain, shift = gain_ref[1:2], shift_ref[1:2]
    own_s[...] = jnp.zeros_like(own_s)
    for i in range(ROWS):
        probs = probabilities(q_ref[i], k_ref[i], bias_ref)
        for h in range(HEADS):
            probs_ref[i, h] = probs[h]
        att = weighted(v_ref[i], [p.astype(BF16) for p in probs])
        gate = gate_ref[i]
        gated = gate * att
        part_ref[i] = gated * (1.0 - gate)
        mixed = gated.astype(BF16)
        mixed_ref[i * N : (i + 1) * N] = mixed
        first = x_ref[i].astype(F32) + dot_nn(mixed, w_out) + out_bias
        first = first.astype(BF16)
        row_ref[i] = first
        first_s[pl.ds(i, N, stride=ROWS), :] = first.astype(F32)
    for i in range(ROWS):
        normed, inverse = normalise(row_ref[i].astype(F32))
        nx = (normed * gain + shift).astype(BF16)
        nx_ref[i] = nx
        norm_ref[i] = normed
        inv_ref[i] = jnp.broadcast_to(inverse, (N, CH))
        own_s[i, :, 0:N] = bias_rows(nx, wb)[0:HEADS]
    bias = own_s[...].reshape(BROWS, CH).astype(BF16)
    for e in range(GROUP):
        msg_ref[e, 0:BLOCK] = first_s[e * BLOCK : (e + 1) * BLOCK].astype(BF16)
        msg_ref[e, BLOCK:PACK] = bias


def k2b_body(recv_ref, wo_ref, up_ref, gm_ref, total_ref, flat_s, row_s):
    gather_rows(recv_ref, flat_s, row_s)
    total = jnp.zeros((8, CH), F32)
    for i in range(ROWS):
        up_f = row_s[i]
        total += fold8(up_f)
        up = up_f.astype(BF16)
        up_ref[i * N : (i + 1) * N] = up
        gm_ref[i] = dot_nt(up, wo_ref[1])
    total_ref[...] = total


def weight_grads(nx_ref, joint_ref, mixed_ref, up_ref, put):
    nx = nx_ref[...]
    for block in range(4):
        put(block, dot_tn(nx, joint_ref[:, block * CH : (block + 1) * CH]))
    put(4, dot_tn(mixed_ref[...], up_ref[...]))


def split2(x):
    top = x.astype(BF16)
    return top, (x - top.astype(F32)).astype(BF16)


def put_sums(msg_ref, e, start, rows, low):
    parts = split2(rows) if low else [rows.astype(BF16)]
    for n, part in enumerate(parts):
        at = start + n * BROWS
        msg_ref[e, at : at + BROWS, 0:N] = part
        msg_ref[e, at : at + BROWS, N:CH] = jnp.zeros((BROWS, CH - N), BF16)


def k3_body(
    recv_ref, mask_ref, gm_ref, gain_ref, shift_ref, wp_ref, gb_ref,
    msg_ref, small_ref, nx_ref, joint_ref, mixed_ref,
    flat_s, x_s, raw_s, bias_s, sum_s, norm_s, inv_s, q_s, k_s, v_s, gate_s, att_s, probs_s, grad_s,
):
    key = key_column(mask_ref)
    for d in range(GROUP):
        raw_s[d * BROWS : (d + 1) * BROWS] = recv_ref[d, BLOCK:PACK].astype(F32)
    for h in range(HEADS):
        bias_s[h] = raw_s[pl.ds(h, N, stride=HEADS), :][:, 0:N] + key
    gather_rows(recv_ref, flat_s, x_s)
    sum_s[...] = jnp.zeros_like(sum_s)
    gain, shift = gain_ref[1:2], shift_ref[1:2]
    gate_bias = gb_ref[1:2]
    for i in range(ROWS):
        normed, inverse = normalise(x_s[i])
        nx_ref[i * N : (i + 1) * N] = (normed * gain + shift).astype(BF16)
        norm_s[i] = normed
        inv_s[i] = jnp.broadcast_to(inverse, (N, CH))
    for i in range(ROWS):
        q_s[i], k_s[i], v_s[i], gate_s[i] = project(nx_ref[i * N : (i + 1) * N], wp_ref[1], gate_bias)
    for i in range(ROWS):
        probs = probabilities(q_s[i], k_s[i], bias_s)
        for h in range(HEADS):
            probs_s[i, h] = probs[h]
        att_s[i] = weighted(v_s[i], [p.astype(BF16) for p in probs])
    logit_sum = jnp.zeros((8, CH), F32)
    for i in range(ROWS):
        gate, att = gate_s[i], att_s[i]
        mixed_ref[i * N : (i + 1) * N] = (gate * att).astype(BF16)
        grad_s[i], grad_logit = gate_back(gm_ref[i], gate, att * gate * (1.0 - gate))
        joint_ref[i * N : (i + 1) * N, 3 * CH :] = grad_logit
        logit_sum += fold8(grad_logit.astype(F32))
    for i in range(ROWS):
        probs = [probs_s[i, h] for h in range(HEADS)]
        joint_ref[i * N : (i + 1) * N, 0 : 3 * CH] = attention_back(
            probs, q_s[i], k_s[i], v_s[i], grad_s[i], sum_s
        )
    gain_sum = jnp.zeros((8, CH), F32)
    shift_sum = jnp.zeros((8, CH), F32)
    for i in range(ROWS):
        grad_normed = dot_nt(joint_ref[i * N : (i + 1) * N], wp_ref[1])
        normed = norm_s[i]
        flat_s[pl.ds(i, N, stride=ROWS), :] = norm_back(grad_normed, gain, normed, inv_s[i])
        gain_sum += fold8(grad_normed * normed)
        shift_sum += fold8(grad_normed)
    small_ref[0:8] = gain_sum
    small_ref[8:16] = shift_sum
    small_ref[16:24] = logit_sum
    for e in range(GROUP):
        msg_ref[e, 0:BLOCK] = flat_s[e * BLOCK : (e + 1) * BLOCK].astype(BF16)
        rows = [sum_s[h, e * ROWS : (e + 1) * ROWS] for h in range(HEADS)]
        put_sums(msg_ref, e, BLOCK, jnp.concatenate(rows, axis=0), LOW2)


def k3w_body(nx_ref, joint_ref, mixed_ref, up_ref, out_ref):
    def put(block, part):
        part = part.astype(BF16)
        for e in range(GROUP):
            out_ref[e, block * SLICE : (block + 1) * SLICE] = part[e * SLICE : (e + 1) * SLICE]

    weight_grads(nx_ref, joint_ref, mixed_ref, up_ref, put)


def bias_sum(recv_ref, start, gb_s, low):
    total = recv_ref[0, start : start + BROWS].astype(F32)
    for d in range(1, GROUP):
        total += recv_ref[d, start : start + BROWS].astype(F32)
    if low:
        for d in range(GROUP):
            total += recv_ref[d, start + BROWS : start + 2 * BROWS].astype(F32)
    gb_s[...] = jnp.zeros_like(gb_s)
    total = total.astype(BF16).astype(F32)
    for r in range(ROWS):
        for h in range(HEADS):
            gb_s[r * 8 + h : r * 8 + h + 1] = total[h * ROWS + r : h * ROWS + r + 1]
    return gb_s[...].T[0:N].astype(BF16)


def bias_part(i, gb_s, gb_t, wb_tiled, nx):
    rows = lax.broadcasted_iota(jnp.int32, (ROWS * 8, CH), 0) // 8
    picked = jnp.where(rows == i, wb_tiled, jnp.zeros_like(wb_tiled))
    grad_w = dot_nn(gb_s[i * 8 : (i + 1) * 8, 0:N].astype(BF16), nx)
    return dot_nn(gb_t, picked), grad_w


def k4_body(
    recv_ref, cot_ref, q_ref, k_ref, v_ref, gate_ref, part_ref, probs_ref, mixed_ref, nx_ref,
    nx1_ref, norm1_ref, inv1_ref, gain_ref, wp_ref, wb_ref, wo_ref, wg1_ref,
    up_ref, gn_ref, msg_ref, small_ref,
    flat_s, la_s, gb_s, sum_s, joint_s, grad_s, upb_s,
):
    gather_rows(recv_ref, flat_s, la_s)
    gb_t = bias_sum(recv_ref, BLOCK, gb_s, LOW2)
    wb = w_bias_rows(wb_ref, 1)
    wb_tiled = jnp.concatenate([wb.astype(F32)] * ROWS, axis=0).astype(BF16)
    sum_s[...] = jnp.zeros_like(sum_s)
    gain1 = gain_ref[1:2]
    zero = jnp.zeros((8, CH), F32)
    gain_sum, shift_sum, bias_w, logit_sum, up_sum = zero, zero, zero, zero, zero
    for i in range(ROWS):
        from_bias, grad_w = bias_part(i, gb_s, gb_t, wb_tiled, nx1_ref[i])
        normed = norm1_ref[i]
        gain_sum += fold8(from_bias * normed)
        shift_sum += fold8(from_bias)
        bias_w += grad_w
        up_f = cot_ref[i].astype(F32) + la_s[i] + norm_back(from_bias, gain1, normed, inv1_ref[i])
        up = up_f.astype(BF16)
        up_ref[i] = up
        upb_s[i * N : (i + 1) * N] = up
        up_sum += fold8(up.astype(F32))
    for i in range(ROWS):
        grad_mixed = dot_nt(up_ref[i], wo_ref[0])
        grad_s[i], grad_logit = gate_back(grad_mixed, gate_ref[i], part_ref[i])
        joint_s[i * N : (i + 1) * N, 3 * CH :] = grad_logit
        logit_sum += fold8(grad_logit.astype(F32))
    for i in range(ROWS):
        probs = [probs_ref[i, h] for h in range(HEADS)]
        joint_s[i * N : (i + 1) * N, 0 : 3 * CH] = attention_back(
            probs, q_ref[i], k_ref[i], v_ref[i], grad_s[i], sum_s
        )
    for i in range(ROWS):
        gn_ref[i] = dot_nt(joint_s[i * N : (i + 1) * N], wp_ref[0])
    small_ref[0:8] = gain_sum
    small_ref[8:16] = shift_sum
    small_ref[16:24] = bias_w
    small_ref[24:32] = logit_sum
    small_ref[32:40] = up_sum
    for h in range(HEADS):
        flat_s[h * N : (h + 1) * N, 0:N] = sum_s[h].T
    for e in range(GROUP):
        rows = [flat_s[h * N + e * ROWS : h * N + (e + 1) * ROWS, 0:N] for h in range(HEADS)]
        put_sums(msg_ref, e, 2 * WROWS, jnp.concatenate(rows, axis=0), LOW3)
        msg_ref[e, WROWS : 2 * WROWS] = wg1_ref[e]

    def put(block, part):
        part = part.astype(BF16)
        for e in range(GROUP):
            msg_ref[e, block * SLICE : (block + 1) * SLICE] = part[e * SLICE : (e + 1) * SLICE]

    weight_grads(nx_ref, joint_s, mixed_ref, upb_s, put)


def k4x_body(x_ref, norm_ref, inv_ref):
    for i in range(ROWS):
        normed, inverse = normalise(x_ref[i].astype(F32))
        norm_ref[i] = normed
        inv_ref[i] = jnp.broadcast_to(inverse, (N, CH))


def k5_body(
    recv_ref, norm_ref, gn_ref, nx_ref, small1_ref, total1_ref, small_ref, wb_ref,
    full_ref, msg_ref, gb_s,
):
    gb_t = bias_sum(recv_ref, 2 * WROWS, gb_s, LOW3)
    wb = w_bias_rows(wb_ref, 0)
    wb_tiled = jnp.concatenate([wb.astype(F32)] * ROWS, axis=0).astype(BF16)
    zero = jnp.zeros((8, CH), F32)
    gain_sum, shift_sum, bias_w = zero, zero, zero
    for i in range(ROWS):
        from_bias, grad_w = bias_part(i, gb_s, gb_t, wb_tiled, nx_ref[i * N : (i + 1) * N])
        grad_normed = gn_ref[i] + from_bias
        full_ref[i] = grad_normed
        gain_sum += fold8(grad_normed * norm_ref[i])
        shift_sum += fold8(grad_normed)
        bias_w += grad_w
    total = recv_ref[0, 0 : 2 * WROWS].astype(F32)
    for d in range(1, GROUP):
        total += recv_ref[d, 0 : 2 * WROWS].astype(F32)
    total *= 1.0 / N
    total = total.astype(BF16)

    def one(x):
        return jnp.sum(x, axis=0, keepdims=True)

    rows = [
        one(gain_sum), one(shift_sum), one(small_ref[24:32]), one(small_ref[32:40]), bias_w[0:HEADS],
        one(small1_ref[0:8] + small_ref[0:8]), one(small1_ref[8:16] + small_ref[8:16]),
        one(small1_ref[16:24]), one(total1_ref[...]), small_ref[16 : 16 + HEADS],
    ]
    top, low = split2(jnp.concatenate(rows, axis=0))
    for e in range(GROUP):
        msg_ref[e, 0 : 2 * WROWS] = total
        msg_ref[e, 2 * WROWS : 2 * WROWS + 16] = top
        msg_ref[e, 2 * WROWS + 16 : 2 * WROWS + 32] = low


def k5b_body(full_ref, norm_ref, inv_ref, up_ref, gain_ref, out_ref):
    gain = gain_ref[0:1]
    for i in range(ROWS):
        back = norm_back(full_ref[i], gain, norm_ref[i], inv_ref[i])
        out_ref[i] = (up_ref[i].astype(F32) + back).astype(BF16)


def k6_body(recv_ref, gain_ref, shift_ref, proj_ref, wb_ref, gate_ref, ow_ref, ob_ref):
    small = jnp.zeros((16, CH), F32)
    for d in range(GROUP):
        for m in range(2):
            for block in range(4):
                at = m * WROWS + block * SLICE
                proj_ref[m, d * SLICE : (d + 1) * SLICE, block * CH : (block + 1) * CH] = recv_ref[
                    d, at : at + SLICE
                ].astype(F32)
            at = m * WROWS + 4 * SLICE
            ow_ref[m, d * SLICE : (d + 1) * SLICE] = recv_ref[d, at : at + SLICE].astype(F32)
        at = 2 * WROWS
        small += recv_ref[d, at : at + 16].astype(F32) + recv_ref[d, at + 16 : at + 32].astype(F32)
    small = small * (1.0 / N)
    for m in range(2):
        at = m * 8
        gain_ref[m : m + 1] = small[at : at + 1]
        shift_ref[m : m + 1] = small[at + 1 : at + 2]
        gate_ref[m : m + 1] = small[at + 2 : at + 3]
        ob_ref[m : m + 1] = small[at + 3 : at + 4]
        wb_ref[m] = small[at + 4 : at + 8]


def call(body, outs, scratch, name, far=(), far_out=(), copies=0, flops=100000000, big=False):
    near_spec = pl.BlockSpec(memory_space=pltpu.VMEM)
    far_spec = pl.BlockSpec(memory_space=pltpu.HBM)
    scratch = [pltpu.VMEM(shape, dtype) for shape, dtype in scratch]
    if copies:
        scratch.append(pltpu.SemaphoreType.DMA((copies,)) if copies > 1 else pltpu.SemaphoreType.DMA)

    def run(*args):
        return pl.pallas_call(
            body,
            in_specs=[far_spec if n in far else near_spec for n in range(len(args))],
            out_specs=[far_spec if n in far_out else near_spec for n in range(len(outs))],
            out_shape=[jax.ShapeDtypeStruct(shape, dtype) for shape, dtype in outs],
            scratch_shapes=scratch,
            compiler_params=pltpu.CompilerParams(vmem_limit_bytes=(62 if big else 24) * 1024 * 1024),
            cost_estimate=pl.CostEstimate(flops=flops, bytes_accessed=2000000, transcendentals=500000),
            name=name,
        )(*args)

    return run


def after(x, y):
    return lax.optimization_barrier((x, y))[0]


def swap(x):
    return lax.all_to_all(x, "dap", 0, 0, tiled=True)


def per_device(
    pair_rep, cotangent, residue_mask, ln_gain, ln_shift, w_proj, w_bias, gate_bias, w_out, out_bias
):
    mask = residue_mask.reshape(1, N)
    w_bias = jnp.swapaxes(w_bias, 1, 2)
    rows_b = ((ROWS, N, CH), BF16)
    rows_f = ((ROWS, N, CH), F32)
    flat_f = ((CELLS, CH), F32)
    flat_b = ((CELLS, CH), BF16)
    joint_b = ((CELLS, 4 * CH), BF16)
    pack = ((GROUP, PACK, CH), BF16)
    mats = ((HEADS, N, N), F32)
    probs = ((ROWS, HEADS, N, N), F32)
    raw = ((GROUP * BROWS, CH), F32)
    own_bias = ((ROWS, HEADS, CH), F32)
    bias_8 = ((ROWS * 8, CH), F32)

    vec_f = ((2, CH), F32)

    nx0, msg0 = call(
        k1_body,
        [flat_b, pack],
        [rows_b, rows_b, vec_f, vec_f, ((2, HEADS, CH), BF16), own_bias, flat_f],
        "norm_first",
        far=range(5),
        copies=5,
        big=True,
    )(pair_rep, cotangent, ln_gain, ln_shift, w_bias)
    recv0 = swap(msg0)
    q, k, v, gate = call(k1b_body, [rows_b, rows_b, rows_b, rows_f], [], "project_first")(
        nx0, w_proj, gate_bias
    )
    part0, mixed0, probs0, nx1, norm1, inv1, msg1 = call(
        k2_body,
        [rows_f, flat_b, probs, rows_b, rows_f, rows_f, pack],
        [raw, own_bias, flat_f, rows_b, mats],
        "attend_first",
    )(pair_rep, q, k, v, gate, recv0, mask, w_out, out_bias, ln_gain, ln_shift, w_bias)
    recv1 = swap(msg1)
    up1, gm1, total1 = call(
        k2b_body, [flat_b, rows_f, ((8, CH), F32)], [flat_f, rows_f], "cotangent_rows"
    )(after(recv0, recv1), w_out)
    msg2, small1, nxw, joint1, mixed1 = call(
        k3_body,
        [((GROUP, BLOCK + (1 + LOW2) * BROWS, CH), BF16), ((24, CH), F32), flat_b, joint_b, flat_b],
        [flat_f, rows_f, raw, mats, mats, rows_f, rows_f]
        + [rows_b, rows_b, rows_b, rows_f, rows_f, probs, rows_b],
        "second_module",
    )(recv1, mask, gm1, ln_gain, ln_shift, w_proj, gate_bias)
    recv2 = swap(msg2)
    (wg1,) = call(k3w_body, [((GROUP, WROWS, CH), BF16)], [], "second_weights")(
        after(nxw, recv2), joint1, mixed1, up1
    )
    up, gn, msg3, small = call(
        k4_body,
        [rows_b, rows_f, ((GROUP, 2 * WROWS + (1 + LOW3) * BROWS, CH), BF16), ((40, CH), F32)],
        [flat_f, rows_f, bias_8, mats, joint_b, rows_b, flat_b],
        "back_first",
    )(
        recv2, cotangent, q, k, v, gate, part0, probs0, mixed0, nx0, nx1, norm1, inv1,
        ln_gain, w_proj, w_bias, w_out, wg1,
    )
    recv3 = swap(msg3)
    norm0, inv0 = call(k4x_body, [rows_f, rows_f], [], "norm_again")(after(pair_rep, recv3))
    full, msg4 = call(
        k5_body, [rows_f, ((GROUP, 2 * WROWS + 32, CH), BF16)], [bias_8], "grad_sums"
    )(recv3, norm0, gn, nx0, small1, total1, small, w_bias)
    recv4 = swap(msg4)
    (grad_pair,) = call(k5b_body, [rows_b], [], "grad_pair")(after(full, recv4), norm0, inv0, up, ln_gain)
    grad_gain, grad_shift, grad_proj, grad_bias_w, grad_gate, grad_out_w, grad_out_bias = call(
        k6_body,
        [
            ((2, CH), F32), ((2, CH), F32), ((2, CH, 4 * CH), F32), ((2, HEADS, CH), F32),
            ((2, CH), F32), ((2, CH, CH), F32), ((2, CH), F32),
        ],
        [],
        "weight_sums",
    )(recv4)
    return (
        grad_pair, grad_gain, grad_shift, grad_proj, jnp.swapaxes(grad_bias_w, 1, 2), grad_gate,
        grad_out_w, grad_out_bias,
    )


def solution(mesh):
    in_specs = (
        P(("dp", "dap"), None, None),
        P(("dp", "dap"), None, None),
        P("dp"),
        P(),
        P(),
        P(),
        P(),
        P(),
        P(),
        P(),
    )
    out_specs = (
        P(("dp", "dap"), None, None),
        P("dp", None),
        P("dp", None),
        P("dp", None, None),
        P("dp", None, None),
        P("dp", None),
        P("dp", None, None),
        P("dp", None),
    )
    return jax.shard_map(
        per_device, mesh=mesh, in_specs=in_specs, out_specs=out_specs, check_vma=False
    )
```

```python
import jax
import jax.numpy as jnp
from jax import lax
from jax.experimental import pallas as pl
from jax.experimental.pallas import tpu as pltpu
from jax.sharding import PartitionSpec as P

HEADS = 4
WIDTH = 32
CH = 128
N = 96
GROUP = 8
ROWS = N // GROUP
CELLS = ROWS * N
BLOCK = ROWS * ROWS
BROWS = HEADS * ROWS
PACK = BLOCK + BROWS
SLICE = CH // GROUP
WROWS = 5 * SLICE
LOW2, LOW3 = 1, 0
EPSILON = 1e-05
SCALING = WIDTH ** (-0.5)
F32 = jnp.float32
BF16 = jnp.bfloat16


def dot_nn(a, b):
    return lax.dot_general(a, b, (((1,), (0,)), ((), ())), preferred_element_type=F32)


def dot_nt(a, b):
    return lax.dot_general(a, b, (((1,), (1,)), ((), ())), preferred_element_type=F32)


def dot_tn(a, b):
    return lax.dot_general(a, b, (((0,), (0,)), ((), ())), preferred_element_type=F32)


def normalise(x):
    center = jnp.mean(x, axis=-1, keepdims=True)
    moved = x - center
    spread = jnp.mean(jnp.square(moved), axis=-1, keepdims=True)
    inverse = lax.rsqrt(spread + EPSILON)
    return moved * inverse, inverse


def norm_back(grad_normed, gain, normed, inverse):
    scaled = grad_normed * gain
    return inverse * (
        scaled
        - jnp.mean(scaled, axis=-1, keepdims=True)
        - normed * jnp.mean(scaled * normed, axis=-1, keepdims=True)
    )


def fold8(x):
    return jnp.sum(x.reshape(x.shape[0] // 8, 8, x.shape[1]), axis=0)


def head_stack(x):
    lane = lax.broadcasted_iota(jnp.int32, x.shape, 1) // WIDTH
    zero = jnp.zeros_like(x)
    return jnp.concatenate([jnp.where(lane == h, x, zero) for h in range(HEADS)], axis=0)


def head_pick(x):
    lane = lax.broadcasted_iota(jnp.int32, (N, CH), 1) // WIDTH
    out = x[0:N]
    for h in range(1, HEADS):
        out = jnp.where(lane == h, x[h * N : (h + 1) * N], out)
    return out


def project(nx, w_proj, gate_bias):
    joint = dot_nn(nx, w_proj)
    q = (joint[:, 0:CH] * SCALING).astype(BF16)
    k = joint[:, CH : 2 * CH].astype(BF16)
    v = joint[:, 2 * CH : 3 * CH].astype(BF16)
    gate = jax.nn.sigmoid(joint[:, 3 * CH :] + gate_bias)
    return q, k, v, gate


def probabilities(q, k, bias_ref):
    scores = dot_nt(head_stack(k), q)
    out = []
    for h in range(HEADS):
        s = scores[h * N : (h + 1) * N] + bias_ref[h]
        e = jnp.exp(s - jnp.max(s, axis=0, keepdims=True))
        out.append(e * (1.0 / jnp.sum(e, axis=0, keepdims=True)))
    return out


def weighted(x, mats):
    x_t = x.T
    parts = [dot_nn(x_t[h * WIDTH : (h + 1) * WIDTH], mats[h]) for h in range(HEADS)]
    return jnp.concatenate(parts, axis=0).T


def key_column(mask_ref):
    row = jnp.where(mask_ref[...] > 0, 0.0, -1000000000.0).astype(F32)
    wide = jnp.broadcast_to(row, (N, N))
    diag = lax.broadcasted_iota(jnp.int32, (N, N), 0) == lax.broadcasted_iota(jnp.int32, (N, N), 1)
    return jnp.sum(jnp.where(diag, wide, 0.0), axis=1, keepdims=True)


def scores_back(i, probs_ref, v_ref, grad_ref, sum_ref, scores_ref):
    grad_probs = dot_nt(head_stack(v_ref[i]), grad_ref[i])
    for h in range(HEADS):
        p = probs_ref[i, h]
        gp = grad_probs[h * N : (h + 1) * N]
        inner = jnp.sum(p * gp, axis=0, keepdims=True)
        ds = p * (gp - inner)
        sum_ref[h] += ds
        scores_ref[i, h] = ds.astype(BF16)


def joint_back(probs_ref, scores_ref, q_ref, k_ref, grad_ref, joint_ref):
    for i in range(ROWS):
        stack = jnp.concatenate([probs_ref[i, h].astype(BF16) for h in range(HEADS)], axis=0)
        grad_v = head_pick(dot_nn(stack, grad_ref[i]))
        joint_ref[i * N : (i + 1) * N, 2 * CH : 3 * CH] = grad_v.astype(BF16)
    for i in range(ROWS):
        stack = jnp.concatenate([scores_ref[i, h] for h in range(HEADS)], axis=0)
        grad_k = head_pick(dot_nn(stack, q_ref[i]))
        joint_ref[i * N : (i + 1) * N, CH : 2 * CH] = grad_k.astype(BF16)
    for i in range(ROWS):
        grad_q = weighted(k_ref[i], [scores_ref[i, h] for h in range(HEADS)]) * SCALING
        joint_ref[i * N : (i + 1) * N, 0:CH] = grad_q.astype(BF16)


def gate_back(grad_mixed, gate, part):
    return (grad_mixed * gate).astype(BF16), (grad_mixed * part).astype(BF16)


def bias_rows(nx, w_bias_t):
    return dot_nt(w_bias_t, nx)


def w_bias_rows(w_bias_ref, m):
    rows = w_bias_ref[m].astype(F32)
    return jnp.concatenate([rows, jnp.zeros((8 - HEADS, CH), F32)], axis=0).astype(BF16)


def fetch(pairs, sems):
    copies = [pltpu.make_async_copy(src, dst, sems.at[n]) for n, (src, dst) in enumerate(pairs)]
    for copy in copies:
        copy.start()
    return copies


def k1_body(
    x_hbm, cot_hbm, gain_hbm, shift_hbm, wb_hbm, msg_ref,
    x_ref, cot_ref, gain_ref, shift_ref, wb_ref, bias_s, cot_s, sems,
):
    copies = fetch(
        [(gain_hbm, gain_ref), (shift_hbm, shift_ref), (wb_hbm, wb_ref), (x_hbm, x_ref), (cot_hbm, cot_ref)],
        sems,
    )
    bias_s[...] = jnp.zeros_like(bias_s)
    for copy in copies[0:4]:
        copy.wait()
    gain, shift = gain_ref[0:1], shift_ref[0:1]
    wb = w_bias_rows(wb_ref, 0)
    for i in range(ROWS):
        normed, _inv = normalise(x_ref[i].astype(F32))
        nx = (normed * gain + shift).astype(BF16)
        bias_s[i, :, 0:N] = bias_rows(nx, wb)[0:HEADS]
    copies[4].wait()
    for i in range(ROWS):
        cot_s[pl.ds(i, N, stride=ROWS), :] = cot_ref[i].astype(F32)
    bias = bias_s[...].reshape(BROWS, CH).astype(BF16)
    for e in range(GROUP):
        msg_ref[e, 0:BLOCK] = cot_s[e * BLOCK : (e + 1) * BLOCK].astype(BF16)
        msg_ref[e, BLOCK:PACK] = bias


def k1b_body(
    x_ref, gain_ref, shift_ref, wp_ref, gb_ref, q_ref, k_ref, v_ref, gate_ref, nx_ref, norm_ref, inv_ref
):
    gain, shift = gain_ref[0:1], shift_ref[0:1]
    for i in range(ROWS):
        normed, inverse = normalise(x_ref[i].astype(F32))
        nx_ref[i * N : (i + 1) * N] = (normed * gain + shift).astype(BF16)
        norm_ref[i] = normed
        inv_ref[i] = jnp.broadcast_to(inverse, (N, CH))
    for i in range(ROWS):
        q, k, v, gate = project(nx_ref[i * N : (i + 1) * N], wp_ref[0], gb_ref[0:1])
        q_ref[i] = q
        k_ref[i] = k
        v_ref[i] = v
        gate_ref[i] = gate


def gather_rows(recv_ref, flat_s, row_s):
    for d in range(GROUP):
        flat_s[d * BLOCK : (d + 1) * BLOCK] = recv_ref[d, 0:BLOCK].astype(F32)
    for i in range(ROWS):
        for d in range(GROUP):
            at = d * BLOCK + i * ROWS
            row_s[i, d * ROWS : (d + 1) * ROWS] = flat_s[at : at + ROWS]


def k2_body(
    x_ref, q_ref, k_ref, v_ref, gate_ref, recv_ref, mask_ref, wo_ref, ob_ref, gain_ref, shift_ref, wb_ref,
    part_ref, mixed_ref, probs_ref, nx_ref, norm_ref, inv_ref, msg_ref,
    raw_s, own_s, first_s, row_ref, bias_ref, att_s,
):
    key = key_column(mask_ref)
    for d in range(GROUP):
        raw_s[d * BROWS : (d + 1) * BROWS] = recv_ref[d, BLOCK:PACK].astype(F32)
    for h in range(HEADS):
        bias_ref[h] = raw_s[pl.ds(h, N, stride=HEADS), :].T[0:N] + key
    wb = w_bias_rows(wb_ref, 1)
    w_out = wo_ref[0]
    out_bias = ob_ref[0:1]
    gain, shift = gain_ref[1:2], shift_ref[1:2]
    own_s[...] = jnp.zeros_like(own_s)
    for i in range(ROWS):
        probs = probabilities(q_ref[i], k_ref[i], bias_ref)
        for h in range(HEADS):
            probs_ref[i, h] = probs[h]
        att_s[i] = weighted(v_ref[i], [p.astype(BF16) for p in probs])
    for i in range(ROWS):
        gate = gate_ref[i]
        gated = gate * att_s[i]
        part_ref[i] = gated * (1.0 - gate)
        mixed = gated.astype(BF16)
        mixed_ref[i * N : (i + 1) * N] = mixed
    for i in range(ROWS):
        mixed = mixed_ref[i * N : (i + 1) * N]
        first = x_ref[i].astype(F32) + dot_nn(mixed, w_out) + out_bias
        first = first.astype(BF16)
        row_ref[i] = first
        first_s[pl.ds(i, N, stride=ROWS), :] = first.astype(F32)
    for i in range(ROWS):
        normed, inverse = normalise(row_ref[i].astype(F32))
        nx = (normed * gain + shift).astype(BF16)
        nx_ref[i] = nx
        norm_ref[i] = normed
        inv_ref[i] = jnp.broadcast_to(inverse, (N, CH))
        own_s[i, :, 0:N] = bias_rows(nx, wb)[0:HEADS]
    bias = own_s[...].reshape(BROWS, CH).astype(BF16)
    for e in range(GROUP):
        msg_ref[e, 0:BLOCK] = first_s[e * BLOCK : (e + 1) * BLOCK].astype(BF16)
        msg_ref[e, BLOCK:PACK] = bias


def k2b_body(recv_ref, wo_ref, up_ref, gm_ref, total_ref, flat_s, row_s):
    gather_rows(recv_ref, flat_s, row_s)
    total = jnp.zeros((8, CH), F32)
    for i in range(ROWS):
        up_f = row_s[i]
        total += fold8(up_f)
        up = up_f.astype(BF16)
        up_ref[i * N : (i + 1) * N] = up
        gm_ref[i] = dot_nt(up, wo_ref[1])
    total_ref[...] = total


def weight_grads(nx_ref, joint_ref, mixed_ref, up_ref, put):
    nx = nx_ref[...]
    for block in range(4):
        put(block, dot_tn(nx, joint_ref[:, block * CH : (block + 1) * CH]))
    put(4, dot_tn(mixed_ref[...], up_ref[...]))


def split2(x):
    top = x.astype(BF16)
    return top, (x - top.astype(F32)).astype(BF16)


def put_sums(msg_ref, e, start, rows, low):
    parts = split2(rows) if low else [rows.astype(BF16)]
    for n, part in enumerate(parts):
        at = start + n * BROWS
        msg_ref[e, at : at + BROWS, 0:N] = part
        msg_ref[e, at : at + BROWS, N:CH] = jnp.zeros((BROWS, CH - N), BF16)


def k3_body(
    recv_ref, mask_ref, gm_ref, gain_ref, shift_ref, wp_ref, gb_ref,
    msg_ref, small_ref, nx_ref, joint_ref, mixed_ref,
    flat_s, x_s, raw_s, bias_s, sum_s, norm_s, inv_s, q_s, k_s, v_s, gate_s, att_s, probs_s, grad_s, scores_s,
):
    key = key_column(mask_ref)
    for d in range(GROUP):
        raw_s[d * BROWS : (d + 1) * BROWS] = recv_ref[d, BLOCK:PACK].astype(F32)
    for h in range(HEADS):
        bias_s[h] = raw_s[pl.ds(h, N, stride=HEADS), :][:, 0:N] + key
    gather_rows(recv_ref, flat_s, x_s)
    sum_s[...] = jnp.zeros_like(sum_s)
    gain, shift = gain_ref[1:2], shift_ref[1:2]
    gate_bias = gb_ref[1:2]
    for i in range(ROWS):
        normed, inverse = normalise(x_s[i])
        nx_ref[i * N : (i + 1) * N] = (normed * gain + shift).astype(BF16)
        norm_s[i] = normed
        inv_s[i] = jnp.broadcast_to(inverse, (N, CH))
    for i in range(ROWS):
        q_s[i], k_s[i], v_s[i], gate_s[i] = project(nx_ref[i * N : (i + 1) * N], wp_ref[1], gate_bias)
    for i in range(ROWS):
        probs = probabilities(q_s[i], k_s[i], bias_s)
        for h in range(HEADS):
            probs_s[i, h] = probs[h]
        att_s[i] = weighted(v_s[i], [p.astype(BF16) for p in probs])
    logit_sum = jnp.zeros((8, CH), F32)
    for i in range(ROWS):
        gate, att = gate_s[i], att_s[i]
        mixed_ref[i * N : (i + 1) * N] = (gate * att).astype(BF16)
        grad_s[i], grad_logit = gate_back(gm_ref[i], gate, att * gate * (1.0 - gate))
        joint_ref[i * N : (i + 1) * N, 3 * CH :] = grad_logit
        logit_sum += fold8(grad_logit.astype(F32))
    for i in range(ROWS):
        scores_back(i, probs_s, v_s, grad_s, sum_s, scores_s)
    joint_back(probs_s, scores_s, q_s, k_s, grad_s, joint_ref)
    gain_sum = jnp.zeros((8, CH), F32)
    shift_sum = jnp.zeros((8, CH), F32)
    for i in range(ROWS):
        grad_normed = dot_nt(joint_ref[i * N : (i + 1) * N], wp_ref[1])
        normed = norm_s[i]
        flat_s[pl.ds(i, N, stride=ROWS), :] = norm_back(grad_normed, gain, normed, inv_s[i])
        gain_sum += fold8(grad_normed * normed)
        shift_sum += fold8(grad_normed)
    small_ref[0:8] = gain_sum
    small_ref[8:16] = shift_sum
    small_ref[16:24] = logit_sum
    for e in range(GROUP):
        msg_ref[e, 0:BLOCK] = flat_s[e * BLOCK : (e + 1) * BLOCK].astype(BF16)
        rows = [sum_s[h, e * ROWS : (e + 1) * ROWS] for h in range(HEADS)]
        put_sums(msg_ref, e, BLOCK, jnp.concatenate(rows, axis=0), LOW2)


def k3w_body(nx_ref, joint_ref, mixed_ref, up_ref, out_ref):
    def put(block, part):
        part = part.astype(BF16)
        for e in range(GROUP):
            out_ref[e, block * SLICE : (block + 1) * SLICE] = part[e * SLICE : (e + 1) * SLICE]

    weight_grads(nx_ref, joint_ref, mixed_ref, up_ref, put)


def bias_sum(recv_ref, start, gb_s, low):
    total = recv_ref[0, start : start + BROWS].astype(F32)
    for d in range(1, GROUP):
        total += recv_ref[d, start : start + BROWS].astype(F32)
    if low:
        for d in range(GROUP):
            total += recv_ref[d, start + BROWS : start + 2 * BROWS].astype(F32)
    gb_s[...] = jnp.zeros_like(gb_s)
    total = total.astype(BF16).astype(F32)
    for r in range(ROWS):
        for h in range(HEADS):
            gb_s[r * 8 + h : r * 8 + h + 1] = total[h * ROWS + r : h * ROWS + r + 1]
    return gb_s[...].T[0:N].astype(BF16)


def bias_part(i, gb_s, gb_t, wb_tiled, nx):
    rows = lax.broadcasted_iota(jnp.int32, (ROWS * 8, CH), 0) // 8
    picked = jnp.where(rows == i, wb_tiled, jnp.zeros_like(wb_tiled))
    grad_w = dot_nn(gb_s[i * 8 : (i + 1) * 8, 0:N].astype(BF16), nx)
    return dot_nn(gb_t, picked), grad_w


def k4_body(
    recv_ref, cot_ref, q_ref, k_ref, v_ref, gate_ref, part_ref, probs_ref, mixed_ref, nx_ref,
    nx1_ref, norm1_ref, inv1_ref, gain_ref, wp_ref, wb_ref, wo_ref, wg1_ref,
    up_ref, gn_ref, msg_ref, small_ref,
    flat_s, la_s, gb_s, sum_s, joint_s, grad_s, upb_s, scores_s,
):
    gather_rows(recv_ref, flat_s, la_s)
    gb_t = bias_sum(recv_ref, BLOCK, gb_s, LOW2)
    wb = w_bias_rows(wb_ref, 1)
    wb_tiled = jnp.concatenate([wb.astype(F32)] * ROWS, axis=0).astype(BF16)
    sum_s[...] = jnp.zeros_like(sum_s)
    gain1 = gain_ref[1:2]
    zero = jnp.zeros((8, CH), F32)
    gain_sum, shift_sum, bias_w, logit_sum, up_sum = zero, zero, zero, zero, zero
    for i in range(ROWS):
        from_bias, grad_w = bias_part(i, gb_s, gb_t, wb_tiled, nx1_ref[i])
        normed = norm1_ref[i]
        gain_sum += fold8(from_bias * normed)
        shift_sum += fold8(from_bias)
        bias_w += grad_w
        up_f = cot_ref[i].astype(F32) + la_s[i] + norm_back(from_bias, gain1, normed, inv1_ref[i])
        up = up_f.astype(BF16)
        up_ref[i] = up
        upb_s[i * N : (i + 1) * N] = up
        up_sum += fold8(up.astype(F32))
    for i in range(ROWS):
        grad_mixed = dot_nt(up_ref[i], wo_ref[0])
        grad_s[i], grad_logit = gate_back(grad_mixed, gate_ref[i], part_ref[i])
        joint_s[i * N : (i + 1) * N, 3 * CH :] = grad_logit
        logit_sum += fold8(grad_logit.astype(F32))
    for i in range(ROWS):
        scores_back(i, probs_ref, v_ref, grad_s, sum_s, scores_s)
    joint_back(probs_ref, scores_s, q_ref, k_ref, grad_s, joint_s)
    for i in range(ROWS):
        gn_ref[i] = dot_nt(joint_s[i * N : (i + 1) * N], wp_ref[0])
    small_ref[0:8] = gain_sum
    small_ref[8:16] = shift_sum
    small_ref[16:24] = bias_w
    small_ref[24:32] = logit_sum
    small_ref[32:40] = up_sum
    for h in range(HEADS):
        flat_s[h * N : (h + 1) * N, 0:N] = sum_s[h].T
    for e in range(GROUP):
        rows = [flat_s[h * N + e * ROWS : h * N + (e + 1) * ROWS, 0:N] for h in range(HEADS)]
        put_sums(msg_ref, e, 2 * WROWS, jnp.concatenate(rows, axis=0), LOW3)
        msg_ref[e, WROWS : 2 * WROWS] = wg1_ref[e]

    def put(block, part):
        part = part.astype(BF16)
        for e in range(GROUP):
            msg_ref[e, block * SLICE : (block + 1) * SLICE] = part[e * SLICE : (e + 1) * SLICE]

    weight_grads(nx_ref, joint_s, mixed_ref, upb_s, put)


def k5_body(
    recv_ref, norm_ref, gn_ref, nx_ref, small1_ref, total1_ref, small_ref, wb_ref,
    full_ref, msg_ref, gb_s,
):
    gb_t = bias_sum(recv_ref, 2 * WROWS, gb_s, LOW3)
    wb = w_bias_rows(wb_ref, 0)
    wb_tiled = jnp.concatenate([wb.astype(F32)] * ROWS, axis=0).astype(BF16)
    zero = jnp.zeros((8, CH), F32)
    gain_sum, shift_sum, bias_w = zero, zero, zero
    for i in range(ROWS):
        from_bias, grad_w = bias_part(i, gb_s, gb_t, wb_tiled, nx_ref[i * N : (i + 1) * N])
        grad_normed = gn_ref[i] + from_bias
        full_ref[i] = grad_normed
        gain_sum += fold8(grad_normed * norm_ref[i])
        shift_sum += fold8(grad_normed)
        bias_w += grad_w
    total = recv_ref[0, 0 : 2 * WROWS].astype(F32)
    for d in range(1, GROUP):
        total += recv_ref[d, 0 : 2 * WROWS].astype(F32)
    total *= 1.0 / N
    total = total.astype(BF16)

    def one(x):
        return jnp.sum(x, axis=0, keepdims=True)

    rows = [
        one(gain_sum), one(shift_sum), one(small_ref[24:32]), one(small_ref[32:40]), bias_w[0:HEADS],
        one(small1_ref[0:8] + small_ref[0:8]), one(small1_ref[8:16] + small_ref[8:16]),
        one(small1_ref[16:24]), one(total1_ref[...]), small_ref[16 : 16 + HEADS],
    ]
    top, low = split2(jnp.concatenate(rows, axis=0))
    for e in range(GROUP):
        msg_ref[e, 0 : 2 * WROWS] = total
        msg_ref[e, 2 * WROWS : 2 * WROWS + 16] = top
        msg_ref[e, 2 * WROWS + 16 : 2 * WROWS + 32] = low


def k5b_body(full_ref, norm_ref, inv_ref, up_ref, gain_ref, out_ref):
    gain = gain_ref[0:1]
    for i in range(ROWS):
        back = norm_back(full_ref[i], gain, norm_ref[i], inv_ref[i])
        out_ref[i] = (up_ref[i].astype(F32) + back).astype(BF16)


def k6_body(recv_ref, gain_ref, shift_ref, proj_ref, wb_ref, gate_ref, ow_ref, ob_ref):
    small = jnp.zeros((16, CH), F32)
    for d in range(GROUP):
        for m in range(2):
            for block in range(4):
                at = m * WROWS + block * SLICE
                proj_ref[m, d * SLICE : (d + 1) * SLICE, block * CH : (block + 1) * CH] = recv_ref[
                    d, at : at + SLICE
                ].astype(F32)
            at = m * WROWS + 4 * SLICE
            ow_ref[m, d * SLICE : (d + 1) * SLICE] = recv_ref[d, at : at + SLICE].astype(F32)
        at = 2 * WROWS
        small += recv_ref[d, at : at + 16].astype(F32) + recv_ref[d, at + 16 : at + 32].astype(F32)
    small = small * (1.0 / N)
    for m in range(2):
        at = m * 8
        gain_ref[m : m + 1] = small[at : at + 1]
        shift_ref[m : m + 1] = small[at + 1 : at + 2]
        gate_ref[m : m + 1] = small[at + 2 : at + 3]
        ob_ref[m : m + 1] = small[at + 3 : at + 4]
        wb_ref[m] = small[at + 4 : at + 8]


def call(body, outs, scratch, name, far=(), far_out=(), copies=0, flops=100000000, big=False):
    near_spec = pl.BlockSpec(memory_space=pltpu.VMEM)
    far_spec = pl.BlockSpec(memory_space=pltpu.HBM)
    scratch = [pltpu.VMEM(shape, dtype) for shape, dtype in scratch]
    if copies:
        scratch.append(pltpu.SemaphoreType.DMA((copies,)) if copies > 1 else pltpu.SemaphoreType.DMA)

    def run(*args):
        return pl.pallas_call(
            body,
            in_specs=[far_spec if n in far else near_spec for n in range(len(args))],
            out_specs=[far_spec if n in far_out else near_spec for n in range(len(outs))],
            out_shape=[jax.ShapeDtypeStruct(shape, dtype) for shape, dtype in outs],
            scratch_shapes=scratch,
            compiler_params=pltpu.CompilerParams(vmem_limit_bytes=(62 if big else 24) * 1024 * 1024),
            cost_estimate=pl.CostEstimate(flops=flops, bytes_accessed=2000000, transcendentals=500000),
            name=name,
        )(*args)

    return run


def after(x, y):
    return lax.optimization_barrier((x, y))[0]


def swap(x):
    return lax.all_to_all(x, "dap", 0, 0, tiled=True)


def per_device(
    pair_rep, cotangent, residue_mask, ln_gain, ln_shift, w_proj, w_bias, gate_bias, w_out, out_bias
):
    mask = residue_mask.reshape(1, N)
    w_bias = jnp.swapaxes(w_bias, 1, 2)
    rows_b = ((ROWS, N, CH), BF16)
    rows_f = ((ROWS, N, CH), F32)
    flat_f = ((CELLS, CH), F32)
    flat_b = ((CELLS, CH), BF16)
    joint_b = ((CELLS, 4 * CH), BF16)
    pack = ((GROUP, PACK, CH), BF16)
    mats = ((HEADS, N, N), F32)
    probs = ((ROWS, HEADS, N, N), F32)
    raw = ((GROUP * BROWS, CH), F32)
    own_bias = ((ROWS, HEADS, CH), F32)
    bias_8 = ((ROWS * 8, CH), F32)

    vec_f = ((2, CH), F32)

    (msg0,) = call(
        k1_body,
        [pack],
        [rows_b, rows_b, vec_f, vec_f, ((2, HEADS, CH), BF16), own_bias, flat_f],
        "norm_first",
        far=range(5),
        copies=5,
        big=True,
    )(pair_rep, cotangent, ln_gain, ln_shift, w_bias)
    recv0 = swap(msg0)
    q, k, v, gate, nx0, norm0, inv0 = call(
        k1b_body, [rows_b, rows_b, rows_b, rows_f, flat_b, rows_f, rows_f], [], "project_first"
    )(pair_rep, ln_gain, ln_shift, w_proj, gate_bias)
    part0, mixed0, probs0, nx1, norm1, inv1, msg1 = call(
        k2_body,
        [rows_f, flat_b, probs, rows_b, rows_f, rows_f, pack],
        [raw, own_bias, flat_f, rows_b, mats, rows_f],
        "attend_first",
    )(pair_rep, q, k, v, gate, recv0, mask, w_out, out_bias, ln_gain, ln_shift, w_bias)
    recv1 = swap(msg1)
    up1, gm1, total1 = call(
        k2b_body, [flat_b, rows_f, ((8, CH), F32)], [flat_f, rows_f], "cotangent_rows"
    )(after(recv0, recv1), w_out)
    msg2, small1, nxw, joint1, mixed1 = call(
        k3_body,
        [((GROUP, BLOCK + (1 + LOW2) * BROWS, CH), BF16), ((24, CH), F32), flat_b, joint_b, flat_b],
        [flat_f, rows_f, raw, mats, mats, rows_f, rows_f]
        + [rows_b, rows_b, rows_b, rows_f, rows_f, probs, rows_b, ((ROWS, HEADS, N, N), BF16)],
        "second_module",
    )(recv1, mask, gm1, ln_gain, ln_shift, w_proj, gate_bias)
    recv2 = swap(msg2)
    (wg1,) = call(k3w_body, [((GROUP, WROWS, CH), BF16)], [], "second_weights")(
        after(nxw, recv2), joint1, mixed1, up1
    )
    up, gn, msg3, small = call(
        k4_body,
        [rows_b, rows_f, ((GROUP, 2 * WROWS + (1 + LOW3) * BROWS, CH), BF16), ((40, CH), F32)],
        [flat_f, rows_f, bias_8, mats, joint_b, rows_b, flat_b, ((ROWS, HEADS, N, N), BF16)],
        "back_first",
    )(
        recv2, cotangent, q, k, v, gate, part0, probs0, mixed0, nx0, nx1, norm1, inv1,
        ln_gain, w_proj, w_bias, w_out, wg1,
    )
    recv3 = swap(msg3)
    full, msg4 = call(
        k5_body, [rows_f, ((GROUP, 2 * WROWS + 32, CH), BF16)], [bias_8], "grad_sums"
    )(recv3, norm0, gn, nx0, small1, total1, small, w_bias)
    recv4 = swap(msg4)
    (grad_pair,) = call(k5b_body, [rows_b], [], "grad_pair")(after(full, recv4), norm0, inv0, up, ln_gain)
    grad_gain, grad_shift, grad_proj, grad_bias_w, grad_gate, grad_out_w, grad_out_bias = call(
        k6_body,
        [
            ((2, CH), F32), ((2, CH), F32), ((2, CH, 4 * CH), F32), ((2, HEADS, CH), F32),
            ((2, CH), F32), ((2, CH, CH), F32), ((2, CH), F32),
        ],
        [],
        "weight_sums",
    )(recv4)
    return (
        grad_pair, grad_gain, grad_shift, grad_proj, jnp.swapaxes(grad_bias_w, 1, 2), grad_gate,
        grad_out_w, grad_out_bias,
    )


def solution(mesh):
    in_specs = (
        P(("dp", "dap"), None, None),
        P(("dp", "dap"), None, None),
        P("dp"),
        P(),
        P(),
        P(),
        P(),
        P(),
        P(),
        P(),
    )
    out_specs = (
        P(("dp", "dap"), None, None),
        P("dp", None),
        P("dp", None),
        P("dp", None, None),
        P("dp", None, None),
        P("dp", None),
        P("dp", None, None),
        P("dp", None),
    )
    return jax.shard_map(
        per_device, mesh=mesh, in_specs=in_specs, out_specs=out_specs, check_vma=False
    )
```

```python
import jax
import jax.numpy as jnp
from jax import lax
from jax.experimental import pallas as pl
from jax.experimental.pallas import tpu as pltpu
from jax.sharding import PartitionSpec as P

HEADS = 4
WIDTH = 32
CH = 128
N = 96
GROUP = 8
ROWS = N // GROUP
CELLS = ROWS * N
BLOCK = ROWS * ROWS
BROWS = HEADS * ROWS
PACK = BLOCK + BROWS
SLICE = CH // GROUP
WROWS = 5 * SLICE
EPSILON = 1e-05
SCALING = WIDTH ** (-0.5)
F32 = jnp.float32
BF16 = jnp.bfloat16


def dot_nn(a, b):
    return lax.dot_general(a, b, (((1,), (0,)), ((), ())), preferred_element_type=F32)


def dot_nt(a, b):
    return lax.dot_general(a, b, (((1,), (1,)), ((), ())), preferred_element_type=F32)


def dot_tn(a, b):
    return lax.dot_general(a, b, (((0,), (0,)), ((), ())), preferred_element_type=F32)


def normalise(x):
    center = jnp.mean(x, axis=-1, keepdims=True)
    moved = x - center
    spread = jnp.mean(jnp.square(moved), axis=-1, keepdims=True)
    inverse = lax.rsqrt(spread + EPSILON)
    return moved * inverse, inverse


def norm_back(grad_normed, gain, normed, inverse):
    scaled = grad_normed * gain
    return inverse * (
        scaled
        - jnp.mean(scaled, axis=-1, keepdims=True)
        - normed * jnp.mean(scaled * normed, axis=-1, keepdims=True)
    )


def fold8(x):
    return jnp.sum(x.reshape(x.shape[0] // 8, 8, x.shape[1]), axis=0)


def head_stack(x):
    lane = lax.broadcasted_iota(jnp.int32, x.shape, 1) // WIDTH
    zero = jnp.zeros_like(x)
    return jnp.concatenate([jnp.where(lane == h, x, zero) for h in range(HEADS)], axis=0)


def head_pick(x):
    lane = lax.broadcasted_iota(jnp.int32, (N, CH), 1) // WIDTH
    out = x[0:N]
    for h in range(1, HEADS):
        out = jnp.where(lane == h, x[h * N : (h + 1) * N], out)
    return out


def project(nx, w_proj, gate_bias):
    joint = dot_nn(nx, w_proj)
    q = (joint[:, 0:CH] * SCALING).astype(BF16)
    k = joint[:, CH : 2 * CH].astype(BF16)
    v = joint[:, 2 * CH : 3 * CH].astype(BF16)
    gate = jax.nn.sigmoid(joint[:, 3 * CH :] + gate_bias)
    return q, k, v, gate


def probabilities(q, k, bias_ref):
    scores = dot_nt(head_stack(k), q)
    out = []
    for h in range(HEADS):
        s = scores[h * N : (h + 1) * N] + bias_ref[h]
        e = jnp.exp(s - jnp.max(s, axis=0, keepdims=True))
        out.append(e * (1.0 / jnp.sum(e, axis=0, keepdims=True)))
    return out


def weighted(x, mats):
    x_t = x.T
    parts = [dot_nn(x_t[h * WIDTH : (h + 1) * WIDTH], mats[h]) for h in range(HEADS)]
    return jnp.concatenate(parts, axis=0).T


def key_column(mask_ref):
    row = jnp.where(mask_ref[...] > 0, 0.0, -1000000000.0).astype(F32)
    wide = jnp.broadcast_to(row, (N, N))
    diag = lax.broadcasted_iota(jnp.int32, (N, N), 0) == lax.broadcasted_iota(jnp.int32, (N, N), 1)
    return jnp.sum(jnp.where(diag, wide, 0.0), axis=1, keepdims=True)


def scores_back(i, probs_ref, v_ref, grad_ref, sum_ref, scores_ref):
    grad_probs = dot_nt(head_stack(v_ref[i]), grad_ref[i])
    for h in range(HEADS):
        p = probs_ref[i, h]
        gp = grad_probs[h * N : (h + 1) * N]
        inner = jnp.sum(p * gp, axis=0, keepdims=True)
        ds = p * (gp - inner)
        sum_ref[h] += ds
        scores_ref[i, h] = ds.astype(BF16)


def joint_back(probs_ref, scores_ref, q_ref, k_ref, grad_ref, joint_ref):
    for i in range(ROWS):
        stack = jnp.concatenate([probs_ref[i, h].astype(BF16) for h in range(HEADS)], axis=0)
        grad_v = head_pick(dot_nn(stack, grad_ref[i]))
        joint_ref[i * N : (i + 1) * N, 2 * CH : 3 * CH] = grad_v.astype(BF16)
    for i in range(ROWS):
        stack = jnp.concatenate([scores_ref[i, h] for h in range(HEADS)], axis=0)
        grad_k = head_pick(dot_nn(stack, q_ref[i]))
        joint_ref[i * N : (i + 1) * N, CH : 2 * CH] = grad_k.astype(BF16)
    for i in range(ROWS):
        grad_q = weighted(k_ref[i], [scores_ref[i, h] for h in range(HEADS)]) * SCALING
        joint_ref[i * N : (i + 1) * N, 0:CH] = grad_q.astype(BF16)


def gate_back(grad_mixed, gate, part):
    return (grad_mixed * gate).astype(BF16), (grad_mixed * part).astype(BF16)


def bias_rows(nx, w_bias_t):
    return dot_nt(w_bias_t, nx)


def w_bias_rows(w_bias_ref, m):
    rows = w_bias_ref[m].astype(F32)
    return jnp.concatenate([rows, jnp.zeros((8 - HEADS, CH), F32)], axis=0).astype(BF16)


def fetch(pairs, sems):
    copies = [pltpu.make_async_copy(src, dst, sems.at[n]) for n, (src, dst) in enumerate(pairs)]
    for copy in copies:
        copy.start()
    return copies


def k1_body(
    x_hbm, cot_hbm, gain_hbm, shift_hbm, wb_hbm, msg_ref,
    x_ref, cot_ref, gain_ref, shift_ref, wb_ref, bias_s, cot_s, sems,
):
    copies = fetch(
        [(gain_hbm, gain_ref), (shift_hbm, shift_ref), (wb_hbm, wb_ref), (x_hbm, x_ref), (cot_hbm, cot_ref)],
        sems,
    )
    bias_s[...] = jnp.zeros_like(bias_s)
    for copy in copies[0:4]:
        copy.wait()
    gain, shift = gain_ref[0:1], shift_ref[0:1]
    wb = w_bias_rows(wb_ref, 0)
    for i in range(ROWS):
        normed, _inv = normalise(x_ref[i].astype(F32))
        nx = (normed * gain + shift).astype(BF16)
        bias_s[i, :, 0:N] = bias_rows(nx, wb)[0:HEADS]
    copies[4].wait()
    for i in range(ROWS):
        cot_s[pl.ds(i, N, stride=ROWS), :] = cot_ref[i].astype(F32)
    bias = bias_s[...].reshape(BROWS, CH).astype(BF16)
    for e in range(GROUP):
        msg_ref[e, 0:BLOCK] = cot_s[e * BLOCK : (e + 1) * BLOCK].astype(BF16)
        msg_ref[e, BLOCK:PACK] = bias


def k1b_body(
    x_ref, gain_ref, shift_ref, wp_ref, gb_ref, q_ref, k_ref, v_ref, gate_ref, nx_ref, norm_ref, inv_ref
):
    gain, shift = gain_ref[0:1], shift_ref[0:1]
    for i in range(ROWS):
        normed, inverse = normalise(x_ref[i].astype(F32))
        nx_ref[i * N : (i + 1) * N] = (normed * gain + shift).astype(BF16)
        norm_ref[i] = normed
        inv_ref[i] = jnp.broadcast_to(inverse, (N, CH))
    for i in range(ROWS):
        q, k, v, gate = project(nx_ref[i * N : (i + 1) * N], wp_ref[0], gb_ref[0:1])
        q_ref[i] = q
        k_ref[i] = k
        v_ref[i] = v
        gate_ref[i] = gate


def gather_rows(recv_ref, flat_s, row_s):
    for d in range(GROUP):
        flat_s[d * BLOCK : (d + 1) * BLOCK] = recv_ref[d, 0:BLOCK].astype(F32)
    for i in range(ROWS):
        for d in range(GROUP):
            at = d * BLOCK + i * ROWS
            row_s[i, d * ROWS : (d + 1) * ROWS] = flat_s[at : at + ROWS]


def k2_body(
    x_ref, q_ref, k_ref, v_ref, gate_ref, recv_ref, mask_ref, wo_ref, ob_ref, gain_ref, shift_ref, wb_ref,
    part_ref, mixed_ref, probs_ref, nx_ref, norm_ref, inv_ref, msg_ref,
    raw_s, own_s, first_s, row_ref, bias_ref, att_s,
):
    key = key_column(mask_ref)
    for d in range(GROUP):
        raw_s[d * BROWS : (d + 1) * BROWS] = recv_ref[d, BLOCK:PACK].astype(F32)
    for h in range(HEADS):
        bias_ref[h] = raw_s[pl.ds(h, N, stride=HEADS), :].T[0:N] + key
    wb = w_bias_rows(wb_ref, 1)
    w_out = wo_ref[0]
    out_bias = ob_ref[0:1]
    gain, shift = gain_ref[1:2], shift_ref[1:2]
    own_s[...] = jnp.zeros_like(own_s)
    for i in range(ROWS):
        probs = probabilities(q_ref[i], k_ref[i], bias_ref)
        for h in range(HEADS):
            probs_ref[i, h] = probs[h]
        att_s[i] = weighted(v_ref[i], [p.astype(BF16) for p in probs])
    for i in range(ROWS):
        gate = gate_ref[i]
        gated = gate * att_s[i]
        part_ref[i] = gated * (1.0 - gate)
        mixed = gated.astype(BF16)
        mixed_ref[i * N : (i + 1) * N] = mixed
    for i in range(ROWS):
        mixed = mixed_ref[i * N : (i + 1) * N]
        first = x_ref[i].astype(F32) + dot_nn(mixed, w_out) + out_bias
        first = first.astype(BF16)
        row_ref[i] = first
        first_s[pl.ds(i, N, stride=ROWS), :] = first.astype(F32)
    for i in range(ROWS):
        normed, inverse = normalise(row_ref[i].astype(F32))
        nx = (normed * gain + shift).astype(BF16)
        nx_ref[i] = nx
        norm_ref[i] = normed
        inv_ref[i] = jnp.broadcast_to(inverse, (N, CH))
        own_s[i, :, 0:N] = bias_rows(nx, wb)[0:HEADS]
    bias = own_s[...].reshape(BROWS, CH).astype(BF16)
    for e in range(GROUP):
        msg_ref[e, 0:BLOCK] = first_s[e * BLOCK : (e + 1) * BLOCK].astype(BF16)
        msg_ref[e, BLOCK:PACK] = bias


def k2b_body(recv_ref, wo_ref, up_ref, gm_ref, total_ref, flat_s, row_s):
    gather_rows(recv_ref, flat_s, row_s)
    total = jnp.zeros((8, CH), F32)
    for i in range(ROWS):
        up_f = row_s[i]
        total += fold8(up_f)
        up = up_f.astype(BF16)
        up_ref[i * N : (i + 1) * N] = up
        gm_ref[i] = dot_nt(up, wo_ref[1])
    total_ref[...] = total


def weight_grads(nx_ref, joint_ref, mixed_ref, up_ref, put):
    nx = nx_ref[...]
    for block in range(4):
        put(block, dot_tn(nx, joint_ref[:, block * CH : (block + 1) * CH]))
    put(4, dot_tn(mixed_ref[...], up_ref[...]))


def split2(x):
    top = x.astype(BF16)
    return top, (x - top.astype(F32)).astype(BF16)


def put_sums(msg_ref, e, start, rows):
    msg_ref[e, start : start + BROWS, 0:N] = rows.astype(BF16)
    msg_ref[e, start : start + BROWS, N:CH] = jnp.zeros((BROWS, CH - N), BF16)


def k3_body(
    recv_ref, mask_ref, gm_ref, gain_ref, shift_ref, wp_ref, gb_ref,
    msg_ref, small_ref, nx_ref, joint_ref, mixed_ref,
    flat_s, x_s, raw_s, bias_s, sum_s, norm_s, inv_s, q_s, k_s, v_s, gate_s, att_s, probs_s, grad_s, scores_s,
):
    key = key_column(mask_ref)
    for d in range(GROUP):
        raw_s[d * BROWS : (d + 1) * BROWS] = recv_ref[d, BLOCK:PACK].astype(F32)
    for h in range(HEADS):
        bias_s[h] = raw_s[pl.ds(h, N, stride=HEADS), :][:, 0:N] + key
    gather_rows(recv_ref, flat_s, x_s)
    sum_s[...] = jnp.zeros_like(sum_s)
    gain, shift = gain_ref[1:2], shift_ref[1:2]
    gate_bias = gb_ref[1:2]
    for i in range(ROWS):
        normed, inverse = normalise(x_s[i])
        nx_ref[i * N : (i + 1) * N] = (normed * gain + shift).astype(BF16)
        norm_s[i] = normed
        inv_s[i] = jnp.broadcast_to(inverse, (N, CH))
    for i in range(ROWS):
        q_s[i], k_s[i], v_s[i], gate_s[i] = project(nx_ref[i * N : (i + 1) * N], wp_ref[1], gate_bias)
    for i in range(ROWS):
        probs = probabilities(q_s[i], k_s[i], bias_s)
        for h in range(HEADS):
            probs_s[i, h] = probs[h]
        att_s[i] = weighted(v_s[i], [p.astype(BF16) for p in probs])
    logit_sum = jnp.zeros((8, CH), F32)
    for i in range(ROWS):
        gate, att = gate_s[i], att_s[i]
        mixed_ref[i * N : (i + 1) * N] = (gate * att).astype(BF16)
        grad_s[i], grad_logit = gate_back(gm_ref[i], gate, att * gate * (1.0 - gate))
        joint_ref[i * N : (i + 1) * N, 3 * CH :] = grad_logit
        logit_sum += fold8(grad_logit.astype(F32))
    for i in range(ROWS):
        scores_back(i, probs_s, v_s, grad_s, sum_s, scores_s)
    joint_back(probs_s, scores_s, q_s, k_s, grad_s, joint_ref)
    gain_sum = jnp.zeros((8, CH), F32)
    shift_sum = jnp.zeros((8, CH), F32)
    for i in range(ROWS):
        grad_normed = dot_nt(joint_ref[i * N : (i + 1) * N], wp_ref[1])
        normed = norm_s[i]
        flat_s[pl.ds(i, N, stride=ROWS), :] = norm_back(grad_normed, gain, normed, inv_s[i])
        gain_sum += fold8(grad_normed * normed)
        shift_sum += fold8(grad_normed)
    small_ref[0:8] = gain_sum
    small_ref[8:16] = shift_sum
    small_ref[16:24] = logit_sum
    for e in range(GROUP):
        msg_ref[e, 0:BLOCK] = flat_s[e * BLOCK : (e + 1) * BLOCK].astype(BF16)
        rows = [sum_s[h, e * ROWS : (e + 1) * ROWS] for h in range(HEADS)]
        put_sums(msg_ref, e, BLOCK, jnp.concatenate(rows, axis=0))


def k3w_body(nx_ref, joint_ref, mixed_ref, up_ref, out_ref):
    def put(block, part):
        part = part.astype(BF16)
        for e in range(GROUP):
            out_ref[e, block * SLICE : (block + 1) * SLICE] = part[e * SLICE : (e + 1) * SLICE]

    weight_grads(nx_ref, joint_ref, mixed_ref, up_ref, put)


def bias_sum(recv_ref, start, gb_s):
    total = recv_ref[0, start : start + BROWS].astype(F32)
    for d in range(1, GROUP):
        total += recv_ref[d, start : start + BROWS].astype(F32)
    gb_s[...] = jnp.zeros_like(gb_s)
    for r in range(ROWS):
        for h in range(HEADS):
            gb_s[r * 8 + h : r * 8 + h + 1] = total[h * ROWS + r : h * ROWS + r + 1]
    return jnp.concatenate(split2(gb_s[...].T[0:N]), axis=1)


def bias_part(i, gb_s, gb_t, wb_tiled, nx):
    rows = lax.broadcasted_iota(jnp.int32, (ROWS * 8, CH), 0) // 8
    picked = jnp.where(rows == i, wb_tiled, jnp.zeros_like(wb_tiled))
    top, low = split2(gb_s[i * 8 : (i + 1) * 8, 0:N])
    return dot_nn(gb_t, jnp.concatenate([picked, picked], axis=0)), dot_nn(top, nx) + dot_nn(low, nx)


def k4_body(
    recv_ref, cot_ref, q_ref, k_ref, v_ref, gate_ref, part_ref, probs_ref, mixed_ref, nx_ref,
    nx1_ref, norm1_ref, inv1_ref, gain_ref, wp_ref, wb_ref, wo_ref, wg1_ref,
    up_ref, gn_ref, msg_ref, small_ref,
    flat_s, la_s, gb_s, sum_s, joint_s, grad_s, upb_s, scores_s,
):
    gather_rows(recv_ref, flat_s, la_s)
    gb_t = bias_sum(recv_ref, BLOCK, gb_s)
    wb = w_bias_rows(wb_ref, 1)
    wb_tiled = jnp.concatenate([wb.astype(F32)] * ROWS, axis=0).astype(BF16)
    sum_s[...] = jnp.zeros_like(sum_s)
    gain1 = gain_ref[1:2]
    zero = jnp.zeros((8, CH), F32)
    gain_sum, shift_sum, bias_w, logit_sum, up_sum = zero, zero, zero, zero, zero
    for i in range(ROWS):
        from_bias, grad_w = bias_part(i, gb_s, gb_t, wb_tiled, nx1_ref[i])
        normed = norm1_ref[i]
        gain_sum += fold8(from_bias * normed)
        shift_sum += fold8(from_bias)
        bias_w += grad_w
        up_f = cot_ref[i].astype(F32) + la_s[i] + norm_back(from_bias, gain1, normed, inv1_ref[i])
        up = up_f.astype(BF16)
        up_ref[i] = up
        upb_s[i * N : (i + 1) * N] = up
        up_sum += fold8(up.astype(F32))
    for i in range(ROWS):
        grad_mixed = dot_nt(up_ref[i], wo_ref[0])
        grad_s[i], grad_logit = gate_back(grad_mixed, gate_ref[i], part_ref[i])
        joint_s[i * N : (i + 1) * N, 3 * CH :] = grad_logit
        logit_sum += fold8(grad_logit.astype(F32))
    for i in range(ROWS):
        scores_back(i, probs_ref, v_ref, grad_s, sum_s, scores_s)
    joint_back(probs_ref, scores_s, q_ref, k_ref, grad_s, joint_s)
    for i in range(ROWS):
        gn_ref[i] = dot_nt(joint_s[i * N : (i + 1) * N], wp_ref[0])
    small_ref[0:8] = gain_sum
    small_ref[8:16] = shift_sum
    small_ref[16:24] = bias_w
    small_ref[24:32] = logit_sum
    small_ref[32:40] = up_sum
    for h in range(HEADS):
        flat_s[h * N : (h + 1) * N, 0:N] = sum_s[h].T
    for e in range(GROUP):
        rows = [flat_s[h * N + e * ROWS : h * N + (e + 1) * ROWS, 0:N] for h in range(HEADS)]
        put_sums(msg_ref, e, 2 * WROWS, jnp.concatenate(rows, axis=0))
        msg_ref[e, WROWS : 2 * WROWS] = wg1_ref[e]

    def put(block, part):
        part = part.astype(BF16)
        for e in range(GROUP):
            msg_ref[e, block * SLICE : (block + 1) * SLICE] = part[e * SLICE : (e + 1) * SLICE]

    weight_grads(nx_ref, joint_s, mixed_ref, upb_s, put)


def k5_body(
    recv_ref, norm_ref, gn_ref, nx_ref, small1_ref, total1_ref, small_ref, wb_ref,
    full_ref, msg_ref, gb_s,
):
    gb_t = bias_sum(recv_ref, 2 * WROWS, gb_s)
    wb = w_bias_rows(wb_ref, 0)
    wb_tiled = jnp.concatenate([wb.astype(F32)] * ROWS, axis=0).astype(BF16)
    zero = jnp.zeros((8, CH), F32)
    gain_sum, shift_sum, bias_w = zero, zero, zero
    for i in range(ROWS):
        from_bias, grad_w = bias_part(i, gb_s, gb_t, wb_tiled, nx_ref[i * N : (i + 1) * N])
        grad_normed = gn_ref[i] + from_bias
        full_ref[i] = grad_normed
        gain_sum += fold8(grad_normed * norm_ref[i])
        shift_sum += fold8(grad_normed)
        bias_w += grad_w
    total = recv_ref[0, 0 : 2 * WROWS].astype(F32)
    for d in range(1, GROUP):
        total += recv_ref[d, 0 : 2 * WROWS].astype(F32)
    total *= 1.0 / N
    total = total.astype(BF16)

    def one(x):
        return jnp.sum(x, axis=0, keepdims=True)

    rows = [
        one(gain_sum), one(shift_sum), one(small_ref[24:32]), one(small_ref[32:40]), bias_w[0:HEADS],
        one(small1_ref[0:8] + small_ref[0:8]), one(small1_ref[8:16] + small_ref[8:16]),
        one(small1_ref[16:24]), one(total1_ref[...]), small_ref[16 : 16 + HEADS],
    ]
    top, low = split2(jnp.concatenate(rows, axis=0))
    for e in range(GROUP):
        msg_ref[e, 0 : 2 * WROWS] = total
        msg_ref[e, 2 * WROWS : 2 * WROWS + 16] = top
        msg_ref[e, 2 * WROWS + 16 : 2 * WROWS + 32] = low


def k5b_body(full_ref, norm_ref, inv_ref, up_ref, gain_ref, out_ref):
    gain = gain_ref[0:1]
    for i in range(ROWS):
        back = norm_back(full_ref[i], gain, norm_ref[i], inv_ref[i])
        out_ref[i] = (up_ref[i].astype(F32) + back).astype(BF16)


def k6_body(recv_ref, gain_ref, shift_ref, proj_ref, wb_ref, gate_ref, ow_ref, ob_ref):
    small = jnp.zeros((16, CH), F32)
    for d in range(GROUP):
        for m in range(2):
            for block in range(4):
                at = m * WROWS + block * SLICE
                proj_ref[m, d * SLICE : (d + 1) * SLICE, block * CH : (block + 1) * CH] = recv_ref[
                    d, at : at + SLICE
                ].astype(F32)
            at = m * WROWS + 4 * SLICE
            ow_ref[m, d * SLICE : (d + 1) * SLICE] = recv_ref[d, at : at + SLICE].astype(F32)
        at = 2 * WROWS
        small += recv_ref[d, at : at + 16].astype(F32) + recv_ref[d, at + 16 : at + 32].astype(F32)
    small = small * (1.0 / N)
    for m in range(2):
        at = m * 8
        gain_ref[m : m + 1] = small[at : at + 1]
        shift_ref[m : m + 1] = small[at + 1 : at + 2]
        gate_ref[m : m + 1] = small[at + 2 : at + 3]
        ob_ref[m : m + 1] = small[at + 3 : at + 4]
        wb_ref[m] = small[at + 4 : at + 8]


def call(body, outs, scratch, name, far=(), far_out=(), copies=0, flops=100000000, big=False):
    near_spec = pl.BlockSpec(memory_space=pltpu.VMEM)
    far_spec = pl.BlockSpec(memory_space=pltpu.HBM)
    scratch = [pltpu.VMEM(shape, dtype) for shape, dtype in scratch]
    if copies:
        scratch.append(pltpu.SemaphoreType.DMA((copies,)) if copies > 1 else pltpu.SemaphoreType.DMA)

    def run(*args):
        return pl.pallas_call(
            body,
            in_specs=[far_spec if n in far else near_spec for n in range(len(args))],
            out_specs=[far_spec if n in far_out else near_spec for n in range(len(outs))],
            out_shape=[jax.ShapeDtypeStruct(shape, dtype) for shape, dtype in outs],
            scratch_shapes=scratch,
            compiler_params=pltpu.CompilerParams(vmem_limit_bytes=(62 if big else 24) * 1024 * 1024),
            cost_estimate=pl.CostEstimate(flops=flops, bytes_accessed=2000000, transcendentals=500000),
            name=name,
        )(*args)

    return run


def after(x, y):
    return lax.optimization_barrier((x, y))[0]


def swap(x):
    return lax.all_to_all(x, "dap", 0, 0, tiled=True)


def per_device(
    pair_rep, cotangent, residue_mask, ln_gain, ln_shift, w_proj, w_bias, gate_bias, w_out, out_bias
):
    mask = residue_mask.reshape(1, N)
    w_bias = jnp.swapaxes(w_bias, 1, 2)
    rows_b = ((ROWS, N, CH), BF16)
    rows_f = ((ROWS, N, CH), F32)
    flat_f = ((CELLS, CH), F32)
    flat_b = ((CELLS, CH), BF16)
    joint_b = ((CELLS, 4 * CH), BF16)
    pack = ((GROUP, PACK, CH), BF16)
    mats = ((HEADS, N, N), F32)
    probs = ((ROWS, HEADS, N, N), F32)
    raw = ((GROUP * BROWS, CH), F32)
    own_bias = ((ROWS, HEADS, CH), F32)
    bias_8 = ((ROWS * 8, CH), F32)

    vec_f = ((2, CH), F32)

    (msg0,) = call(
        k1_body,
        [pack],
        [rows_b, rows_b, vec_f, vec_f, ((2, HEADS, CH), BF16), own_bias, flat_f],
        "norm_first",
        far=range(5),
        copies=5,
        big=True,
    )(pair_rep, cotangent, ln_gain, ln_shift, w_bias)
    recv0 = swap(msg0)
    q, k, v, gate, nx0, norm0, inv0 = call(
        k1b_body, [rows_b, rows_b, rows_b, rows_f, flat_b, rows_f, rows_f], [], "project_first"
    )(pair_rep, ln_gain, ln_shift, w_proj, gate_bias)
    part0, mixed0, probs0, nx1, norm1, inv1, msg1 = call(
        k2_body,
        [rows_f, flat_b, probs, rows_b, rows_f, rows_f, pack],
        [raw, own_bias, flat_f, rows_b, mats, rows_f],
        "attend_first",
    )(pair_rep, q, k, v, gate, recv0, mask, w_out, out_bias, ln_gain, ln_shift, w_bias)
    recv1 = swap(msg1)
    up1, gm1, total1 = call(
        k2b_body, [flat_b, rows_f, ((8, CH), F32)], [flat_f, rows_f], "cotangent_rows"
    )(after(recv0, recv1), w_out)
    msg2, small1, nxw, joint1, mixed1 = call(
        k3_body,
        [pack, ((24, CH), F32), flat_b, joint_b, flat_b],
        [flat_f, rows_f, raw, mats, mats, rows_f, rows_f]
        + [rows_b, rows_b, rows_b, rows_f, rows_f, probs, rows_b, ((ROWS, HEADS, N, N), BF16)],
        "second_module",
    )(recv1, mask, gm1, ln_gain, ln_shift, w_proj, gate_bias)
    recv2 = swap(msg2)
    (wg1,) = call(k3w_body, [((GROUP, WROWS, CH), BF16)], [], "second_weights")(
        after(nxw, recv2), joint1, mixed1, up1
    )
    up, gn, msg3, small = call(
        k4_body,
        [rows_b, rows_f, ((GROUP, 2 * WROWS + BROWS, CH), BF16), ((40, CH), F32)],
        [flat_f, rows_f, bias_8, mats, joint_b, rows_b, flat_b, ((ROWS, HEADS, N, N), BF16)],
        "back_first",
    )(
        recv2, cotangent, q, k, v, gate, part0, probs0, mixed0, nx0, nx1, norm1, inv1,
        ln_gain, w_proj, w_bias, w_out, wg1,
    )
    recv3 = swap(msg3)
    full, msg4 = call(
        k5_body, [rows_f, ((GROUP, 2 * WROWS + 32, CH), BF16)], [bias_8], "grad_sums"
    )(recv3, norm0, gn, nx0, small1, total1, small, w_bias)
    recv4 = swap(msg4)
    (grad_pair,) = call(k5b_body, [rows_b], [], "grad_pair")(after(full, recv4), norm0, inv0, up, ln_gain)
    grad_gain, grad_shift, grad_proj, grad_bias_w, grad_gate, grad_out_w, grad_out_bias = call(
        k6_body,
        [
            ((2, CH), F32), ((2, CH), F32), ((2, CH, 4 * CH), F32), ((2, HEADS, CH), F32),
            ((2, CH), F32), ((2, CH, CH), F32), ((2, CH), F32),
        ],
        [],
        "weight_sums",
    )(recv4)
    return (
        grad_pair, grad_gain, grad_shift, grad_proj, jnp.swapaxes(grad_bias_w, 1, 2), grad_gate,
        grad_out_w, grad_out_bias,
    )


def solution(mesh):
    in_specs = (
        P(("dp", "dap"), None, None),
        P(("dp", "dap"), None, None),
        P("dp"),
        P(),
        P(),
        P(),
        P(),
        P(),
        P(),
        P(),
    )
    out_specs = (
        P(("dp", "dap"), None, None),
        P("dp", None),
        P("dp", None),
        P("dp", None, None),
        P("dp", None, None),
        P("dp", None),
        P("dp", None, None),
        P("dp", None),
    )
    return jax.shard_map(
        per_device, mesh=mesh, in_specs=in_specs, out_specs=out_specs, check_vma=False
    )
```

```python
import functools

import jax
import jax.numpy as jnp
from jax import lax
from jax.experimental import pallas as pl
from jax.experimental.pallas import tpu as pltpu
from jax.sharding import PartitionSpec as P

HEADS = 4
WIDTH = 32
CH = 128
N = 96
GROUP = 8
ROWS = N // GROUP
CELLS = ROWS * N
BLOCK = ROWS * ROWS
BROWS = HEADS * ROWS
PACK = BLOCK + BROWS
SLICE = CH // GROUP
WROWS = 5 * SLICE
EPSILON = 1e-05
SCALING = WIDTH ** (-0.5)
F32 = jnp.float32
BF16 = jnp.bfloat16


def dot_nn(a, b):
    return lax.dot_general(a, b, (((1,), (0,)), ((), ())), preferred_element_type=F32)


def dot_nt(a, b):
    return lax.dot_general(a, b, (((1,), (1,)), ((), ())), preferred_element_type=F32)


def dot_tn(a, b):
    return lax.dot_general(a, b, (((0,), (0,)), ((), ())), preferred_element_type=F32)


def normalise(x):
    center = jnp.mean(x, axis=-1, keepdims=True)
    moved = x - center
    spread = jnp.mean(jnp.square(moved), axis=-1, keepdims=True)
    inverse = lax.rsqrt(spread + EPSILON)
    return moved * inverse, inverse


def norm_back(grad_normed, gain, normed, inverse):
    scaled = grad_normed * gain
    return inverse * (
        scaled
        - jnp.mean(scaled, axis=-1, keepdims=True)
        - normed * jnp.mean(scaled * normed, axis=-1, keepdims=True)
    )


def fold8(x):
    return jnp.sum(x.reshape(x.shape[0] // 8, 8, x.shape[1]), axis=0)


def head_stack(x):
    lane = lax.broadcasted_iota(jnp.int32, x.shape, 1) // WIDTH
    zero = jnp.zeros_like(x)
    return jnp.concatenate([jnp.where(lane == h, x, zero) for h in range(HEADS)], axis=0)


def head_pick(x):
    lane = lax.broadcasted_iota(jnp.int32, (N, CH), 1) // WIDTH
    out = x[0:N]
    for h in range(1, HEADS):
        out = jnp.where(lane == h, x[h * N : (h + 1) * N], out)
    return out


def project(nx, w_proj, gate_bias):
    joint = dot_nn(nx, w_proj)
    q = (joint[:, 0:CH] * SCALING).astype(BF16)
    k = joint[:, CH : 2 * CH].astype(BF16)
    v = joint[:, 2 * CH : 3 * CH].astype(BF16)
    gate = jax.nn.sigmoid(joint[:, 3 * CH :] + gate_bias)
    return q, k, v, gate


def probabilities(q, k, bias_ref):
    scores = dot_nt(head_stack(k), q)
    out = []
    for h in range(HEADS):
        s = scores[h * N : (h + 1) * N] + bias_ref[h]
        e = jnp.exp(s - jnp.max(s, axis=0, keepdims=True))
        out.append(e * (1.0 / jnp.sum(e, axis=0, keepdims=True)))
    return out


def weighted(x, mats):
    x_t = x.T
    parts = [dot_nn(x_t[h * WIDTH : (h + 1) * WIDTH], mats[h]) for h in range(HEADS)]
    return jnp.concatenate(parts, axis=0).T


def key_column(mask_ref):
    row = jnp.where(mask_ref[...] > 0, 0.0, -1000000000.0).astype(F32)
    wide = jnp.broadcast_to(row, (N, N))
    diag = lax.broadcasted_iota(jnp.int32, (N, N), 0) == lax.broadcasted_iota(jnp.int32, (N, N), 1)
    return jnp.sum(jnp.where(diag, wide, 0.0), axis=1, keepdims=True)


def scores_back(i, probs_ref, v_ref, grad_ref, sum_ref, scores_ref):
    grad_probs = dot_nt(head_stack(v_ref[i]), grad_ref[i])
    for h in range(HEADS):
        p = probs_ref[i, h]
        gp = grad_probs[h * N : (h + 1) * N]
        inner = jnp.sum(p * gp, axis=0, keepdims=True)
        ds = p * (gp - inner)
        sum_ref[h] += ds
        scores_ref[i, h] = ds.astype(BF16)


def joint_back(probs_ref, scores_ref, q_ref, k_ref, grad_ref, joint_ref):
    for i in range(ROWS):
        stack = jnp.concatenate([probs_ref[i, h].astype(BF16) for h in range(HEADS)], axis=0)
        grad_v = head_pick(dot_nn(stack, grad_ref[i]))
        joint_ref[i * N : (i + 1) * N, 2 * CH : 3 * CH] = grad_v.astype(BF16)
    for i in range(ROWS):
        stack = jnp.concatenate([scores_ref[i, h] for h in range(HEADS)], axis=0)
        grad_k = head_pick(dot_nn(stack, q_ref[i]))
        joint_ref[i * N : (i + 1) * N, CH : 2 * CH] = grad_k.astype(BF16)
    for i in range(ROWS):
        grad_q = weighted(k_ref[i], [scores_ref[i, h] for h in range(HEADS)]) * SCALING
        joint_ref[i * N : (i + 1) * N, 0:CH] = grad_q.astype(BF16)


def gate_back(grad_mixed, gate, part):
    return (grad_mixed * gate).astype(BF16), (grad_mixed * part).astype(BF16)


def bias_rows(nx, w_bias_t):
    return dot_nt(w_bias_t, nx)


def w_bias_rows(w_bias_ref, m):
    rows = w_bias_ref[m].astype(F32)
    return jnp.concatenate([rows, jnp.zeros((8 - HEADS, CH), F32)], axis=0).astype(BF16)


def fetch(pairs, sems):
    copies = [pltpu.make_async_copy(src, dst, sems.at[n]) for n, (src, dst) in enumerate(pairs)]
    for copy in copies:
        copy.start()
    return copies


def k1_body(
    x_hbm, cot_hbm, gain_hbm, shift_hbm, wb_hbm, msg_ref,
    x_ref, cot_ref, gain_ref, shift_ref, wb_ref, bias_s, cot_s, sems,
):
    copies = fetch(
        [(gain_hbm, gain_ref), (shift_hbm, shift_ref), (wb_hbm, wb_ref), (x_hbm, x_ref), (cot_hbm, cot_ref)],
        sems,
    )
    bias_s[...] = jnp.zeros_like(bias_s)
    for copy in copies[0:4]:
        copy.wait()
    gain, shift = gain_ref[0:1], shift_ref[0:1]
    wb = w_bias_rows(wb_ref, 0)
    for i in range(ROWS):
        normed, _inv = normalise(x_ref[i].astype(F32))
        nx = (normed * gain + shift).astype(BF16)
        bias_s[i, :, 0:N] = bias_rows(nx, wb)[0:HEADS]
    copies[4].wait()
    for i in range(ROWS):
        cot_s[pl.ds(i, N, stride=ROWS), :] = cot_ref[i].astype(F32)
    bias = bias_s[...].reshape(BROWS, CH).astype(BF16)
    for e in range(GROUP):
        msg_ref[e, 0:BLOCK] = cot_s[e * BLOCK : (e + 1) * BLOCK].astype(BF16)
        msg_ref[e, BLOCK:PACK] = bias


def k1b_body(
    x_ref, gain_ref, shift_ref, wp_ref, gb_ref, q_ref, k_ref, v_ref, gate_ref, nx_ref, norm_ref, inv_ref
):
    gain, shift = gain_ref[0:1], shift_ref[0:1]
    for i in range(ROWS):
        normed, inverse = normalise(x_ref[i].astype(F32))
        nx_ref[i * N : (i + 1) * N] = (normed * gain + shift).astype(BF16)
        norm_ref[i] = normed
        inv_ref[i] = jnp.broadcast_to(inverse, (N, CH))
    for i in range(ROWS):
        q, k, v, gate = project(nx_ref[i * N : (i + 1) * N], wp_ref[0], gb_ref[0:1])
        q_ref[i] = q
        k_ref[i] = k
        v_ref[i] = v
        gate_ref[i] = gate


def gather_rows(recv_ref, flat_s, row_s):
    for d in range(GROUP):
        flat_s[d * BLOCK : (d + 1) * BLOCK] = recv_ref[d, 0:BLOCK].astype(F32)
    for i in range(ROWS):
        for d in range(GROUP):
            at = d * BLOCK + i * ROWS
            row_s[i, d * ROWS : (d + 1) * ROWS] = flat_s[at : at + ROWS]


def k2_body(
    x_ref, q_ref, k_ref, v_ref, gate_ref, recv_ref, mask_ref, wo_ref, ob_ref, gain_ref, shift_ref, wb_ref,
    part_ref, mixed_ref, probs_ref, nx_ref, norm_ref, inv_ref, msg_ref,
    raw_s, own_s, first_s, row_ref, bias_ref, att_s,
):
    key = key_column(mask_ref)
    for d in range(GROUP):
        raw_s[d * BROWS : (d + 1) * BROWS] = recv_ref[d, BLOCK:PACK].astype(F32)
    for h in range(HEADS):
        bias_ref[h] = raw_s[pl.ds(h, N, stride=HEADS), :].T[0:N] + key
    wb = w_bias_rows(wb_ref, 1)
    w_out = wo_ref[0]
    out_bias = ob_ref[0:1]
    gain, shift = gain_ref[1:2], shift_ref[1:2]
    own_s[...] = jnp.zeros_like(own_s)
    for i in range(ROWS):
        probs = probabilities(q_ref[i], k_ref[i], bias_ref)
        for h in range(HEADS):
            probs_ref[i, h] = probs[h]
        att_s[i] = weighted(v_ref[i], [p.astype(BF16) for p in probs])
    for i in range(ROWS):
        gate = gate_ref[i]
        gated = gate * att_s[i]
        part_ref[i] = gated * (1.0 - gate)
        mixed = gated.astype(BF16)
        mixed_ref[i * N : (i + 1) * N] = mixed
    for i in range(ROWS):
        mixed = mixed_ref[i * N : (i + 1) * N]
        first = x_ref[i].astype(F32) + dot_nn(mixed, w_out) + out_bias
        first = first.astype(BF16)
        row_ref[i] = first
        first_s[pl.ds(i, N, stride=ROWS), :] = first.astype(F32)
    for i in range(ROWS):
        normed, inverse = normalise(row_ref[i].astype(F32))
        nx = (normed * gain + shift).astype(BF16)
        nx_ref[i] = nx
        norm_ref[i] = normed
        inv_ref[i] = jnp.broadcast_to(inverse, (N, CH))
        own_s[i, :, 0:N] = bias_rows(nx, wb)[0:HEADS]
    bias = own_s[...].reshape(BROWS, CH).astype(BF16)
    for e in range(GROUP):
        msg_ref[e, 0:BLOCK] = first_s[e * BLOCK : (e + 1) * BLOCK].astype(BF16)
        msg_ref[e, BLOCK:PACK] = bias


def k2b_body(recv_ref, wo_ref, up_ref, gm_ref, total_ref, flat_s, row_s):
    gather_rows(recv_ref, flat_s, row_s)
    total = jnp.zeros((8, CH), F32)
    for i in range(ROWS):
        up_f = row_s[i]
        total += fold8(up_f)
        up = up_f.astype(BF16)
        up_ref[i * N : (i + 1) * N] = up
        gm_ref[i] = dot_nt(up, wo_ref[1])
    total_ref[...] = total


def weight_grads(nx_ref, joint_ref, mixed_ref, up_ref, put):
    part = dot_tn(nx_ref[...], joint_ref[...])
    for block in range(4):
        put(block, part[:, block * CH : (block + 1) * CH])
    put(4, dot_tn(mixed_ref[...], up_ref[...]))


def split2(x):
    top = x.astype(BF16)
    return top, (x - top.astype(F32)).astype(BF16)


def put_sums(msg_ref, e, start, rows, rest):
    msg_ref[e, start : start + BROWS, 0:N] = rows.astype(BF16)
    msg_ref[e, start : start + BROWS, N:CH] = rest


def one(x):
    return jnp.sum(x, axis=0, keepdims=True)


def fold_lanes(x):
    return jnp.concatenate([x[:, g * WIDTH : (g + 1) * WIDTH] for g in range(4)], axis=0)


def unfold_lanes(x):
    r = x.shape[0] // 4
    return jnp.concatenate([x[g * r : (g + 1) * r] for g in range(4)], axis=1)


def k3_body(
    recv_ref, mask_ref, gm_ref, gain_ref, shift_ref, wp_ref, gb_ref,
    msg_ref, small_ref, nx_ref, joint_ref, mixed_ref,
    flat_s, x_s, raw_s, bias_s, sum_s, norm_s, inv_s, q_s, k_s, v_s, gate_s, att_s, probs_s, grad_s, scores_s,
):
    key = key_column(mask_ref)
    for d in range(GROUP):
        raw_s[d * BROWS : (d + 1) * BROWS] = recv_ref[d, BLOCK:PACK].astype(F32)
    for h in range(HEADS):
        bias_s[h] = raw_s[pl.ds(h, N, stride=HEADS), :][:, 0:N] + key
    gather_rows(recv_ref, flat_s, x_s)
    sum_s[...] = jnp.zeros_like(sum_s)
    gain, shift = gain_ref[1:2], shift_ref[1:2]
    gate_bias = gb_ref[1:2]
    for i in range(ROWS):
        normed, inverse = normalise(x_s[i])
        nx_ref[i * N : (i + 1) * N] = (normed * gain + shift).astype(BF16)
        norm_s[i] = normed
        inv_s[i] = jnp.broadcast_to(inverse, (N, CH))
    for i in range(ROWS):
        q_s[i], k_s[i], v_s[i], gate_s[i] = project(nx_ref[i * N : (i + 1) * N], wp_ref[1], gate_bias)
    for i in range(ROWS):
        probs = probabilities(q_s[i], k_s[i], bias_s)
        for h in range(HEADS):
            probs_s[i, h] = probs[h]
        att_s[i] = weighted(v_s[i], [p.astype(BF16) for p in probs])
    logit_sum = jnp.zeros((8, CH), F32)
    for i in range(ROWS):
        gate, att = gate_s[i], att_s[i]
        mixed_ref[i * N : (i + 1) * N] = (gate * att).astype(BF16)
        grad_s[i], grad_logit = gate_back(gm_ref[i], gate, att * gate * (1.0 - gate))
        joint_ref[i * N : (i + 1) * N, 3 * CH :] = grad_logit
        logit_sum += fold8(grad_logit.astype(F32))
    for i in range(ROWS):
        scores_back(i, probs_s, v_s, grad_s, sum_s, scores_s)
    joint_back(probs_s, scores_s, q_s, k_s, grad_s, joint_ref)
    gain_sum = jnp.zeros((8, CH), F32)
    shift_sum = jnp.zeros((8, CH), F32)
    for i in range(ROWS):
        grad_normed = dot_nt(joint_ref[i * N : (i + 1) * N], wp_ref[1])
        normed = norm_s[i]
        flat_s[pl.ds(i, N, stride=ROWS), :] = norm_back(grad_normed, gain, normed, inv_s[i])
        gain_sum += fold8(grad_normed * normed)
        shift_sum += fold8(grad_normed)
    small_ref[0:8] = gain_sum
    small_ref[8:16] = shift_sum
    small_ref[16:24] = logit_sum
    rest = jnp.zeros((BROWS, CH - N), BF16)
    for e in range(GROUP):
        msg_ref[e, 0:BLOCK] = flat_s[e * BLOCK : (e + 1) * BLOCK].astype(BF16)
        rows = [sum_s[h, e * ROWS : (e + 1) * ROWS] for h in range(HEADS)]
        put_sums(msg_ref, e, BLOCK, jnp.concatenate(rows, axis=0), rest)


def bias_sum(recv_ref, start, gb_s):
    total = recv_ref[0, start : start + BROWS].astype(F32)
    for d in range(1, GROUP):
        total += recv_ref[d, start : start + BROWS].astype(F32)
    gb_s[...] = jnp.zeros_like(gb_s)
    for r in range(ROWS):
        for h in range(HEADS):
            gb_s[r * 8 + h : r * 8 + h + 1] = total[h * ROWS + r : h * ROWS + r + 1]
    return jnp.concatenate(split2(gb_s[...].T[0:N]), axis=1), total[:, N:CH]


def bias_part(i, gb_s, gb_t, wb_tiled, nx):
    rows = lax.broadcasted_iota(jnp.int32, (ROWS * 8, CH), 0) // 8
    picked = jnp.where(rows == i, wb_tiled, jnp.zeros_like(wb_tiled))
    top, low = split2(gb_s[i * 8 : (i + 1) * 8, 0:N])
    return dot_nn(gb_t, jnp.concatenate([picked, picked], axis=0)), dot_nn(top, nx) + dot_nn(low, nx)


def k4_body(
    recv_ref, cot_ref, q_ref, k_ref, v_ref, gate_ref, part_ref, probs_ref, mixed_ref, nx_ref,
    nx1_ref, norm1_ref, inv1_ref, gain_ref, wp_ref, wb_ref, wo_ref,
    nxw_ref, joint1_ref, mixed1_ref, upw_ref, small1_ref, total1_ref,
    up_ref, gn_ref, msg_ref, small_ref,
    flat_s, la_s, gb_s, sum_s, joint_s, grad_s, upb_s, scores_s,
):
    gather_rows(recv_ref, flat_s, la_s)
    gb_t, _rest = bias_sum(recv_ref, BLOCK, gb_s)
    wb = w_bias_rows(wb_ref, 1)
    wb_tiled = jnp.concatenate([wb.astype(F32)] * ROWS, axis=0).astype(BF16)
    sum_s[...] = jnp.zeros_like(sum_s)
    gain1 = gain_ref[1:2]
    zero = jnp.zeros((8, CH), F32)
    gain_sum, shift_sum, bias_w, logit_sum, up_sum = zero, zero, zero, zero, zero
    for i in range(ROWS):
        from_bias, grad_w = bias_part(i, gb_s, gb_t, wb_tiled, nx1_ref[i])
        normed = norm1_ref[i]
        gain_sum += fold8(from_bias * normed)
        shift_sum += fold8(from_bias)
        bias_w += grad_w
        up_f = cot_ref[i].astype(F32) + la_s[i] + norm_back(from_bias, gain1, normed, inv1_ref[i])
        up = up_f.astype(BF16)
        up_ref[i] = up
        upb_s[i * N : (i + 1) * N] = up
        up_sum += fold8(up.astype(F32))
    for i in range(ROWS):
        grad_mixed = dot_nt(up_ref[i], wo_ref[0])
        grad_s[i], grad_logit = gate_back(grad_mixed, gate_ref[i], part_ref[i])
        joint_s[i * N : (i + 1) * N, 3 * CH :] = grad_logit
        logit_sum += fold8(grad_logit.astype(F32))
    for i in range(ROWS):
        scores_back(i, probs_ref, v_ref, grad_s, sum_s, scores_s)
    joint_back(probs_ref, scores_s, q_ref, k_ref, grad_s, joint_s)
    for i in range(ROWS):
        gn_ref[i] = dot_nt(joint_s[i * N : (i + 1) * N], wp_ref[0])
    small_ref[0:8] = logit_sum
    small_ref[8:16] = up_sum
    rows = [
        one(small1_ref[0:8] + gain_sum), one(small1_ref[8:16] + shift_sum), one(small1_ref[16:24]),
        one(total1_ref[...]), bias_w[0:HEADS],
    ]
    top, low = split2(jnp.concatenate(rows, axis=0))
    rest = [fold_lanes(top.astype(F32)), fold_lanes(low.astype(F32)[HEADS:8])]
    rest = jnp.concatenate(rest, axis=0).astype(BF16)
    for h in range(HEADS):
        flat_s[h * N : (h + 1) * N, 0:N] = sum_s[h].T
    for e in range(GROUP):
        rows = [flat_s[h * N + e * ROWS : h * N + (e + 1) * ROWS, 0:N] for h in range(HEADS)]
        put_sums(msg_ref, e, 2 * WROWS, jnp.concatenate(rows, axis=0), rest)

    def put(start, block, part):
        part = part.astype(BF16)
        for e in range(GROUP):
            at = start + block * SLICE
            msg_ref[e, at : at + SLICE] = part[e * SLICE : (e + 1) * SLICE]

    weight_grads(nx_ref, joint_s, mixed_ref, upb_s, functools.partial(put, 0))
    weight_grads(nxw_ref, joint1_ref, mixed1_ref, upw_ref, functools.partial(put, WROWS))


def k5_body(
    recv_ref, norm_ref, gn_ref, nx_ref, small_ref, wb_ref,
    full_ref, msg_ref, sums1_ref, gb_s,
):
    gb_t, rest = bias_sum(recv_ref, 2 * WROWS, gb_s)
    wb = w_bias_rows(wb_ref, 0)
    wb_tiled = jnp.concatenate([wb.astype(F32)] * ROWS, axis=0).astype(BF16)
    zero = jnp.zeros((8, CH), F32)
    gain_sum, shift_sum, bias_w = zero, zero, zero
    for i in range(ROWS):
        from_bias, grad_w = bias_part(i, gb_s, gb_t, wb_tiled, nx_ref[i * N : (i + 1) * N])
        grad_normed = gn_ref[i] + from_bias
        full_ref[i] = grad_normed
        gain_sum += fold8(grad_normed * norm_ref[i])
        shift_sum += fold8(grad_normed)
        bias_w += grad_w
    total = recv_ref[0, 0 : 2 * WROWS].astype(F32)
    for d in range(1, GROUP):
        total += recv_ref[d, 0 : 2 * WROWS].astype(F32)
    total *= 1.0 / N
    total = total.astype(BF16)
    sums1_ref[...] = unfold_lanes(rest[0:32])
    sums1_ref[HEADS:8] += unfold_lanes(rest[32:48])
    rows = [one(gain_sum), one(shift_sum), one(small_ref[0:8]), one(small_ref[8:16]), bias_w[0:HEADS]]
    sums = jnp.concatenate([part.astype(F32) for part in split2(jnp.concatenate(rows, axis=0))], axis=0)
    sums = sums.astype(BF16)
    for e in range(GROUP):
        msg_ref[e, 0 : 2 * WROWS] = total
        msg_ref[e, 2 * WROWS : 2 * WROWS + 16] = sums


def k5b_body(full_ref, norm_ref, inv_ref, up_ref, gain_ref, out_ref):
    gain = gain_ref[0:1]
    for i in range(ROWS):
        back = norm_back(full_ref[i], gain, norm_ref[i], inv_ref[i])
        out_ref[i] = (up_ref[i].astype(F32) + back).astype(BF16)


def k6_body(recv_ref, sums1_ref, gain_ref, shift_ref, proj_ref, wb_ref, gate_ref, ow_ref, ob_ref):
    small = jnp.zeros((8, CH), F32)
    for d in range(GROUP):
        for m in range(2):
            for block in range(4):
                at = m * WROWS + block * SLICE
                proj_ref[m, d * SLICE : (d + 1) * SLICE, block * CH : (block + 1) * CH] = recv_ref[
                    d, at : at + SLICE
                ].astype(F32)
            at = m * WROWS + 4 * SLICE
            ow_ref[m, d * SLICE : (d + 1) * SLICE] = recv_ref[d, at : at + SLICE].astype(F32)
        at = 2 * WROWS
        both = recv_ref[d, at : at + 16].astype(F32)
        small += both[0:8] + both[8:16]
    small = jnp.concatenate([small, sums1_ref[...]], axis=0) * (1.0 / N)
    for m in range(2):
        at = m * 8
        gain_ref[m : m + 1] = small[at : at + 1]
        shift_ref[m : m + 1] = small[at + 1 : at + 2]
        gate_ref[m : m + 1] = small[at + 2 : at + 3]
        ob_ref[m : m + 1] = small[at + 3 : at + 4]
        wb_ref[m] = small[at + 4 : at + 8]


def call(body, outs, scratch, name, far=(), far_out=(), copies=0, flops=100000000, big=False):
    near_spec = pl.BlockSpec(memory_space=pltpu.VMEM)
    far_spec = pl.BlockSpec(memory_space=pltpu.HBM)
    scratch = [pltpu.VMEM(shape, dtype) for shape, dtype in scratch]
    if copies:
        scratch.append(pltpu.SemaphoreType.DMA((copies,)) if copies > 1 else pltpu.SemaphoreType.DMA)

    def run(*args):
        return pl.pallas_call(
            body,
            in_specs=[far_spec if n in far else near_spec for n in range(len(args))],
            out_specs=[far_spec if n in far_out else near_spec for n in range(len(outs))],
            out_shape=[jax.ShapeDtypeStruct(shape, dtype) for shape, dtype in outs],
            scratch_shapes=scratch,
            compiler_params=pltpu.CompilerParams(vmem_limit_bytes=(62 if big else 24) * 1024 * 1024),
            cost_estimate=pl.CostEstimate(flops=flops, bytes_accessed=2000000, transcendentals=500000),
            name=name,
        )(*args)

    return run


def after(x, y):
    return lax.optimization_barrier((x, y))[0]


def swap(x):
    return lax.all_to_all(x, "dap", 0, 0, tiled=True)


def per_device(
    pair_rep, cotangent, residue_mask, ln_gain, ln_shift, w_proj, w_bias, gate_bias, w_out, out_bias
):
    mask = residue_mask.reshape(1, N)
    w_bias = jnp.swapaxes(w_bias, 1, 2)
    rows_b = ((ROWS, N, CH), BF16)
    rows_f = ((ROWS, N, CH), F32)
    flat_f = ((CELLS, CH), F32)
    flat_b = ((CELLS, CH), BF16)
    joint_b = ((CELLS, 4 * CH), BF16)
    pack = ((GROUP, PACK, CH), BF16)
    mats = ((HEADS, N, N), F32)
    probs = ((ROWS, HEADS, N, N), F32)
    raw = ((GROUP * BROWS, CH), F32)
    own_bias = ((ROWS, HEADS, CH), F32)
    bias_8 = ((ROWS * 8, CH), F32)

    vec_f = ((2, CH), F32)

    (msg0,) = call(
        k1_body,
        [pack],
        [rows_b, rows_b, vec_f, vec_f, ((2, HEADS, CH), BF16), own_bias, flat_f],
        "norm_first",
        far=range(5),
        copies=5,
        big=True,
    )(pair_rep, cotangent, ln_gain, ln_shift, w_bias)
    recv0 = swap(msg0)
    q, k, v, gate, nx0, norm0, inv0 = call(
        k1b_body, [rows_b, rows_b, rows_b, rows_f, flat_b, rows_f, rows_f], [], "project_first"
    )(pair_rep, ln_gain, ln_shift, w_proj, gate_bias)
    part0, mixed0, probs0, nx1, norm1, inv1, msg1 = call(
        k2_body,
        [rows_f, flat_b, probs, rows_b, rows_f, rows_f, pack],
        [raw, own_bias, flat_f, rows_b, mats, rows_f],
        "attend_first",
    )(pair_rep, q, k, v, gate, recv0, mask, w_out, out_bias, ln_gain, ln_shift, w_bias)
    recv1 = swap(msg1)
    up1, gm1, total1 = call(
        k2b_body, [flat_b, rows_f, ((8, CH), F32)], [flat_f, rows_f], "cotangent_rows"
    )(after(recv0, recv1), w_out)
    msg2, small1, nxw, joint1, mixed1 = call(
        k3_body,
        [pack, ((24, CH), F32), flat_b, joint_b, flat_b],
        [flat_f, rows_f, raw, mats, mats, rows_f, rows_f]
        + [rows_b, rows_b, rows_b, rows_f, rows_f, probs, rows_b, ((ROWS, HEADS, N, N), BF16)],
        "second_module",
    )(recv1, mask, gm1, ln_gain, ln_shift, w_proj, gate_bias)
    recv2 = swap(msg2)
    up, gn, msg3, small = call(
        k4_body,
        [rows_b, rows_f, ((GROUP, 2 * WROWS + BROWS, CH), BF16), ((16, CH), F32)],
        [flat_f, rows_f, bias_8, mats, joint_b, rows_b, flat_b, ((ROWS, HEADS, N, N), BF16)],
        "back_first",
    )(
        recv2, cotangent, q, k, v, gate, part0, probs0, mixed0, nx0, nx1, norm1, inv1,
        ln_gain, w_proj, w_bias, w_out, nxw, joint1, mixed1, up1, small1, total1,
    )
    recv3 = swap(msg3)
    full, msg4, sums1 = call(
        k5_body,
        [rows_f, ((GROUP, 2 * WROWS + 16, CH), BF16), ((8, CH), F32)],
        [bias_8],
        "grad_sums",
    )(recv3, norm0, gn, nx0, small, w_bias)
    recv4 = swap(msg4)
    (grad_pair,) = call(k5b_body, [rows_b], [], "grad_pair")(after(full, recv4), norm0, inv0, up, ln_gain)
    grad_gain, grad_shift, grad_proj, grad_bias_w, grad_gate, grad_out_w, grad_out_bias = call(
        k6_body,
        [
            ((2, CH), F32), ((2, CH), F32), ((2, CH, 4 * CH), F32), ((2, HEADS, CH), F32),
            ((2, CH), F32), ((2, CH, CH), F32), ((2, CH), F32),
        ],
        [],
        "weight_sums",
    )(recv4, sums1)
    return (
        grad_pair, grad_gain, grad_shift, grad_proj, jnp.swapaxes(grad_bias_w, 1, 2), grad_gate,
        grad_out_w, grad_out_bias,
    )


def solution(mesh):
    in_specs = (
        P(("dp", "dap"), None, None),
        P(("dp", "dap"), None, None),
        P("dp"),
        P(),
        P(),
        P(),
        P(),
        P(),
        P(),
        P(),
    )
    out_specs = (
        P(("dp", "dap"), None, None),
        P("dp", None),
        P("dp", None),
        P("dp", None, None),
        P("dp", None, None),
        P("dp", None),
        P("dp", None, None),
        P("dp", None),
    )
    return jax.shard_map(
        per_device, mesh=mesh, in_specs=in_specs, out_specs=out_specs, check_vma=False
    )
```

```python
import functools

import jax
import jax.numpy as jnp
from jax import lax
from jax.experimental import pallas as pl
from jax.experimental.pallas import tpu as pltpu
from jax.sharding import PartitionSpec as P

HEADS = 4
WIDTH = 32
CH = 128
N = 96
GROUP = 8
ROWS = N // GROUP
CELLS = ROWS * N
BLOCK = ROWS * ROWS
BROWS = HEADS * ROWS
PACK = BLOCK + BROWS
SLICE = CH // GROUP
WROWS = 5 * SLICE
EPSILON = 1e-05
SCALING = WIDTH ** (-0.5)
F32 = jnp.float32
BF16 = jnp.bfloat16


def dot_nn(a, b):
    return lax.dot_general(a, b, (((1,), (0,)), ((), ())), preferred_element_type=F32)


def dot_nt(a, b):
    return lax.dot_general(a, b, (((1,), (1,)), ((), ())), preferred_element_type=F32)


def dot_tn(a, b):
    return lax.dot_general(a, b, (((0,), (0,)), ((), ())), preferred_element_type=F32)


def normalise(x):
    center = jnp.mean(x, axis=-1, keepdims=True)
    moved = x - center
    spread = jnp.mean(jnp.square(moved), axis=-1, keepdims=True)
    inverse = lax.rsqrt(spread + EPSILON)
    return moved * inverse, inverse


def norm_back(grad_normed, gain, normed, inverse):
    scaled = grad_normed * gain
    return inverse * (
        scaled
        - jnp.mean(scaled, axis=-1, keepdims=True)
        - normed * jnp.mean(scaled * normed, axis=-1, keepdims=True)
    )


def fold8(x):
    return jnp.sum(x.reshape(x.shape[0] // 8, 8, x.shape[1]), axis=0)


def head_stack(x):
    lane = lax.broadcasted_iota(jnp.int32, x.shape, 1) // WIDTH
    zero = jnp.zeros_like(x)
    return jnp.concatenate([jnp.where(lane == h, x, zero) for h in range(HEADS)], axis=0)


def head_pick(x):
    lane = lax.broadcasted_iota(jnp.int32, (N, CH), 1) // WIDTH
    out = x[0:N]
    for h in range(1, HEADS):
        out = jnp.where(lane == h, x[h * N : (h + 1) * N], out)
    return out


def project(nx, w_proj, gate_bias):
    joint = dot_nn(nx, w_proj)
    q = (joint[:, 0:CH] * SCALING).astype(BF16)
    k = joint[:, CH : 2 * CH].astype(BF16)
    v = joint[:, 2 * CH : 3 * CH].astype(BF16)
    gate = jax.nn.sigmoid(joint[:, 3 * CH :] + gate_bias)
    return q, k, v, gate


def probabilities(q, k, bias_ref):
    scores = dot_nt(head_stack(k), q)
    out = []
    for h in range(HEADS):
        s = scores[h * N : (h + 1) * N] + bias_ref[h]
        e = jnp.exp(s - jnp.max(s, axis=0, keepdims=True))
        out.append(e * (1.0 / jnp.sum(e, axis=0, keepdims=True)))
    return out


def weighted(x, mats):
    x_t = x.T
    parts = [dot_nn(x_t[h * WIDTH : (h + 1) * WIDTH], mats[h]) for h in range(HEADS)]
    return jnp.concatenate(parts, axis=0).T


def key_column(mask_ref):
    row = jnp.where(mask_ref[...] > 0, 0.0, -1000000000.0).astype(F32)
    wide = jnp.broadcast_to(row, (N, N))
    diag = lax.broadcasted_iota(jnp.int32, (N, N), 0) == lax.broadcasted_iota(jnp.int32, (N, N), 1)
    return jnp.sum(jnp.where(diag, wide, 0.0), axis=1, keepdims=True)


def scores_back(i, probs_ref, v_ref, grad_ref, sum_ref, scores_ref):
    grad_probs = dot_nt(head_stack(v_ref[i]), grad_ref[i])
    for h in range(HEADS):
        p = probs_ref[i, h]
        gp = grad_probs[h * N : (h + 1) * N]
        inner = jnp.sum(p * gp, axis=0, keepdims=True)
        ds = p * (gp - inner)
        sum_ref[h] += ds
        scores_ref[i, h] = ds.astype(BF16)


def joint_back(probs_ref, scores_ref, q_ref, k_ref, grad_ref, joint_ref):
    for i in range(ROWS):
        stack = jnp.concatenate([probs_ref[i, h].astype(BF16) for h in range(HEADS)], axis=0)
        grad_v = head_pick(dot_nn(stack, grad_ref[i]))
        joint_ref[i * N : (i + 1) * N, 2 * CH : 3 * CH] = grad_v.astype(BF16)
    for i in range(ROWS):
        stack = jnp.concatenate([scores_ref[i, h] for h in range(HEADS)], axis=0)
        grad_k = head_pick(dot_nn(stack, q_ref[i]))
        joint_ref[i * N : (i + 1) * N, CH : 2 * CH] = grad_k.astype(BF16)
    for i in range(ROWS):
        grad_q = weighted(k_ref[i], [scores_ref[i, h] for h in range(HEADS)]) * SCALING
        joint_ref[i * N : (i + 1) * N, 0:CH] = grad_q.astype(BF16)


def gate_back(grad_mixed, gate, part):
    return (grad_mixed * gate).astype(BF16), (grad_mixed * part).astype(BF16)


def bias_rows(nx, w_bias_t):
    return dot_nt(w_bias_t, nx)


def w_bias_rows(w_bias_ref, m):
    rows = w_bias_ref[m].astype(F32)
    return jnp.concatenate([rows, jnp.zeros((8 - HEADS, CH), F32)], axis=0).astype(BF16)


def fetch(pairs, sems):
    copies = [pltpu.make_async_copy(src, dst, sems.at[n]) for n, (src, dst) in enumerate(pairs)]
    for copy in copies:
        copy.start()
    return copies


def k1_body(
    x_hbm, cot_hbm, gain_hbm, shift_hbm, wb_hbm, msg_ref,
    x_ref, cot_ref, gain_ref, shift_ref, wb_ref, bias_s, cot_s, sems,
):
    copies = fetch(
        [(gain_hbm, gain_ref), (shift_hbm, shift_ref), (wb_hbm, wb_ref), (x_hbm, x_ref), (cot_hbm, cot_ref)],
        sems,
    )
    bias_s[...] = jnp.zeros_like(bias_s)
    for copy in copies[0:4]:
        copy.wait()
    gain, shift = gain_ref[0:1], shift_ref[0:1]
    wb = w_bias_rows(wb_ref, 0)
    for i in range(ROWS):
        normed, _inv = normalise(x_ref[i].astype(F32))
        nx = (normed * gain + shift).astype(BF16)
        bias_s[i, :, 0:N] = bias_rows(nx, wb)[0:HEADS]
    copies[4].wait()
    for i in range(ROWS):
        cot_s[pl.ds(i, N, stride=ROWS), :] = cot_ref[i].astype(F32)
    bias = bias_s[...].reshape(BROWS, CH).astype(BF16)
    for e in range(GROUP):
        msg_ref[e, 0:BLOCK] = cot_s[e * BLOCK : (e + 1) * BLOCK].astype(BF16)
        msg_ref[e, BLOCK:PACK] = bias


def k1b_body(
    x_ref, gain_ref, shift_ref, wp_ref, gb_ref, q_ref, k_ref, v_ref, gate_ref, nx_ref, norm_ref, inv_ref
):
    gain, shift = gain_ref[0:1], shift_ref[0:1]
    for i in range(ROWS):
        normed, inverse = normalise(x_ref[i].astype(F32))
        nx_ref[i * N : (i + 1) * N] = (normed * gain + shift).astype(BF16)
        norm_ref[i] = normed
        inv_ref[i] = jnp.broadcast_to(inverse, (N, CH))
    for i in range(ROWS):
        q, k, v, gate = project(nx_ref[i * N : (i + 1) * N], wp_ref[0], gb_ref[0:1])
        q_ref[i] = q
        k_ref[i] = k
        v_ref[i] = v
        gate_ref[i] = gate


def gather_rows(recv_ref, flat_s, row_s):
    for d in range(GROUP):
        flat_s[d * BLOCK : (d + 1) * BLOCK] = recv_ref[d, 0:BLOCK].astype(F32)
    for i in range(ROWS):
        for d in range(GROUP):
            at = d * BLOCK + i * ROWS
            row_s[i, d * ROWS : (d + 1) * ROWS] = flat_s[at : at + ROWS]


def k2_body(
    x_ref, q_ref, k_ref, v_ref, gate_ref, recv_ref, mask_ref, wo_ref, ob_ref, gain_ref, shift_ref, wb_ref,
    part_ref, mixed_ref, probs_ref, nx_ref, norm_ref, inv_ref, msg_ref,
    raw_s, own_s, first_s, row_ref, bias_ref, att_s,
):
    key = key_column(mask_ref)
    for d in range(GROUP):
        raw_s[d * BROWS : (d + 1) * BROWS] = recv_ref[d, BLOCK:PACK].astype(F32)
    for h in range(HEADS):
        bias_ref[h] = raw_s[pl.ds(h, N, stride=HEADS), :].T[0:N] + key
    wb = w_bias_rows(wb_ref, 1)
    w_out = wo_ref[0]
    out_bias = ob_ref[0:1]
    gain, shift = gain_ref[1:2], shift_ref[1:2]
    own_s[...] = jnp.zeros_like(own_s)
    for i in range(ROWS):
        probs = probabilities(q_ref[i], k_ref[i], bias_ref)
        for h in range(HEADS):
            probs_ref[i, h] = probs[h]
        att_s[i] = weighted(v_ref[i], [p.astype(BF16) for p in probs])
    for i in range(ROWS):
        gate = gate_ref[i]
        gated = gate * att_s[i]
        part_ref[i] = gated * (1.0 - gate)
        mixed = gated.astype(BF16)
        mixed_ref[i * N : (i + 1) * N] = mixed
    for i in range(ROWS):
        mixed = mixed_ref[i * N : (i + 1) * N]
        first = x_ref[i].astype(F32) + dot_nn(mixed, w_out) + out_bias
        first = first.astype(BF16)
        row_ref[i] = first
        first_s[pl.ds(i, N, stride=ROWS), :] = first.astype(F32)
    for i in range(ROWS):
        normed, inverse = normalise(row_ref[i].astype(F32))
        nx = (normed * gain + shift).astype(BF16)
        nx_ref[i] = nx
        norm_ref[i] = normed
        inv_ref[i] = jnp.broadcast_to(inverse, (N, CH))
        own_s[i, :, 0:N] = bias_rows(nx, wb)[0:HEADS]
    bias = own_s[...].reshape(BROWS, CH).astype(BF16)
    for e in range(GROUP):
        msg_ref[e, 0:BLOCK] = first_s[e * BLOCK : (e + 1) * BLOCK].astype(BF16)
        msg_ref[e, BLOCK:PACK] = bias


def k2b_body(recv_ref, wo_ref, up_ref, gm_ref, total_ref, flat_s, row_s):
    gather_rows(recv_ref, flat_s, row_s)
    total = jnp.zeros((8, CH), F32)
    for i in range(ROWS):
        up_f = row_s[i]
        total += fold8(up_f)
        up = up_f.astype(BF16)
        up_ref[i * N : (i + 1) * N] = up
        gm_ref[i] = dot_nt(up, wo_ref[1])
    total_ref[...] = total


def weight_grads(nx_ref, joint_ref, mixed_ref, up_ref, put):
    part = dot_tn(nx_ref[...], joint_ref[...])
    for block in range(4):
        put(block, part[:, block * CH : (block + 1) * CH])
    put(4, dot_tn(mixed_ref[...], up_ref[...]))


def split2(x):
    top = x.astype(BF16)
    return top, (x - top.astype(F32)).astype(BF16)


def put_sums(msg_ref, e, start, rows, rest):
    msg_ref[e, start : start + BROWS, 0:N] = rows.astype(BF16)
    msg_ref[e, start : start + BROWS, N:CH] = rest


def one(x):
    return jnp.sum(x, axis=0, keepdims=True)


def fold_lanes(x):
    return jnp.concatenate([x[:, g * WIDTH : (g + 1) * WIDTH] for g in range(4)], axis=0)


def unfold_lanes(x):
    r = x.shape[0] // 4
    return jnp.concatenate([x[g * r : (g + 1) * r] for g in range(4)], axis=1)


def k3_body(
    recv_ref, mask_ref, gm_ref, gain_ref, shift_ref, wp_ref, gb_ref,
    msg_ref, small_ref, nx_ref, joint_ref, mixed_ref,
    flat_s, x_s, raw_s, bias_s, sum_s, norm_s, inv_s, q_s, k_s, v_s, gate_s, att_s, probs_s, grad_s, scores_s,
):
    key = key_column(mask_ref)
    for d in range(GROUP):
        raw_s[d * BROWS : (d + 1) * BROWS] = recv_ref[d, BLOCK:PACK].astype(F32)
    for h in range(HEADS):
        bias_s[h] = raw_s[pl.ds(h, N, stride=HEADS), :][:, 0:N] + key
    gather_rows(recv_ref, flat_s, x_s)
    sum_s[...] = jnp.zeros_like(sum_s)
    gain, shift = gain_ref[1:2], shift_ref[1:2]
    gate_bias = gb_ref[1:2]
    for i in range(ROWS):
        normed, inverse = normalise(x_s[i])
        nx_ref[i * N : (i + 1) * N] = (normed * gain + shift).astype(BF16)
        norm_s[i] = normed
        inv_s[i] = jnp.broadcast_to(inverse, (N, CH))
    for i in range(ROWS):
        q_s[i], k_s[i], v_s[i], gate_s[i] = project(nx_ref[i * N : (i + 1) * N], wp_ref[1], gate_bias)
    for i in range(ROWS):
        probs = probabilities(q_s[i], k_s[i], bias_s)
        for h in range(HEADS):
            probs_s[i, h] = probs[h]
        att_s[i] = weighted(v_s[i], [p.astype(BF16) for p in probs])
    logit_sum = jnp.zeros((8, CH), F32)
    for i in range(ROWS):
        gate, att = gate_s[i], att_s[i]
        mixed_ref[i * N : (i + 1) * N] = (gate * att).astype(BF16)
        grad_s[i], grad_logit = gate_back(gm_ref[i], gate, att * gate * (1.0 - gate))
        joint_ref[i * N : (i + 1) * N, 3 * CH :] = grad_logit
        logit_sum += fold8(grad_logit.astype(F32))
    for i in range(ROWS):
        scores_back(i, probs_s, v_s, grad_s, sum_s, scores_s)
    joint_back(probs_s, scores_s, q_s, k_s, grad_s, joint_ref)
    gain_sum = jnp.zeros((8, CH), F32)
    shift_sum = jnp.zeros((8, CH), F32)
    for i in range(ROWS):
        grad_normed = dot_nt(joint_ref[i * N : (i + 1) * N], wp_ref[1])
        normed = norm_s[i]
        flat_s[pl.ds(i, N, stride=ROWS), :] = norm_back(grad_normed, gain, normed, inv_s[i])
        gain_sum += fold8(grad_normed * normed)
        shift_sum += fold8(grad_normed)
    small_ref[0:8] = gain_sum
    small_ref[8:16] = shift_sum
    small_ref[16:24] = logit_sum
    rest = jnp.zeros((BROWS, CH - N), BF16)
    for e in range(GROUP):
        msg_ref[e, 0:BLOCK] = flat_s[e * BLOCK : (e + 1) * BLOCK].astype(BF16)
        rows = [sum_s[h, e * ROWS : (e + 1) * ROWS] for h in range(HEADS)]
        put_sums(msg_ref, e, BLOCK, jnp.concatenate(rows, axis=0), rest)


def bias_sum(recv_ref, start, gb_s):
    total = recv_ref[0, start : start + BROWS].astype(F32)
    for d in range(1, GROUP):
        total += recv_ref[d, start : start + BROWS].astype(F32)
    gb_s[...] = jnp.zeros_like(gb_s)
    for r in range(ROWS):
        for h in range(HEADS):
            gb_s[r * 8 + h : r * 8 + h + 1] = total[h * ROWS + r : h * ROWS + r + 1]
    return jnp.concatenate(split2(gb_s[...].T[0:N]), axis=1), total[:, N:CH]


def bias_part(i, gb_s, gb_t, wb_tiled, nx):
    rows = lax.broadcasted_iota(jnp.int32, (ROWS * 8, CH), 0) // 8
    picked = jnp.where(rows == i, wb_tiled, jnp.zeros_like(wb_tiled))
    top, low = split2(gb_s[i * 8 : (i + 1) * 8, 0:N])
    return dot_nn(gb_t, jnp.concatenate([picked, picked], axis=0)), dot_nn(top, nx) + dot_nn(low, nx)


def k4_body(
    recv_ref, cot_ref, q_ref, k_ref, v_ref, gate_ref, part_ref, probs_ref, mixed_ref, nx_ref,
    nx1_ref, norm1_ref, inv1_ref, gain_ref, wp_ref, wb_ref, wo_ref,
    nxw_ref, joint1_ref, mixed1_ref, upw_ref, small1_ref, total1_ref,
    up_ref, gn_ref, msg_ref, small_ref,
    flat_s, la_s, gb_s, sum_s, joint_s, grad_s, upb_s, scores_s,
):
    gather_rows(recv_ref, flat_s, la_s)
    gb_t, _rest = bias_sum(recv_ref, BLOCK, gb_s)
    wb = w_bias_rows(wb_ref, 1)
    wb_tiled = jnp.concatenate([wb.astype(F32)] * ROWS, axis=0).astype(BF16)
    sum_s[...] = jnp.zeros_like(sum_s)
    gain1 = gain_ref[1:2]
    zero = jnp.zeros((8, CH), F32)
    gain_sum, shift_sum, bias_w, logit_sum, up_sum = zero, zero, zero, zero, zero
    for i in range(ROWS):
        from_bias, grad_w = bias_part(i, gb_s, gb_t, wb_tiled, nx1_ref[i])
        normed = norm1_ref[i]
        gain_sum += fold8(from_bias * normed)
        shift_sum += fold8(from_bias)
        bias_w += grad_w
        up_f = cot_ref[i].astype(F32) + la_s[i] + norm_back(from_bias, gain1, normed, inv1_ref[i])
        up = up_f.astype(BF16)
        up_ref[i] = up
        upb_s[i * N : (i + 1) * N] = up
        up_sum += fold8(up.astype(F32))
    for i in range(ROWS):
        grad_mixed = dot_nt(up_ref[i], wo_ref[0])
        grad_s[i], grad_logit = gate_back(grad_mixed, gate_ref[i], part_ref[i])
        joint_s[i * N : (i + 1) * N, 3 * CH :] = grad_logit
        logit_sum += fold8(grad_logit.astype(F32))
    for i in range(ROWS):
        scores_back(i, probs_ref, v_ref, grad_s, sum_s, scores_s)
    joint_back(probs_ref, scores_s, q_ref, k_ref, grad_s, joint_s)
    for i in range(ROWS):
        gn_ref[i] = dot_nt(joint_s[i * N : (i + 1) * N], wp_ref[0])
    small_ref[0:8] = logit_sum
    small_ref[8:16] = up_sum
    rows = [
        one(small1_ref[0:8] + gain_sum), one(small1_ref[8:16] + shift_sum), one(small1_ref[16:24]),
        one(total1_ref[...]), bias_w[0:HEADS],
    ]
    top, low = split2(jnp.concatenate(rows, axis=0))
    rest = [fold_lanes(top.astype(F32)), fold_lanes(low.astype(F32)[HEADS:8])]
    rest = jnp.concatenate(rest, axis=0).astype(BF16)
    for h in range(HEADS):
        flat_s[h * N : (h + 1) * N, 0:N] = sum_s[h].T
    for e in range(GROUP):
        rows = [flat_s[h * N + e * ROWS : h * N + (e + 1) * ROWS, 0:N] for h in range(HEADS)]
        put_sums(msg_ref, e, 2 * WROWS, jnp.concatenate(rows, axis=0), rest)

    def put(start, block, part):
        part = part.astype(BF16)
        for e in range(GROUP):
            at = start + block * SLICE
            msg_ref[e, at : at + SLICE] = part[e * SLICE : (e + 1) * SLICE]

    weight_grads(nx_ref, joint_s, mixed_ref, upb_s, functools.partial(put, 0))
    weight_grads(nxw_ref, joint1_ref, mixed1_ref, upw_ref, functools.partial(put, WROWS))


def k5_body(
    recv_ref, norm_ref, gn_ref, nx_ref, small_ref, wb_ref,
    full_ref, msg_ref, sums1_ref, gb_s,
):
    gb_t, rest = bias_sum(recv_ref, 2 * WROWS, gb_s)
    wb = w_bias_rows(wb_ref, 0)
    wb_tiled = jnp.concatenate([wb.astype(F32)] * ROWS, axis=0).astype(BF16)
    zero = jnp.zeros((8, CH), F32)
    gain_sum, shift_sum, bias_w = zero, zero, zero
    for i in range(ROWS):
        from_bias, grad_w = bias_part(i, gb_s, gb_t, wb_tiled, nx_ref[i * N : (i + 1) * N])
        grad_normed = gn_ref[i] + from_bias
        full_ref[i] = grad_normed
        gain_sum += fold8(grad_normed * norm_ref[i])
        shift_sum += fold8(grad_normed)
        bias_w += grad_w
    total = recv_ref[0, 0 : 2 * WROWS].astype(F32)
    for d in range(1, GROUP):
        total += recv_ref[d, 0 : 2 * WROWS].astype(F32)
    total *= 1.0 / N
    total = total.astype(BF16)
    sums1_ref[...] = unfold_lanes(rest[0:32])
    sums1_ref[HEADS:8] += unfold_lanes(rest[32:48])
    rows = [one(gain_sum), one(shift_sum), one(small_ref[0:8]), one(small_ref[8:16]), bias_w[0:HEADS]]
    sums = jnp.concatenate([part.astype(F32) for part in split2(jnp.concatenate(rows, axis=0))], axis=0)
    sums = sums.astype(BF16)
    for e in range(GROUP):
        msg_ref[e, 0 : 2 * WROWS] = total
        msg_ref[e, 2 * WROWS : 2 * WROWS + 16] = sums


def k5b_body(full_ref, norm_ref, inv_ref, up_ref, gain_ref, out_ref):
    gain = gain_ref[0:1]
    for i in range(ROWS):
        back = norm_back(full_ref[i], gain, norm_ref[i], inv_ref[i])
        out_ref[i] = (up_ref[i].astype(F32) + back).astype(BF16)


def k6_body(
    recv_ref, sums1_ref, full_ref, norm_ref, inv_ref, up_ref, ln_gain_ref,
    out_ref, gain_ref, shift_ref, proj_ref, wb_ref, gate_ref, ow_ref, ob_ref,
):
    k5b_body(full_ref, norm_ref, inv_ref, up_ref, ln_gain_ref, out_ref)
    small = jnp.zeros((8, CH), F32)
    for d in range(GROUP):
        for m in range(2):
            for block in range(4):
                at = m * WROWS + block * SLICE
                proj_ref[m, d * SLICE : (d + 1) * SLICE, block * CH : (block + 1) * CH] = recv_ref[
                    d, at : at + SLICE
                ].astype(F32)
            at = m * WROWS + 4 * SLICE
            ow_ref[m, d * SLICE : (d + 1) * SLICE] = recv_ref[d, at : at + SLICE].astype(F32)
        at = 2 * WROWS
        both = recv_ref[d, at : at + 16].astype(F32)
        small += both[0:8] + both[8:16]
    small = jnp.concatenate([small, sums1_ref[...]], axis=0) * (1.0 / N)
    for m in range(2):
        at = m * 8
        gain_ref[m : m + 1] = small[at : at + 1]
        shift_ref[m : m + 1] = small[at + 1 : at + 2]
        gate_ref[m : m + 1] = small[at + 2 : at + 3]
        ob_ref[m : m + 1] = small[at + 3 : at + 4]
        wb_ref[m] = small[at + 4 : at + 8]


def call(body, outs, scratch, name, far=(), far_out=(), copies=0, flops=100000000, big=False):
    near_spec = pl.BlockSpec(memory_space=pltpu.VMEM)
    far_spec = pl.BlockSpec(memory_space=pltpu.HBM)
    scratch = [pltpu.VMEM(shape, dtype) for shape, dtype in scratch]
    if copies:
        scratch.append(pltpu.SemaphoreType.DMA((copies,)) if copies > 1 else pltpu.SemaphoreType.DMA)

    def run(*args):
        return pl.pallas_call(
            body,
            in_specs=[far_spec if n in far else near_spec for n in range(len(args))],
            out_specs=[far_spec if n in far_out else near_spec for n in range(len(outs))],
            out_shape=[jax.ShapeDtypeStruct(shape, dtype) for shape, dtype in outs],
            scratch_shapes=scratch,
            compiler_params=pltpu.CompilerParams(vmem_limit_bytes=(62 if big else 24) * 1024 * 1024),
            cost_estimate=pl.CostEstimate(flops=flops, bytes_accessed=2000000, transcendentals=500000),
            name=name,
        )(*args)

    return run


def after(x, y):
    return lax.optimization_barrier((x, y))[0]


def swap(x):
    return lax.all_to_all(x, "dap", 0, 0, tiled=True)


def per_device(
    pair_rep, cotangent, residue_mask, ln_gain, ln_shift, w_proj, w_bias, gate_bias, w_out, out_bias
):
    mask = residue_mask.reshape(1, N)
    w_bias = jnp.swapaxes(w_bias, 1, 2)
    rows_b = ((ROWS, N, CH), BF16)
    rows_f = ((ROWS, N, CH), F32)
    flat_f = ((CELLS, CH), F32)
    flat_b = ((CELLS, CH), BF16)
    joint_b = ((CELLS, 4 * CH), BF16)
    pack = ((GROUP, PACK, CH), BF16)
    mats = ((HEADS, N, N), F32)
    probs = ((ROWS, HEADS, N, N), F32)
    raw = ((GROUP * BROWS, CH), F32)
    own_bias = ((ROWS, HEADS, CH), F32)
    bias_8 = ((ROWS * 8, CH), F32)

    vec_f = ((2, CH), F32)

    (msg0,) = call(
        k1_body,
        [pack],
        [rows_b, rows_b, vec_f, vec_f, ((2, HEADS, CH), BF16), own_bias, flat_f],
        "norm_first",
        far=range(5),
        copies=5,
        big=True,
    )(pair_rep, cotangent, ln_gain, ln_shift, w_bias)
    recv0 = swap(msg0)
    q, k, v, gate, nx0, norm0, inv0 = call(
        k1b_body, [rows_b, rows_b, rows_b, rows_f, flat_b, rows_f, rows_f], [], "project_first"
    )(pair_rep, ln_gain, ln_shift, w_proj, gate_bias)
    part0, mixed0, probs0, nx1, norm1, inv1, msg1 = call(
        k2_body,
        [rows_f, flat_b, probs, rows_b, rows_f, rows_f, pack],
        [raw, own_bias, flat_f, rows_b, mats, rows_f],
        "attend_first",
    )(pair_rep, q, k, v, gate, recv0, mask, w_out, out_bias, ln_gain, ln_shift, w_bias)
    recv1 = swap(msg1)
    up1, gm1, total1 = call(
        k2b_body, [flat_b, rows_f, ((8, CH), F32)], [flat_f, rows_f], "cotangent_rows"
    )(after(recv0, recv1), w_out)
    msg2, small1, nxw, joint1, mixed1 = call(
        k3_body,
        [pack, ((24, CH), F32), flat_b, joint_b, flat_b],
        [flat_f, rows_f, raw, mats, mats, rows_f, rows_f]
        + [rows_b, rows_b, rows_b, rows_f, rows_f, probs, rows_b, ((ROWS, HEADS, N, N), BF16)],
        "second_module",
    )(recv1, mask, gm1, ln_gain, ln_shift, w_proj, gate_bias)
    recv2 = swap(msg2)
    up, gn, msg3, small = call(
        k4_body,
        [rows_b, rows_f, ((GROUP, 2 * WROWS + BROWS, CH), BF16), ((16, CH), F32)],
        [flat_f, rows_f, bias_8, mats, joint_b, rows_b, flat_b, ((ROWS, HEADS, N, N), BF16)],
        "back_first",
    )(
        recv2, cotangent, q, k, v, gate, part0, probs0, mixed0, nx0, nx1, norm1, inv1,
        ln_gain, w_proj, w_bias, w_out, nxw, joint1, mixed1, up1, small1, total1,
    )
    recv3 = swap(msg3)
    full, msg4, sums1 = call(
        k5_body,
        [rows_f, ((GROUP, 2 * WROWS + 16, CH), BF16), ((8, CH), F32)],
        [bias_8],
        "grad_sums",
    )(recv3, norm0, gn, nx0, small, w_bias)
    recv4 = swap(msg4)
    grad_pair, grad_gain, grad_shift, grad_proj, grad_bias_w, grad_gate, grad_out_w, grad_out_bias = call(
        k6_body,
        [
            rows_b, ((2, CH), F32), ((2, CH), F32), ((2, CH, 4 * CH), F32), ((2, HEADS, CH), F32),
            ((2, CH), F32), ((2, CH, CH), F32), ((2, CH), F32),
        ],
        [],
        "weight_sums",
    )(recv4, sums1, full, norm0, inv0, up, ln_gain)
    return (
        grad_pair, grad_gain, grad_shift, grad_proj, jnp.swapaxes(grad_bias_w, 1, 2), grad_gate,
        grad_out_w, grad_out_bias,
    )


def solution(mesh):
    in_specs = (
        P(("dp", "dap"), None, None),
        P(("dp", "dap"), None, None),
        P("dp"),
        P(),
        P(),
        P(),
        P(),
        P(),
        P(),
        P(),
    )
    out_specs = (
        P(("dp", "dap"), None, None),
        P("dp", None),
        P("dp", None),
        P("dp", None, None),
        P("dp", None, None),
        P("dp", None),
        P("dp", None, None),
        P("dp", None),
    )
    return jax.shard_map(
        per_device, mesh=mesh, in_specs=in_specs, out_specs=out_specs, check_vma=False
    )
```

```python
import functools

import jax
import jax.numpy as jnp
from jax import lax
from jax.experimental import pallas as pl
from jax.experimental.pallas import tpu as pltpu
from jax.sharding import PartitionSpec as P

HEADS = 4
WIDTH = 32
CH = 128
N = 96
GROUP = 8
ROWS = N // GROUP
CELLS = ROWS * N
BLOCK = ROWS * ROWS
BROWS = HEADS * ROWS
PACK = BLOCK + BROWS
SLICE = CH // GROUP
WROWS = 5 * SLICE
EPSILON = 1e-05
SCALING = WIDTH ** (-0.5)
F32 = jnp.float32
BF16 = jnp.bfloat16


def dot_nn(a, b):
    return lax.dot_general(a, b, (((1,), (0,)), ((), ())), preferred_element_type=F32)


def dot_nt(a, b):
    return lax.dot_general(a, b, (((1,), (1,)), ((), ())), preferred_element_type=F32)


def dot_tn(a, b):
    return lax.dot_general(a, b, (((0,), (0,)), ((), ())), preferred_element_type=F32)


def normalise(x):
    center = jnp.mean(x, axis=-1, keepdims=True)
    moved = x - center
    spread = jnp.mean(jnp.square(moved), axis=-1, keepdims=True)
    inverse = lax.rsqrt(spread + EPSILON)
    return moved * inverse, inverse


def norm_back(grad_normed, gain, normed, inverse):
    scaled = grad_normed * gain
    return inverse * (
        scaled
        - jnp.mean(scaled, axis=-1, keepdims=True)
        - normed * jnp.mean(scaled * normed, axis=-1, keepdims=True)
    )


def fold8(x):
    return jnp.sum(x.reshape(x.shape[0] // 8, 8, x.shape[1]), axis=0)


def head_stack(x):
    lane = lax.broadcasted_iota(jnp.int32, x.shape, 1) // WIDTH
    zero = jnp.zeros_like(x)
    return jnp.concatenate([jnp.where(lane == h, x, zero) for h in range(HEADS)], axis=0)


def head_pick(x):
    lane = lax.broadcasted_iota(jnp.int32, (N, CH), 1) // WIDTH
    out = x[0:N]
    for h in range(1, HEADS):
        out = jnp.where(lane == h, x[h * N : (h + 1) * N], out)
    return out


def project(nx, w_proj, gate_bias):
    joint = dot_nn(nx, w_proj)
    q = (joint[:, 0:CH] * SCALING).astype(BF16)
    k = joint[:, CH : 2 * CH].astype(BF16)
    v = joint[:, 2 * CH : 3 * CH].astype(BF16)
    gate = jax.nn.sigmoid(joint[:, 3 * CH :] + gate_bias)
    return q, k, v, gate


def probabilities(q, k, bias_ref):
    scores = dot_nt(head_stack(k), q)
    out = []
    for h in range(HEADS):
        s = scores[h * N : (h + 1) * N] + bias_ref[h]
        e = jnp.exp(s - jnp.max(s, axis=0, keepdims=True))
        out.append(e * (1.0 / jnp.sum(e, axis=0, keepdims=True)))
    return out


def weighted(x, mats):
    x_t = x.T
    parts = [dot_nn(x_t[h * WIDTH : (h + 1) * WIDTH], mats[h]) for h in range(HEADS)]
    return jnp.concatenate(parts, axis=0).T


def key_column(mask_ref):
    row = jnp.where(mask_ref[...] > 0, 0.0, -1000000000.0).astype(F32)
    wide = jnp.broadcast_to(row, (N, N))
    diag = lax.broadcasted_iota(jnp.int32, (N, N), 0) == lax.broadcasted_iota(jnp.int32, (N, N), 1)
    return jnp.sum(jnp.where(diag, wide, 0.0), axis=1, keepdims=True)


def scores_back(i, probs_ref, v_ref, grad_ref, sum_ref, scores_ref):
    grad_probs = dot_nt(head_stack(v_ref[i]), grad_ref[i])
    for h in range(HEADS):
        p = probs_ref[i, h]
        gp = grad_probs[h * N : (h + 1) * N]
        inner = jnp.sum(p * gp, axis=0, keepdims=True)
        ds = p * (gp - inner)
        sum_ref[h] += ds
        scores_ref[i, h] = ds.astype(BF16)


def joint_back(probs_ref, scores_ref, q_ref, k_ref, grad_ref, joint_ref):
    for i in range(ROWS):
        stack = jnp.concatenate([probs_ref[i, h].astype(BF16) for h in range(HEADS)], axis=0)
        grad_v = head_pick(dot_nn(stack, grad_ref[i]))
        joint_ref[i * N : (i + 1) * N, 2 * CH : 3 * CH] = grad_v.astype(BF16)
    for i in range(ROWS):
        stack = jnp.concatenate([scores_ref[i, h] for h in range(HEADS)], axis=0)
        grad_k = head_pick(dot_nn(stack, q_ref[i]))
        joint_ref[i * N : (i + 1) * N, CH : 2 * CH] = grad_k.astype(BF16)
    for i in range(ROWS):
        grad_q = weighted(k_ref[i], [scores_ref[i, h] for h in range(HEADS)]) * SCALING
        joint_ref[i * N : (i + 1) * N, 0:CH] = grad_q.astype(BF16)


def gate_back(grad_mixed, gate, part):
    return (grad_mixed * gate).astype(BF16), (grad_mixed * part).astype(BF16)


def bias_rows(nx, w_bias_t):
    return dot_nt(w_bias_t, nx)


def w_bias_rows(w_bias_ref, m):
    rows = w_bias_ref[m].astype(F32)
    return jnp.concatenate([rows, jnp.zeros((8 - HEADS, CH), F32)], axis=0).astype(BF16)


def fetch(pairs, sems):
    copies = [pltpu.make_async_copy(src, dst, sems.at[n]) for n, (src, dst) in enumerate(pairs)]
    for copy in copies:
        copy.start()
    return copies


def k1_body(
    x_hbm, cot_hbm, gain_hbm, shift_hbm, wb_hbm, msg_ref,
    x_ref, cot_ref, gain_ref, shift_ref, wb_ref, bias_s, cot_s, sems,
):
    copies = fetch(
        [(gain_hbm, gain_ref), (shift_hbm, shift_ref), (wb_hbm, wb_ref), (x_hbm, x_ref), (cot_hbm, cot_ref)],
        sems,
    )
    bias_s[...] = jnp.zeros_like(bias_s)
    for copy in copies[0:4]:
        copy.wait()
    gain, shift = gain_ref[0:1], shift_ref[0:1]
    wb = w_bias_rows(wb_ref, 0)
    for i in range(ROWS):
        normed, _inv = normalise(x_ref[i].astype(F32))
        nx = (normed * gain + shift).astype(BF16)
        bias_s[i, :, 0:N] = bias_rows(nx, wb)[0:HEADS]
    copies[4].wait()
    for i in range(ROWS):
        cot_s[pl.ds(i, N, stride=ROWS), :] = cot_ref[i].astype(F32)
    bias = bias_s[...].reshape(BROWS, CH).astype(BF16)
    for e in range(GROUP):
        msg_ref[e, 0:BLOCK] = cot_s[e * BLOCK : (e + 1) * BLOCK].astype(BF16)
        msg_ref[e, BLOCK:PACK] = bias


def k1b_body(
    x_ref, gain_ref, shift_ref, wp_ref, gb_ref, q_ref, k_ref, v_ref, gate_ref, nx_ref, norm_ref, inv_ref
):
    gain, shift = gain_ref[0:1], shift_ref[0:1]
    for i in range(ROWS):
        normed, inverse = normalise(x_ref[i].astype(F32))
        nx_ref[i * N : (i + 1) * N] = (normed * gain + shift).astype(BF16)
        norm_ref[i] = normed
        inv_ref[i] = jnp.broadcast_to(inverse, (N, CH))
    for i in range(ROWS):
        q, k, v, gate = project(nx_ref[i * N : (i + 1) * N], wp_ref[0], gb_ref[0:1])
        q_ref[i] = q
        k_ref[i] = k
        v_ref[i] = v
        gate_ref[i] = gate


def gather_rows(recv_ref, flat_s, row_s):
    for d in range(GROUP):
        flat_s[d * BLOCK : (d + 1) * BLOCK] = recv_ref[d, 0:BLOCK].astype(F32)
    for i in range(ROWS):
        for d in range(GROUP):
            at = d * BLOCK + i * ROWS
            row_s[i, d * ROWS : (d + 1) * ROWS] = flat_s[at : at + ROWS]


def k2_body(
    x_ref, q_ref, k_ref, v_ref, gate_ref, recv_ref, mask_ref, wo_ref, ob_ref, gain_ref, shift_ref, wb_ref,
    part_ref, mixed_ref, probs_ref, nx_ref, norm_ref, inv_ref, msg_ref,
    raw_s, own_s, first_s, row_ref, bias_ref, att_s,
):
    key = key_column(mask_ref)
    for d in range(GROUP):
        raw_s[d * BROWS : (d + 1) * BROWS] = recv_ref[d, BLOCK:PACK].astype(F32)
    for h in range(HEADS):
        bias_ref[h] = raw_s[pl.ds(h, N, stride=HEADS), :].T[0:N] + key
    wb = w_bias_rows(wb_ref, 1)
    w_out = wo_ref[0]
    out_bias = ob_ref[0:1]
    gain, shift = gain_ref[1:2], shift_ref[1:2]
    own_s[...] = jnp.zeros_like(own_s)
    for i in range(ROWS):
        probs = probabilities(q_ref[i], k_ref[i], bias_ref)
        for h in range(HEADS):
            probs_ref[i, h] = probs[h]
        att_s[i] = weighted(v_ref[i], [p.astype(BF16) for p in probs])
    for i in range(ROWS):
        gate = gate_ref[i]
        gated = gate * att_s[i]
        part_ref[i] = gated * (1.0 - gate)
        mixed = gated.astype(BF16)
        mixed_ref[i * N : (i + 1) * N] = mixed
    for i in range(ROWS):
        mixed = mixed_ref[i * N : (i + 1) * N]
        first = x_ref[i].astype(F32) + dot_nn(mixed, w_out) + out_bias
        first = first.astype(BF16)
        row_ref[i] = first
        first_s[pl.ds(i, N, stride=ROWS), :] = first.astype(F32)
    for i in range(ROWS):
        normed, inverse = normalise(row_ref[i].astype(F32))
        nx = (normed * gain + shift).astype(BF16)
        nx_ref[i] = nx
        norm_ref[i] = normed
        inv_ref[i] = jnp.broadcast_to(inverse, (N, CH))
        own_s[i, :, 0:N] = bias_rows(nx, wb)[0:HEADS]
    bias = own_s[...].reshape(BROWS, CH).astype(BF16)
    for e in range(GROUP):
        msg_ref[e, 0:BLOCK] = first_s[e * BLOCK : (e + 1) * BLOCK].astype(BF16)
        msg_ref[e, BLOCK:PACK] = bias


def k2b_body(recv_ref, wo_ref, up_ref, gm_ref, total_ref, flat_s, row_s):
    gather_rows(recv_ref, flat_s, row_s)
    total = jnp.zeros((8, CH), F32)
    for i in range(ROWS):
        up_f = row_s[i]
        total += fold8(up_f)
        up = up_f.astype(BF16)
        up_ref[i * N : (i + 1) * N] = up
        gm_ref[i] = dot_nt(up, wo_ref[1])
    total_ref[...] = total


def weight_grads(nx_ref, joint_ref, mixed_ref, up_ref, put):
    part = dot_tn(nx_ref[...], joint_ref[...])
    for block in range(4):
        put(block, part[:, block * CH : (block + 1) * CH])
    put(4, dot_tn(mixed_ref[...], up_ref[...]))


def split2(x):
    top = x.astype(BF16)
    return top, (x - top.astype(F32)).astype(BF16)


def put_sums(msg_ref, e, start, rows, rest):
    msg_ref[e, start : start + BROWS, 0:N] = rows.astype(BF16)
    msg_ref[e, start : start + BROWS, N:CH] = rest


def one(x):
    return jnp.sum(x, axis=0, keepdims=True)


def fold_lanes(x):
    return jnp.concatenate([x[:, g * WIDTH : (g + 1) * WIDTH] for g in range(4)], axis=0)


def unfold_lanes(x):
    r = x.shape[0] // 4
    return jnp.concatenate([x[g * r : (g + 1) * r] for g in range(4)], axis=1)


def k3_body(
    recv_ref, recv0_ref, mask_ref, wo_ref, gain_ref, shift_ref, wp_ref, gb_ref,
    msg_ref, small_ref, nx_ref, joint_ref, mixed_ref, up_ref, total_ref,
    flat_s, x_s, raw_s, bias_s, sum_s, norm_s, inv_s, q_s, k_s, v_s, gate_s, att_s, probs_s, grad_s, scores_s, gm_ref,
):
    k2b_body(recv0_ref, wo_ref, up_ref, gm_ref, total_ref, flat_s, x_s)
    key = key_column(mask_ref)
    for d in range(GROUP):
        raw_s[d * BROWS : (d + 1) * BROWS] = recv_ref[d, BLOCK:PACK].astype(F32)
    for h in range(HEADS):
        bias_s[h] = raw_s[pl.ds(h, N, stride=HEADS), :][:, 0:N] + key
    gather_rows(recv_ref, flat_s, x_s)
    sum_s[...] = jnp.zeros_like(sum_s)
    gain, shift = gain_ref[1:2], shift_ref[1:2]
    gate_bias = gb_ref[1:2]
    for i in range(ROWS):
        normed, inverse = normalise(x_s[i])
        nx_ref[i * N : (i + 1) * N] = (normed * gain + shift).astype(BF16)
        norm_s[i] = normed
        inv_s[i] = jnp.broadcast_to(inverse, (N, CH))
    for i in range(ROWS):
        q_s[i], k_s[i], v_s[i], gate_s[i] = project(nx_ref[i * N : (i + 1) * N], wp_ref[1], gate_bias)
    for i in range(ROWS):
        probs = probabilities(q_s[i], k_s[i], bias_s)
        for h in range(HEADS):
            probs_s[i, h] = probs[h]
        att_s[i] = weighted(v_s[i], [p.astype(BF16) for p in probs])
    logit_sum = jnp.zeros((8, CH), F32)
    for i in range(ROWS):
        gate, att = gate_s[i], att_s[i]
        mixed_ref[i * N : (i + 1) * N] = (gate * att).astype(BF16)
        grad_s[i], grad_logit = gate_back(gm_ref[i], gate, att * gate * (1.0 - gate))
        joint_ref[i * N : (i + 1) * N, 3 * CH :] = grad_logit
        logit_sum += fold8(grad_logit.astype(F32))
    for i in range(ROWS):
        scores_back(i, probs_s, v_s, grad_s, sum_s, scores_s)
    joint_back(probs_s, scores_s, q_s, k_s, grad_s, joint_ref)
    gain_sum = jnp.zeros((8, CH), F32)
    shift_sum = jnp.zeros((8, CH), F32)
    for i in range(ROWS):
        grad_normed = dot_nt(joint_ref[i * N : (i + 1) * N], wp_ref[1])
        normed = norm_s[i]
        flat_s[pl.ds(i, N, stride=ROWS), :] = norm_back(grad_normed, gain, normed, inv_s[i])
        gain_sum += fold8(grad_normed * normed)
        shift_sum += fold8(grad_normed)
    small_ref[0:8] = gain_sum
    small_ref[8:16] = shift_sum
    small_ref[16:24] = logit_sum
    rest = jnp.zeros((BROWS, CH - N), BF16)
    for e in range(GROUP):
        msg_ref[e, 0:BLOCK] = flat_s[e * BLOCK : (e + 1) * BLOCK].astype(BF16)
        rows = [sum_s[h, e * ROWS : (e + 1) * ROWS] for h in range(HEADS)]
        put_sums(msg_ref, e, BLOCK, jnp.concatenate(rows, axis=0), rest)


def bias_sum(recv_ref, start, gb_s):
    total = recv_ref[0, start : start + BROWS].astype(F32)
    for d in range(1, GROUP):
        total += recv_ref[d, start : start + BROWS].astype(F32)
    gb_s[...] = jnp.zeros_like(gb_s)
    for r in range(ROWS):
        for h in range(HEADS):
            gb_s[r * 8 + h : r * 8 + h + 1] = total[h * ROWS + r : h * ROWS + r + 1]
    return jnp.concatenate(split2(gb_s[...].T[0:N]), axis=1), total[:, N:CH]


def bias_part(i, gb_s, gb_t, wb_tiled, nx):
    rows = lax.broadcasted_iota(jnp.int32, (ROWS * 8, CH), 0) // 8
    picked = jnp.where(rows == i, wb_tiled, jnp.zeros_like(wb_tiled))
    top, low = split2(gb_s[i * 8 : (i + 1) * 8, 0:N])
    return dot_nn(gb_t, jnp.concatenate([picked, picked], axis=0)), dot_nn(top, nx) + dot_nn(low, nx)


def k4_body(
    recv_ref, cot_ref, q_ref, k_ref, v_ref, gate_ref, part_ref, probs_ref, mixed_ref, nx_ref,
    nx1_ref, norm1_ref, inv1_ref, gain_ref, wp_ref, wb_ref, wo_ref,
    nxw_ref, joint1_ref, mixed1_ref, upw_ref, small1_ref, total1_ref,
    up_ref, gn_ref, msg_ref, small_ref,
    flat_s, la_s, gb_s, sum_s, joint_s, grad_s, upb_s, scores_s,
):
    gather_rows(recv_ref, flat_s, la_s)
    gb_t, _rest = bias_sum(recv_ref, BLOCK, gb_s)
    wb = w_bias_rows(wb_ref, 1)
    wb_tiled = jnp.concatenate([wb.astype(F32)] * ROWS, axis=0).astype(BF16)
    sum_s[...] = jnp.zeros_like(sum_s)
    gain1 = gain_ref[1:2]
    zero = jnp.zeros((8, CH), F32)
    gain_sum, shift_sum, bias_w, logit_sum, up_sum = zero, zero, zero, zero, zero
    for i in range(ROWS):
        from_bias, grad_w = bias_part(i, gb_s, gb_t, wb_tiled, nx1_ref[i])
        normed = norm1_ref[i]
        gain_sum += fold8(from_bias * normed)
        shift_sum += fold8(from_bias)
        bias_w += grad_w
        up_f = cot_ref[i].astype(F32) + la_s[i] + norm_back(from_bias, gain1, normed, inv1_ref[i])
        up = up_f.astype(BF16)
        up_ref[i] = up
        upb_s[i * N : (i + 1) * N] = up
        up_sum += fold8(up.astype(F32))
    for i in range(ROWS):
        grad_mixed = dot_nt(up_ref[i], wo_ref[0])
        grad_s[i], grad_logit = gate_back(grad_mixed, gate_ref[i], part_ref[i])
        joint_s[i * N : (i + 1) * N, 3 * CH :] = grad_logit
        logit_sum += fold8(grad_logit.astype(F32))
    for i in range(ROWS):
        scores_back(i, probs_ref, v_ref, grad_s, sum_s, scores_s)
    joint_back(probs_ref, scores_s, q_ref, k_ref, grad_s, joint_s)
    for i in range(ROWS):
        gn_ref[i] = dot_nt(joint_s[i * N : (i + 1) * N], wp_ref[0])
    small_ref[0:8] = logit_sum
    small_ref[8:16] = up_sum
    rows = [
        one(small1_ref[0:8] + gain_sum), one(small1_ref[8:16] + shift_sum), one(small1_ref[16:24]),
        one(total1_ref[...]), bias_w[0:HEADS],
    ]
    top, low = split2(jnp.concatenate(rows, axis=0))
    rest = [fold_lanes(top.astype(F32)), fold_lanes(low.astype(F32)[HEADS:8])]
    rest = jnp.concatenate(rest, axis=0).astype(BF16)
    for h in range(HEADS):
        flat_s[h * N : (h + 1) * N, 0:N] = sum_s[h].T
    for e in range(GROUP):
        rows = [flat_s[h * N + e * ROWS : h * N + (e + 1) * ROWS, 0:N] for h in range(HEADS)]
        put_sums(msg_ref, e, 2 * WROWS, jnp.concatenate(rows, axis=0), rest)

    def put(start, block, part):
        part = part.astype(BF16)
        for e in range(GROUP):
            at = start + block * SLICE
            msg_ref[e, at : at + SLICE] = part[e * SLICE : (e + 1) * SLICE]

    weight_grads(nx_ref, joint_s, mixed_ref, upb_s, functools.partial(put, 0))
    weight_grads(nxw_ref, joint1_ref, mixed1_ref, upw_ref, functools.partial(put, WROWS))


def k5_body(
    recv_ref, norm_ref, gn_ref, nx_ref, small_ref, wb_ref,
    full_ref, msg_ref, sums1_ref, gb_s,
):
    gb_t, rest = bias_sum(recv_ref, 2 * WROWS, gb_s)
    wb = w_bias_rows(wb_ref, 0)
    wb_tiled = jnp.concatenate([wb.astype(F32)] * ROWS, axis=0).astype(BF16)
    zero = jnp.zeros((8, CH), F32)
    gain_sum, shift_sum, bias_w = zero, zero, zero
    for i in range(ROWS):
        from_bias, grad_w = bias_part(i, gb_s, gb_t, wb_tiled, nx_ref[i * N : (i + 1) * N])
        grad_normed = gn_ref[i] + from_bias
        full_ref[i] = grad_normed
        gain_sum += fold8(grad_normed * norm_ref[i])
        shift_sum += fold8(grad_normed)
        bias_w += grad_w
    total = recv_ref[0, 0 : 2 * WROWS].astype(F32)
    for d in range(1, GROUP):
        total += recv_ref[d, 0 : 2 * WROWS].astype(F32)
    total *= 1.0 / N
    total = total.astype(BF16)
    sums1_ref[...] = unfold_lanes(rest[0:32])
    sums1_ref[HEADS:8] += unfold_lanes(rest[32:48])
    rows = [one(gain_sum), one(shift_sum), one(small_ref[0:8]), one(small_ref[8:16]), bias_w[0:HEADS]]
    sums = jnp.concatenate([part.astype(F32) for part in split2(jnp.concatenate(rows, axis=0))], axis=0)
    sums = sums.astype(BF16)
    for e in range(GROUP):
        msg_ref[e, 0 : 2 * WROWS] = total
        msg_ref[e, 2 * WROWS : 2 * WROWS + 16] = sums


def k5b_body(full_ref, norm_ref, inv_ref, up_ref, gain_ref, out_ref):
    gain = gain_ref[0:1]
    for i in range(ROWS):
        back = norm_back(full_ref[i], gain, norm_ref[i], inv_ref[i])
        out_ref[i] = (up_ref[i].astype(F32) + back).astype(BF16)


def k6_body(
    recv_ref, sums1_ref, full_ref, norm_ref, inv_ref, up_ref, ln_gain_ref,
    out_ref, gain_ref, shift_ref, proj_ref, wb_ref, gate_ref, ow_ref, ob_ref,
):
    k5b_body(full_ref, norm_ref, inv_ref, up_ref, ln_gain_ref, out_ref)
    small = jnp.zeros((8, CH), F32)
    for d in range(GROUP):
        for m in range(2):
            for block in range(4):
                at = m * WROWS + block * SLICE
                proj_ref[m, d * SLICE : (d + 1) * SLICE, block * CH : (block + 1) * CH] = recv_ref[
                    d, at : at + SLICE
                ].astype(F32)
            at = m * WROWS + 4 * SLICE
            ow_ref[m, d * SLICE : (d + 1) * SLICE] = recv_ref[d, at : at + SLICE].astype(F32)
        at = 2 * WROWS
        both = recv_ref[d, at : at + 16].astype(F32)
        small += both[0:8] + both[8:16]
    small = jnp.concatenate([small, sums1_ref[...]], axis=0) * (1.0 / N)
    for m in range(2):
        at = m * 8
        gain_ref[m : m + 1] = small[at : at + 1]
        shift_ref[m : m + 1] = small[at + 1 : at + 2]
        gate_ref[m : m + 1] = small[at + 2 : at + 3]
        ob_ref[m : m + 1] = small[at + 3 : at + 4]
        wb_ref[m] = small[at + 4 : at + 8]


def call(body, outs, scratch, name, far=(), far_out=(), copies=0, flops=100000000, big=False):
    near_spec = pl.BlockSpec(memory_space=pltpu.VMEM)
    far_spec = pl.BlockSpec(memory_space=pltpu.HBM)
    scratch = [pltpu.VMEM(shape, dtype) for shape, dtype in scratch]
    if copies:
        scratch.append(pltpu.SemaphoreType.DMA((copies,)) if copies > 1 else pltpu.SemaphoreType.DMA)

    def run(*args):
        return pl.pallas_call(
            body,
            in_specs=[far_spec if n in far else near_spec for n in range(len(args))],
            out_specs=[far_spec if n in far_out else near_spec for n in range(len(outs))],
            out_shape=[jax.ShapeDtypeStruct(shape, dtype) for shape, dtype in outs],
            scratch_shapes=scratch,
            compiler_params=pltpu.CompilerParams(vmem_limit_bytes=(62 if big else 24) * 1024 * 1024),
            cost_estimate=pl.CostEstimate(flops=flops, bytes_accessed=2000000, transcendentals=500000),
            name=name,
        )(*args)

    return run


def after(x, y):
    return lax.optimization_barrier((x, y))[0]


def swap(x):
    return lax.all_to_all(x, "dap", 0, 0, tiled=True)


def per_device(
    pair_rep, cotangent, residue_mask, ln_gain, ln_shift, w_proj, w_bias, gate_bias, w_out, out_bias
):
    mask = residue_mask.reshape(1, N)
    w_bias = jnp.swapaxes(w_bias, 1, 2)
    rows_b = ((ROWS, N, CH), BF16)
    rows_f = ((ROWS, N, CH), F32)
    flat_f = ((CELLS, CH), F32)
    flat_b = ((CELLS, CH), BF16)
    joint_b = ((CELLS, 4 * CH), BF16)
    pack = ((GROUP, PACK, CH), BF16)
    mats = ((HEADS, N, N), F32)
    probs = ((ROWS, HEADS, N, N), F32)
    raw = ((GROUP * BROWS, CH), F32)
    own_bias = ((ROWS, HEADS, CH), F32)
    bias_8 = ((ROWS * 8, CH), F32)

    vec_f = ((2, CH), F32)

    (msg0,) = call(
        k1_body,
        [pack],
        [rows_b, rows_b, vec_f, vec_f, ((2, HEADS, CH), BF16), own_bias, flat_f],
        "norm_first",
        far=range(5),
        copies=5,
        big=True,
    )(pair_rep, cotangent, ln_gain, ln_shift, w_bias)
    recv0 = swap(msg0)
    q, k, v, gate, nx0, norm0, inv0 = call(
        k1b_body, [rows_b, rows_b, rows_b, rows_f, flat_b, rows_f, rows_f], [], "project_first"
    )(pair_rep, ln_gain, ln_shift, w_proj, gate_bias)
    part0, mixed0, probs0, nx1, norm1, inv1, msg1 = call(
        k2_body,
        [rows_f, flat_b, probs, rows_b, rows_f, rows_f, pack],
        [raw, own_bias, flat_f, rows_b, mats, rows_f],
        "attend_first",
    )(pair_rep, q, k, v, gate, recv0, mask, w_out, out_bias, ln_gain, ln_shift, w_bias)
    recv1 = swap(msg1)
    msg2, small1, nxw, joint1, mixed1, up1, total1 = call(
        k3_body,
        [pack, ((24, CH), F32), flat_b, joint_b, flat_b, flat_b, ((8, CH), F32)],
        [flat_f, rows_f, raw, mats, mats, rows_f, rows_f]
        + [rows_b, rows_b, rows_b, rows_f, rows_f, probs, rows_b, ((ROWS, HEADS, N, N), BF16), rows_f],
        "second_module",
    )(recv1, recv0, mask, w_out, ln_gain, ln_shift, w_proj, gate_bias)
    recv2 = swap(msg2)
    up, gn, msg3, small = call(
        k4_body,
        [rows_b, rows_f, ((GROUP, 2 * WROWS + BROWS, CH), BF16), ((16, CH), F32)],
        [flat_f, rows_f, bias_8, mats, joint_b, rows_b, flat_b, ((ROWS, HEADS, N, N), BF16)],
        "back_first",
    )(
        recv2, cotangent, q, k, v, gate, part0, probs0, mixed0, nx0, nx1, norm1, inv1,
        ln_gain, w_proj, w_bias, w_out, nxw, joint1, mixed1, up1, small1, total1,
    )
    recv3 = swap(msg3)
    full, msg4, sums1 = call(
        k5_body,
        [rows_f, ((GROUP, 2 * WROWS + 16, CH), BF16), ((8, CH), F32)],
        [bias_8],
        "grad_sums",
    )(recv3, norm0, gn, nx0, small, w_bias)
    recv4 = swap(msg4)
    grad_pair, grad_gain, grad_shift, grad_proj, grad_bias_w, grad_gate, grad_out_w, grad_out_bias = call(
        k6_body,
        [
            rows_b, ((2, CH), F32), ((2, CH), F32), ((2, CH, 4 * CH), F32), ((2, HEADS, CH), F32),
            ((2, CH), F32), ((2, CH, CH), F32), ((2, CH), F32),
        ],
        [],
        "weight_sums",
    )(recv4, sums1, full, norm0, inv0, up, ln_gain)
    return (
        grad_pair, grad_gain, grad_shift, grad_proj, jnp.swapaxes(grad_bias_w, 1, 2), grad_gate,
        grad_out_w, grad_out_bias,
    )


def solution(mesh):
    in_specs = (
        P(("dp", "dap"), None, None),
        P(("dp", "dap"), None, None),
        P("dp"),
        P(),
        P(),
        P(),
        P(),
        P(),
        P(),
        P(),
    )
    out_specs = (
        P(("dp", "dap"), None, None),
        P("dp", None),
        P("dp", None),
        P("dp", None, None),
        P("dp", None, None),
        P("dp", None),
        P("dp", None, None),
        P("dp", None),
    )
    return jax.shard_map(
        per_device, mesh=mesh, in_specs=in_specs, out_specs=out_specs, check_vma=False
    )
```
